32 devices in a mesh: rep: 2 (over y), grp: 4 (over x, core), ing: 4 (over z).
Axes of the slice: x: 2, y: 2, z: 4, core: 2. Of those that a mesh axis runs over, the one named last changes fastest.
Arguments:
- tokens: bfloat16 [8192, 3584], P(('rep', 'grp', 'ing')), parts along dimension 0, may hold values from -6 to 6
- router_logits: float32 [8192, 96], P(('rep', 'grp', 'ing')), parts along dimension 0, may hold values from -8 to 8
- expert_ids: int32 [8192, 8], P(('rep', 'grp', 'ing')), parts along dimension 0, may hold values from 0 to 95, as said below
- w_gate: bfloat16 [4, 3584, 2048], P('grp', None, 'ing'), may hold values from -0.09375 to 0.09375
- w_up: bfloat16 [4, 3584, 2048], P('grp', None, 'ing'), may hold values from -0.09375 to 0.09375
- w_down: bfloat16 [4, 2048, 3584], P('grp', None, 'ing'), may hold values from -0.125 to 0.125
Outputs:
- mixed_out: bfloat16 [8192, 3584], P(('rep', 'grp', 'ing')), parts along dimension 0
The draws below stay inside these ranges and needn't reach their ends.
There are 2 independent parts, one for each index of `rep`. The reference program is written for one: setup_inputs(seed, part) draws one part's arguments, and reference() takes and returns one part's arrays. A program takes and returns all parts, laid end to end along the dimension named above; an argument that names none is the same for every part. Nothing has to cross between parts.
Inputs may be any that keep to these rules, and one draw needn't show every extreme that they name: `expert_ids`: each row names 8 different experts, two in each of exactly 4 groups, expert e lying in group e // 24. Among the tokens of one device at most 8 name the first expert of any one group; among the tokens of the 4 devices that share one ing index at most 16 name the first expert of any one group; both bounds are reached in every draw.
All inputs are finite; a program needn't handle non-finite values.
Results may differ from the reference program's by a relative error of at most 0.0067.
Values may be sent and summed in bfloat16 or wider, within the bound.
No kernel may reach another device: no remote copies, remote signals or barrier semaphores. Data moves between devices by JAX's collectives and lax.ppermute only.
A program may use at most 64 MiB of HBM per device.

```python
import jax
import jax.numpy as jnp
from jax import lax

D = 3584
FFN = 2048
TOP = 8
GSEL = 4
GROUP_EXPERTS = 24
TOK_DEV = 256
CAP = 8
GROUPS = 4
EXPERTS = 96
SLOTS = 16
TOKENS = 4096
N_ING = 4


def draw_expert_ids(key, part):
    key = jax.random.fold_in(key, 11)
    subkeys = jax.random.split(key, 8)
    devices = TOKENS // TOK_DEV
    columns = devices // GROUPS
    classes = GROUPS // GSEL
    heat_level = jax.random.randint(subkeys[0], (GROUPS,), 1, 5)
    hottest = jax.random.randint(subkeys[1], (), 0, GROUPS)
    heat_level = jnp.where(jnp.arange(GROUPS) == hottest, 4, heat_level)
    shortfall = jax.random.randint(subkeys[2], (columns, GROUPS), 0, SLOTS // 4 + 1)
    totals = jnp.where(heat_level[None, :] == 4, SLOTS, jnp.maximum(SLOTS * heat_level[None, :] // 4 - shortfall, 0))
    source_scores = jax.random.randint(subkeys[3], (columns, GROUPS, GROUPS), 0, 1 << 20) * GROUPS + jnp.arange(GROUPS)
    source_rank = jnp.argsort(jnp.argsort(source_scores, axis=2), axis=2)
    per_source = jnp.clip(totals[:, :, None] - CAP * source_rank, 0, CAP)
    device_counts = jnp.transpose(per_source, (2, 0, 1)).reshape(devices, GROUPS)
    group_scores = jax.random.randint(subkeys[4], (devices, GROUPS), 0, 1 << 20) * GROUPS + jnp.arange(GROUPS)
    group_class = jnp.argsort(jnp.argsort(group_scores, axis=1), axis=1) // GSEL
    token_scores = jax.random.randint(subkeys[5], (devices, TOK_DEV), 0, 1 << 20) * TOK_DEV + jnp.arange(TOK_DEV)
    token_class = jnp.argsort(jnp.argsort(token_scores, axis=1), axis=1) % classes
    member = group_class[:, None, :] == token_class[:, :, None]
    class_rank = jnp.cumsum(member.astype(jnp.int32), axis=1) - 1
    hit_mask = member & (class_rank < device_counts[:, None, :])
    first_pick = jax.random.randint(subkeys[6], (devices, TOK_DEV, GROUPS), 1, GROUP_EXPERTS)
    second_pick = jax.random.randint(subkeys[7], (devices, TOK_DEV, GROUPS), 1, GROUP_EXPERTS - 1)
    second_pick = second_pick + (second_pick >= first_pick).astype(jnp.int32)
    lead_expert = jnp.where(hit_mask, 0, first_pick)
    trail_expert = jnp.where(hit_mask, first_pick, second_pick)
    group_base = jnp.arange(GROUPS, dtype=jnp.int32) * GROUP_EXPERTS
    pair_ids = jnp.stack([group_base + lead_expert, group_base + trail_expert], axis=-1)
    position = jnp.cumsum(member.astype(jnp.int32), axis=2) - 1
    selector = (member[..., None] & (position[..., None] == jnp.arange(GSEL))).astype(jnp.int32)
    expert_list = jnp.sum(selector[..., :, None] * pair_ids[..., None, :], axis=2)
    return expert_list.reshape(TOKENS, TOP).astype(jnp.int32)


def levels(own_key, extent, pieces, low, high):
    def one(axis_at, blocks):
        steps = jax.random.uniform(jax.random.fold_in(jax.random.fold_in(own_key, 6), axis_at), (blocks,), jnp.float32, low / len(pieces), high / len(pieces))
        return jnp.repeat(jnp.exp(steps), extent[axis_at] // blocks).reshape((-1,) + (1,) * (len(extent) - axis_at - 1))

    factor_of = one(*pieces[0])
    for cut in pieces[1:]:
        factor_of = factor_of * one(*cut)
    return factor_of


def bell_draw(key, extent, deviation, reach, pieces=(), kind=jnp.bfloat16):
    values = deviation * jax.random.normal(key, extent, jnp.float32)
    if pieces:
        values = values * levels(key, extent, pieces, -0.22, 0.18)
    return jnp.clip(values, -reach, reach).astype(kind)


def setup_inputs(seed: int = 0, part: int = 0) -> dict:
    streams_of = jax.random.split(jax.random.key(seed), 7)
    part_keys = jax.random.split(jax.random.fold_in(streams_of[6], part), 7)
    return {
        "tokens": bell_draw(part_keys[0], (TOKENS, D), 1.0, 6.0, ((0, 16),)),
        "router_logits": bell_draw(part_keys[1], (TOKENS, EXPERTS), 2.0, 8.0, ((0, 16),), jnp.float32),
        "expert_ids": draw_expert_ids(jax.random.fold_in(jax.random.fold_in(streams_of[6], part), 71), part),
        "w_gate": bell_draw(streams_of[3], (GROUPS, D, FFN), D ** -0.5, 0.09375, ((0, 4), (2, 4))),
        "w_up": bell_draw(streams_of[4], (GROUPS, D, FFN), D ** -0.5, 0.09375, ((0, 4), (2, 4))),
        "w_down": bell_draw(streams_of[5], (GROUPS, FFN, D), FFN ** -0.5, 0.125, ((0, 4), (2, 4))),
    }


route_scale = 2.827


def reference(tokens, router_logits, expert_ids, w_gate, w_up, w_down):
    firsts = jnp.arange(GROUPS, dtype=jnp.int32) * GROUP_EXPERTS
    window_hits = jnp.any(expert_ids[:, :, None] == firsts[None, None, :], axis=1)
    scores = jax.nn.sigmoid(router_logits.astype(jnp.float32))
    chosen = jnp.sum(jnp.take_along_axis(scores, expert_ids, axis=1), axis=1)
    leading = scores[:, firsts]
    weights = (route_scale * leading / chosen[:, None]).astype(jnp.bfloat16)
    weights = jnp.where(window_hits, weights, jnp.zeros_like(weights))
    row_limit = N_ING * SLOTS

    def one_group(running, group_index):
        column = window_hits[:, group_index]
        row_index = jnp.nonzero(column, size=row_limit, fill_value=0)[0].astype(jnp.int32)
        live_rows = jnp.arange(row_limit, dtype=jnp.int32) < jnp.sum(column.astype(jnp.int32))
        picked = tokens[row_index]
        gate_out = jnp.dot(picked, w_gate[group_index], preferred_element_type=jnp.float32)
        up_out = jnp.dot(picked, w_up[group_index], preferred_element_type=jnp.float32)
        activated = (jax.nn.silu(gate_out) * up_out).astype(jnp.bfloat16)
        result = jnp.dot(activated, w_down[group_index], preferred_element_type=jnp.float32).astype(jnp.bfloat16)
        row_weight = jnp.where(live_rows, weights[row_index, group_index].astype(jnp.float32), jnp.float32(0.0))
        running = running.at[row_index].add(row_weight[:, None] * result.astype(jnp.float32))
        return running, None

    mixed_out, _ = lax.scan(one_group, jnp.zeros((TOKENS, D), jnp.float32), jnp.arange(GROUPS, dtype=jnp.int32))
    return mixed_out.astype(jnp.bfloat16)
```

```python
import functools

import jax
import jax.numpy as jnp
from jax import lax
from jax.experimental import pallas as pl
from jax.experimental.pallas import tpu as pltpu
from jax.sharding import PartitionSpec as P

GROUP_EXPERTS = 24
CAP = 8
LANES = 128
ROUTE_SCALE = 2.827
VMEM_LIMIT = 48 * 1024 * 1024

BF16 = jnp.bfloat16
F32 = jnp.float32
VMEM = pl.BlockSpec(memory_space=pltpu.VMEM)
ANY = pl.BlockSpec(memory_space=pl.ANY)


def params():
    return pltpu.CompilerParams(vmem_limit_bytes=VMEM_LIMIT)


def cost(flops, nbytes):
    return pl.CostEstimate(flops=flops, bytes_accessed=nbytes, transcendentals=0)


def named(ids, expert):
    hit = jnp.zeros(expert.shape, F32)
    for k in range(ids.shape[0]):
        hit = jnp.where(ids[k : k + 1, :] == expert, 1.0, hit)
    return hit


def placing(ids, groups, me):
    rows, count = groups * CAP, ids.shape[1]
    row = lax.broadcasted_iota(jnp.int32, (rows, count), 0)
    group = lax.rem(row // CAP + me, groups)
    hit = named(ids, group * GROUP_EXPERTS)
    before = (
        lax.broadcasted_iota(jnp.int32, (count, count), 0)
        <= lax.broadcasted_iota(jnp.int32, (count, count), 1)
    ).astype(BF16)
    rank = jnp.dot(hit.astype(BF16), before, preferred_element_type=F32)
    slot = lax.rem(row, CAP).astype(F32)
    return jnp.where((hit > 0.5) & (rank == slot + 1.0), 1.0, 0.0), group


def dispatch_kernel(groups, width, ids_ref, tokens_ref, *refs):
    outs, (staged, sems) = refs[:groups], refs[groups:]
    me = lax.axis_index("grp")
    features = tokens_ref.shape[1]
    copies = []
    for c in range(features // width):
        part = pl.ds(c * width, width)
        copies.append(pltpu.make_async_copy(tokens_ref.at[:, part], staged.at[:, part], sems.at[c]))
        copies[-1].start()
    place, _ = placing(ids_ref[...], groups, me)
    live = jnp.sum(place, axis=1, keepdims=True)
    place = place.astype(BF16)
    for d in range(groups):
        outs[d][:, features:] = jnp.broadcast_to(live[d * CAP : (d + 1) * CAP], (CAP, LANES)).astype(BF16)
    for c in range(features // width):
        copies[c].wait()
        part = slice(c * width, (c + 1) * width)
        rows = jnp.dot(place, staged[:, part], preferred_element_type=F32)
        for d in range(groups):
            outs[d][:, part] = rows[d * CAP : (d + 1) * CAP].astype(BF16)


def mixing_kernel(groups, ids_ref, logits_ref, out_ref):
    me = lax.axis_index("grp")
    ids = ids_ref[...]
    place, group = placing(ids, groups, me)
    scores = 1.0 / (1.0 + jnp.exp(-logits_ref[...]))
    expert = lax.broadcasted_iota(jnp.int32, scores.shape, 0)
    chosen = jnp.sum(jnp.where(named(ids, expert) > 0.5, scores, 0.0), axis=0, keepdims=True)
    leading = jnp.zeros(place.shape, F32)
    for g in range(groups):
        leading = jnp.where(group == g, scores[g * GROUP_EXPERTS : g * GROUP_EXPERTS + 1, :], leading)
    weight = (ROUTE_SCALE * leading / chosen).astype(BF16).astype(F32)
    out_ref[...] = jnp.where(place > 0.5, weight, 0.0).astype(BF16)


def compact_kernel(groups, slots, *refs):
    arrived, out_ref = refs[:groups], refs[groups]
    rows, features = groups * CAP, out_ref.shape[1] - LANES
    live = jnp.concatenate([a[:, features:].astype(F32) for a in arrived], axis=0)
    row = lax.broadcasted_iota(jnp.int32, (rows, rows), 0)
    column = lax.broadcasted_iota(jnp.int32, (rows, rows), 1)
    before = (column <= row).astype(BF16)
    rank = jnp.dot(before, live.astype(BF16), preferred_element_type=F32)
    rank = jnp.broadcast_to(rank[:, :1], (rows, LANES))
    lane = lax.broadcasted_iota(jnp.int32, (rows, LANES), 1).astype(F32)
    pick = jnp.where((live > 0.5) & (rank == lane + 1.0), 1.0, 0.0).astype(BF16)[:, :slots]
    origin = (lax.broadcasted_iota(jnp.int32, (rows, LANES), 0) + 1).astype(BF16)
    contract = (((0,), (0,)), ((), ()))
    out_ref[:, features:] = lax.dot_general(pick, origin, contract, preferred_element_type=F32).astype(BF16)
    step = 512
    for c in range(features // step):
        part = slice(c * step, (c + 1) * step)
        whole = jnp.concatenate([a[:, part].astype(F32) for a in arrived], axis=0).astype(BF16)
        out_ref[:, part] = lax.dot_general(pick, whole, contract, preferred_element_type=F32).astype(BF16)


def hidden_kernel(columns, *refs):
    blocks, (gate_ref, up_ref, hidden_ref, tag_ref, held) = refs[:columns], refs[columns:]
    slots = blocks[0].shape[0]
    features, units = gate_ref.shape
    for e in range(columns):
        held[e * slots : (e + 1) * slots, :] = blocks[e][:, :features]
        tag_ref[e * slots : (e + 1) * slots, :] = blocks[e][:, features:].astype(F32)
    step = min(256, units)
    for c in range(units // step):
        part = slice(c * step, (c + 1) * step)
        gate = jnp.dot(held[...], gate_ref[:, part], preferred_element_type=F32)
        up = jnp.dot(held[...], up_ref[:, part], preferred_element_type=F32)
        hidden_ref[:, part] = (gate / (1.0 + jnp.exp(-gate)) * up).astype(BF16)


def down_kernel(groups, columns, *refs):
    hiddens, (tag_ref, down_ref), outs = refs[:columns], refs[columns : columns + 2], refs[columns + 2 :]
    me = lax.axis_index("ing")
    rows, units = hiddens[0].shape
    slots = rows // columns
    total = jnp.zeros((rows, down_ref.shape[1]), F32)
    for f in range(columns):
        owner = lax.rem(me - f + columns, columns)
        order = [(e - f) % columns for e in range(columns)]
        block = jnp.concatenate([hiddens[f][slots * o : slots * (o + 1), :] for o in order], axis=0)
        total += jnp.dot(
            block, down_ref[pl.ds(pl.multiple_of(owner * units, units), units), :], preferred_element_type=F32
        )
    result = total.astype(BF16)
    wide = groups * CAP
    for e in range(columns):
        mine = slice(e * slots, (e + 1) * slots)
        origin = tag_ref[mine, :][:, :1] - 1.0
        lane = lax.broadcasted_iota(jnp.int32, (slots, wide), 1).astype(F32)
        spread = jnp.where(origin == lane, 1.0, 0.0).astype(BF16)
        back = lax.dot_general(spread, result[mine], (((0,), (0,)), ((), ())), preferred_element_type=F32)
        for d in range(groups):
            outs[d * columns + e][...] = back[d * CAP : (d + 1) * CAP].astype(BF16)


def combine_kernel(groups, columns, mixing_ref, *refs):
    blocks, out_ref = refs[:-1], refs[-1]
    me = lax.axis_index("ing")
    width = blocks[0].shape[1]
    for e in range(columns):
        rows = jnp.concatenate([blocks[d * columns + e][...].astype(F32) for d in range(groups)], axis=0)
        value = lax.dot_general(
            mixing_ref[...], rows.astype(BF16), (((0,), (0,)), ((), ())), preferred_element_type=F32
        )
        at = pl.multiple_of(lax.rem(me + e, columns) * width, width)
        out_ref[:, pl.ds(at, width)] = value.astype(BF16)


def shift(x, names, sizes, steps):
    if not any(steps):
        return x
    pairs = []
    for a in range(sizes[0]):
        for b in range(sizes[1]):
            to = (a + steps[0]) % sizes[0], (b + steps[1]) % sizes[1]
            pairs.append((a * sizes[1] + b, to[0] * sizes[1] + to[1]))
    return lax.ppermute(x, names, pairs)


def local(tokens, router_logits, expert_ids, w_gate, w_up, w_down):
    groups = lax.axis_size("grp")
    columns = lax.axis_size("ing")
    count, features = tokens.shape
    units, share = w_gate.shape[2], w_down.shape[2]
    slots = groups * CAP // 2
    wide = features + LANES
    move = functools.partial(shift, names=("grp", "ing"), sizes=(groups, columns))
    ids = expert_ids.T

    outbound = pl.pallas_call(
        functools.partial(dispatch_kernel, groups, 512),
        out_shape=[jax.ShapeDtypeStruct((CAP, wide), BF16)] * groups,
        in_specs=[VMEM, ANY],
        out_specs=[VMEM] * groups,
        scratch_shapes=[pltpu.VMEM((count, features), BF16), pltpu.SemaphoreType.DMA((features // 512,))],
        compiler_params=params(),
        name="dispatch",
    )(ids, tokens)
    arrived = [move(outbound[d], steps=(d, 0)) for d in range(groups)]

    mixing = pl.pallas_call(
        functools.partial(mixing_kernel, groups),
        out_shape=jax.ShapeDtypeStruct((groups * CAP, count), BF16),
        in_specs=[VMEM, VMEM],
        out_specs=VMEM,
        compiler_params=params(),
        name="mixing",
    )(ids, router_logits.T)

    compacted = pl.pallas_call(
        functools.partial(compact_kernel, groups, slots),
        out_shape=jax.ShapeDtypeStruct((slots, wide), BF16),
        in_specs=[VMEM] * groups,
        out_specs=VMEM,
        compiler_params=params(),
        name="compact",
    )(*arrived)
    blocks = [move(compacted, steps=(0, e)) for e in range(columns)]

    gate = pltpu.with_memory_space_constraint(w_gate[0], pltpu.VMEM)
    up = pltpu.with_memory_space_constraint(w_up[0], pltpu.VMEM)
    down = pltpu.with_memory_space_constraint(w_down[0], pltpu.VMEM)
    hidden, tags = pl.pallas_call(
        functools.partial(hidden_kernel, columns),
        out_shape=[
            jax.ShapeDtypeStruct((columns * slots, units), BF16),
            jax.ShapeDtypeStruct((columns * slots, LANES), F32),
        ],
        in_specs=[VMEM] * (columns + 2),
        out_specs=[VMEM, VMEM],
        scratch_shapes=[pltpu.VMEM((columns * slots, features), BF16)],
        compiler_params=params(),
        name="hidden",
    )(*blocks, gate, up)
    hiddens = [move(hidden, steps=(0, f)) for f in range(columns)]

    results = pl.pallas_call(
        functools.partial(down_kernel, groups, columns),
        out_shape=[jax.ShapeDtypeStruct((CAP, share), BF16)] * (groups * columns),
        in_specs=[VMEM] * (columns + 2),
        out_specs=[VMEM] * (groups * columns),
        compiler_params=params(),
        name="down",
    )(*hiddens, tags, down)
    returned = [
        move(results[d * columns + e], steps=(-d, -e)) for d in range(groups) for e in range(columns)
    ]

    if share % LANES:
        me = lax.axis_index("ing")
        rows = jnp.stack(returned).reshape(groups, columns, CAP, share)
        rows = jnp.roll(rows, me, axis=1).transpose(0, 2, 1, 3).reshape(groups * CAP, features)
        return jnp.dot(mixing.T, rows, preferred_element_type=F32).astype(BF16)
    return pl.pallas_call(
        functools.partial(combine_kernel, groups, columns),
        out_shape=jax.ShapeDtypeStruct((count, features), BF16),
        in_specs=[VMEM] * (1 + groups * columns),
        out_specs=VMEM,
        compiler_params=params(),
        name="combine",
    )(mixing, *returned)


def solution(mesh):
    placed = (
        P(("rep", "grp", "ing"), None),
        P(("rep", "grp", "ing"), None),
        P(("rep", "grp", "ing"), None),
        P("grp", None, "ing"),
        P("grp", None, "ing"),
        P("grp", None, "ing"),
    )
    return jax.shard_map(
        local, mesh=mesh, in_specs=placed, out_specs=P(("rep", "grp", "ing"), None), check_vma=False
    )
```

```python
import functools

import jax
import jax.numpy as jnp
from jax import lax
from jax.experimental import pallas as pl
from jax.experimental.pallas import tpu as pltpu
from jax.sharding import PartitionSpec as P

GROUP_EXPERTS = 24
CAP = 8
LANES = 128
ROUTE_SCALE = 2.827
MIB = 1024 * 1024

BF16 = jnp.bfloat16
F32 = jnp.float32
VMEM = pl.BlockSpec(memory_space=pltpu.VMEM)
ANY = pl.BlockSpec(memory_space=pl.ANY)


def params(nbytes):
    return pltpu.CompilerParams(vmem_limit_bytes=2 * nbytes + 4 * MIB)


def named(ids, expert):
    hit = jnp.zeros(expert.shape, F32)
    for k in range(ids.shape[0]):
        hit = jnp.where(ids[k : k + 1, :] == expert, 1.0, hit)
    return hit


def placing(ids, groups, me):
    rows, count = groups * CAP, ids.shape[1]
    row = lax.broadcasted_iota(jnp.int32, (rows, count), 0)
    group = (row // CAP) ^ me
    hit = named(ids, group * GROUP_EXPERTS)
    before = (
        lax.broadcasted_iota(jnp.int32, (count, count), 0)
        <= lax.broadcasted_iota(jnp.int32, (count, count), 1)
    ).astype(BF16)
    rank = jnp.dot(hit.astype(BF16), before, preferred_element_type=F32)
    slot = lax.rem(row, CAP).astype(F32)
    return jnp.where((hit > 0.5) & (rank == slot + 1.0), 1.0, 0.0), group


def dispatch_kernel(groups, width, ids_ref, tokens_ref, *refs):
    outs, (ids_held, staged, sems) = refs[:groups], refs[groups:]
    me = lax.axis_index("grp")
    features = tokens_ref.shape[1]
    first = pltpu.make_async_copy(ids_ref, ids_held, sems.at[features // width])
    first.start()
    copies = []
    for c in range(features // width):
        part = pl.ds(c * width, width)
        copies.append(pltpu.make_async_copy(tokens_ref.at[:, part], staged.at[:, part], sems.at[c]))
        copies[-1].start()
    first.wait()
    place, _ = placing(ids_held[...], groups, me)
    live = jnp.sum(place, axis=1, keepdims=True)
    place = place.astype(BF16)
    for d in range(groups):
        outs[d][:, features:] = jnp.broadcast_to(live[d * CAP : (d + 1) * CAP], (CAP, LANES)).astype(BF16)
    for c in range(features // width):
        copies[c].wait()
        part = slice(c * width, (c + 1) * width)
        rows = jnp.dot(place, staged[:, part], preferred_element_type=F32)
        for d in range(groups):
            outs[d][:, part] = rows[d * CAP : (d + 1) * CAP].astype(BF16)


def prepare_kernel(groups, after_ref, ids_ref, logits_ref, *refs):
    del after_ref
    weights, loaded, (out_ref, ids_held, logits_held, sems) = refs[:3], refs[3:6], refs[6:]
    small = [
        pltpu.make_async_copy(ids_ref, ids_held, sems.at[12]),
        pltpu.make_async_copy(logits_ref, logits_held, sems.at[13]),
    ]
    for copy in small:
        copy.start()
    copies = []
    for k in range(3):
        depth = weights[k].shape[0]
        for c in range(4):
            part = pl.ds(c * (depth // 4), depth // 4)
            copies.append(pltpu.make_async_copy(weights[k].at[part], loaded[k].at[part], sems.at[4 * k + c]))
            copies[-1].start()
    for copy in small:
        copy.wait()
    me = lax.axis_index("grp")
    ids = ids_held[...]
    place, group = placing(ids, groups, me)
    scores = 1.0 / (1.0 + jnp.exp(-logits_held[...]))
    expert = lax.broadcasted_iota(jnp.int32, scores.shape, 0)
    chosen = jnp.sum(jnp.where(named(ids, expert) > 0.5, scores, 0.0), axis=0, keepdims=True)
    leading = jnp.zeros(place.shape, F32)
    for g in range(groups):
        leading = jnp.where(group == g, scores[g * GROUP_EXPERTS : g * GROUP_EXPERTS + 1, :], leading)
    weight = (ROUTE_SCALE * leading / chosen).astype(BF16).astype(F32)
    out_ref[...] = jnp.where(place > 0.5, weight, 0.0).astype(BF16)
    for copy in copies:
        copy.wait()


def compact_kernel(groups, slots, after_ref, *refs):
    del after_ref
    arrived, out_ref = refs[:groups], refs[groups]
    rows, features = groups * CAP, out_ref.shape[1] - LANES
    live = jnp.concatenate([a[:, features:].astype(F32) for a in arrived], axis=0)
    row = lax.broadcasted_iota(jnp.int32, (rows, rows), 0)
    column = lax.broadcasted_iota(jnp.int32, (rows, rows), 1)
    before = (column <= row).astype(BF16)
    rank = jnp.dot(before, live.astype(BF16), preferred_element_type=F32)
    rank = jnp.broadcast_to(rank[:, :1], (rows, LANES))
    lane = lax.broadcasted_iota(jnp.int32, (rows, LANES), 1).astype(F32)
    pick = jnp.where((live > 0.5) & (rank == lane + 1.0), 1.0, 0.0).astype(BF16)[:, :slots]
    origin = (lax.broadcasted_iota(jnp.int32, (rows, LANES), 0) + 1).astype(BF16)
    contract = (((0,), (0,)), ((), ()))
    out_ref[:, features:] = lax.dot_general(pick, origin, contract, preferred_element_type=F32).astype(BF16)
    step = 512
    for c in range(features // step):
        part = slice(c * step, (c + 1) * step)
        whole = jnp.concatenate([a[:, part].astype(F32) for a in arrived], axis=0).astype(BF16)
        out_ref[:, part] = lax.dot_general(pick, whole, contract, preferred_element_type=F32).astype(BF16)


def hidden_kernel(columns, *refs):
    blocks, (gate_ref, up_ref, hidden_ref, tag_ref, held) = refs[:columns], refs[columns:]
    slots = blocks[0].shape[0]
    features, units = gate_ref.shape
    for e in range(columns):
        held[e * slots : (e + 1) * slots, :] = blocks[e][:, :features]
        tag_ref[e * slots : (e + 1) * slots, :] = blocks[e][:, features:].astype(F32)
    step = min(256, units)
    for c in range(units // step):
        part = slice(c * step, (c + 1) * step)
        gate = jnp.dot(held[...], gate_ref[:, part], preferred_element_type=F32)
        up = jnp.dot(held[...], up_ref[:, part], preferred_element_type=F32)
        hidden_ref[:, part] = (gate / (1.0 + jnp.exp(-gate)) * up).astype(BF16)


def down_kernel(groups, columns, *refs):
    hiddens, (tag_ref, down_ref, out_ref) = refs[:columns], refs[columns:]
    me, group = lax.axis_index("ing"), lax.axis_index("grp")
    rows, units = hiddens[0].shape
    slots = rows // columns
    total = jnp.zeros((rows, down_ref.shape[1]), F32)
    for f in range(columns):
        block = jnp.concatenate(
            [hiddens[f][slots * (e ^ f) : slots * ((e ^ f) + 1), :] for e in range(columns)], axis=0
        )
        at = pl.multiple_of((me ^ f) * units, units)
        total += jnp.dot(block, down_ref[pl.ds(at, units), :], preferred_element_type=F32)
    result = total.astype(BF16)
    wide = groups * CAP
    for e in range(columns):
        mine = slice(e * slots, (e + 1) * slots)
        origin = tag_ref[mine, :][:, :1] - 1.0
        lane = lax.broadcasted_iota(jnp.int32, (slots, wide), 1).astype(F32)
        spread = jnp.where(origin == lane, 1.0, 0.0).astype(BF16)
        back = lax.dot_general(spread, result[mine], (((0,), (0,)), ((), ())), preferred_element_type=F32)
        for d in range(groups):
            out_ref[(group ^ d) * columns + (me ^ e)] = back[d * CAP : (d + 1) * CAP].astype(BF16)


def combine_kernel(groups, columns, mixing_ref, back_ref, out_ref, held, sems):
    group = lax.axis_index("grp")
    width = back_ref.shape[2]
    copies = []
    for i in range(columns):
        rows = jnp.concatenate(
            [back_ref[(group ^ d) * columns + i].astype(F32) for d in range(groups)], axis=0
        )
        value = lax.dot_general(
            mixing_ref[...], rows.astype(BF16), (((0,), (0,)), ((), ())), preferred_element_type=F32
        )
        part = pl.ds(i * width, width)
        held[:, part] = value.astype(BF16)
        copies.append(pltpu.make_async_copy(held.at[:, part], out_ref.at[:, part], sems.at[i]))
        copies[-1].start()
    for copy in copies:
        copy.wait()


def swap(x, name, step):
    if step == 0:
        return x
    return lax.ppermute(x, name, [(a, a ^ step) for a in range(lax.axis_size(name))])


def local(tokens, router_logits, expert_ids, w_gate, w_up, w_down):
    groups = lax.axis_size("grp")
    columns = lax.axis_size("ing")
    count, features = tokens.shape
    units, share = w_gate.shape[2], w_down.shape[2]
    slots = groups * CAP // 2
    wide = features + LANES
    ids = pltpu.with_memory_space_constraint(expert_ids.T, pltpu.HBM)
    logits = pltpu.with_memory_space_constraint(router_logits.T, pltpu.HBM)

    outbound = pl.pallas_call(
        functools.partial(dispatch_kernel, groups, 512),
        out_shape=[jax.ShapeDtypeStruct((CAP, wide), BF16)] * groups,
        in_specs=[ANY, ANY],
        out_specs=[VMEM] * groups,
        scratch_shapes=[
            pltpu.VMEM(ids.shape, jnp.int32),
            pltpu.VMEM((count, features), BF16),
            pltpu.SemaphoreType.DMA((features // 512 + 1,)),
        ],
        compiler_params=params(2 * count * features),
        name="dispatch",
    )(ids, pltpu.with_memory_space_constraint(tokens, pltpu.HBM))
    arrived = [swap(outbound[d], "grp", d) for d in range(groups)]

    weights = [w_gate[0], w_up[0], w_down[0]]
    gate, up, down, mixing = pl.pallas_call(
        functools.partial(prepare_kernel, groups),
        out_shape=[pltpu.VMEM(w.shape, BF16) for w in weights]
        + [jax.ShapeDtypeStruct((groups * CAP, count), BF16)],
        in_specs=[ANY] * 6,
        out_specs=[VMEM] * 4,
        scratch_shapes=[
            pltpu.VMEM(ids.shape, jnp.int32),
            pltpu.VMEM(logits.shape, F32),
            pltpu.SemaphoreType.DMA((14,)),
        ],
        compiler_params=params(0),
        name="prepare",
    )(
        outbound[0],
        ids,
        logits,
        *[pltpu.with_memory_space_constraint(w, pltpu.HBM) for w in weights],
    )

    compacted = pl.pallas_call(
        functools.partial(compact_kernel, groups, slots),
        out_shape=jax.ShapeDtypeStruct((slots, wide), BF16),
        in_specs=[ANY] + [VMEM] * groups,
        out_specs=VMEM,
        compiler_params=params(2 * (groups * CAP + slots) * wide),
        name="compact",
    )(mixing, *arrived)
    blocks = [swap(compacted, "ing", e) for e in range(columns)]

    hidden, tags = pl.pallas_call(
        functools.partial(hidden_kernel, columns),
        out_shape=[
            jax.ShapeDtypeStruct((columns * slots, units), BF16),
            jax.ShapeDtypeStruct((columns * slots, LANES), F32),
        ],
        in_specs=[VMEM] * (columns + 2),
        out_specs=[VMEM, VMEM],
        scratch_shapes=[pltpu.VMEM((columns * slots, features), BF16)],
        compiler_params=params(2 * columns * slots * (2 * features + units)),
        name="hidden",
    )(*blocks, gate, up)
    hiddens = [swap(hidden, "ing", f) for f in range(columns)]

    results = pl.pallas_call(
        functools.partial(down_kernel, groups, columns),
        out_shape=jax.ShapeDtypeStruct((groups * columns, CAP, share), BF16),
        in_specs=[VMEM] * (columns + 2),
        out_specs=VMEM,
        compiler_params=params(2 * columns * slots * (columns * units + 4 * share)),
        name="down",
    )(*hiddens, tags, down)
    returned = lax.all_to_all(results, ("grp", "ing"), split_axis=0, concat_axis=0, tiled=True)

    if share % LANES:
        me = lax.axis_index("grp")
        rows = returned.reshape(groups, columns, CAP, share)[jnp.arange(groups) ^ me]
        rows = rows.transpose(0, 2, 1, 3).reshape(groups * CAP, features)
        return jnp.dot(mixing.T, rows, preferred_element_type=F32).astype(BF16)
    return pl.pallas_call(
        functools.partial(combine_kernel, groups, columns),
        out_shape=jax.ShapeDtypeStruct((count, features), BF16),
        in_specs=[VMEM, VMEM],
        out_specs=ANY,
        scratch_shapes=[pltpu.VMEM((count, features), BF16), pltpu.SemaphoreType.DMA((columns,))],
        compiler_params=params(2 * (count + groups * CAP) * features),
        name="combine",
    )(mixing, returned)


def solution(mesh):
    placed = (
        P(("rep", "grp", "ing"), None),
        P(("rep", "grp", "ing"), None),
        P(("rep", "grp", "ing"), None),
        P("grp", None, "ing"),
        P("grp", None, "ing"),
        P("grp", None, "ing"),
    )
    return jax.shard_map(
        local, mesh=mesh, in_specs=placed, out_specs=P(("rep", "grp", "ing"), None), check_vma=False
    )
```

```python
import functools

import jax
import jax.numpy as jnp
from jax import lax
from jax.experimental import pallas as pl
from jax.experimental.pallas import tpu as pltpu
from jax.sharding import PartitionSpec as P

GROUP_EXPERTS = 24
CAP = 8
LANES = 128
ROUTE_SCALE = 2.827
MIB = 1024 * 1024

BF16 = jnp.bfloat16
F32 = jnp.float32
VMEM = pl.BlockSpec(memory_space=pltpu.VMEM)
ANY = pl.BlockSpec(memory_space=pl.ANY)


def params(nbytes):
    return pltpu.CompilerParams(vmem_limit_bytes=2 * nbytes + 4 * MIB)


def named(ids, expert):
    hit = jnp.zeros(expert.shape, F32)
    for k in range(ids.shape[0]):
        hit = jnp.where(ids[k : k + 1, :] == expert, 1.0, hit)
    return hit


def upto(count):
    return (
        lax.broadcasted_iota(jnp.int32, (count, count), 0)
        <= lax.broadcasted_iota(jnp.int32, (count, count), 1)
    ).astype(BF16)


def placing(ids, groups, me, before):
    rows, count = groups * CAP, ids.shape[1]
    row = lax.broadcasted_iota(jnp.int32, (rows, count), 0)
    group = (row // CAP) ^ me
    hit = named(ids, group * GROUP_EXPERTS)
    rank = jnp.dot(hit.astype(BF16), before, preferred_element_type=F32)
    slot = lax.rem(row, CAP).astype(F32)
    return jnp.where((hit > 0.5) & (rank == slot + 1.0), 1.0, 0.0), group


def dispatch_kernel(groups, width, ids_ref, tokens_ref, *refs):
    outs, (ids_held, staged, before_ref, sems) = refs[:groups], refs[groups:]
    me = lax.axis_index("grp")
    features = tokens_ref.shape[1]
    first = pltpu.make_async_copy(ids_ref, ids_held, sems.at[features // width])
    first.start()
    copies = []
    for c in range(features // width):
        part = pl.ds(c * width, width)
        copies.append(pltpu.make_async_copy(tokens_ref.at[:, part], staged.at[:, part], sems.at[c]))
        copies[-1].start()
    before_ref[...] = upto(tokens_ref.shape[0])
    first.wait()
    place, _ = placing(ids_held[...], groups, me, before_ref[...])
    live = jnp.sum(place, axis=1, keepdims=True)
    place = place.astype(BF16)
    for d in range(groups):
        outs[d][:, features:] = jnp.broadcast_to(live[d * CAP : (d + 1) * CAP], (CAP, LANES)).astype(BF16)
    for c in range(features // width):
        copies[c].wait()
        part = slice(c * width, (c + 1) * width)
        rows = jnp.dot(place, staged[:, part], preferred_element_type=F32)
        for d in range(groups):
            outs[d][:, part] = rows[d * CAP : (d + 1) * CAP].astype(BF16)


def prepare_kernel(groups, after_ref, ids_ref, logits_ref, *refs):
    del after_ref
    weights, loaded, (out_ref, ids_held, logits_held, sems) = refs[:3], refs[3:6], refs[6:]
    small = [
        pltpu.make_async_copy(ids_ref, ids_held, sems.at[12]),
        pltpu.make_async_copy(logits_ref, logits_held, sems.at[13]),
    ]
    for copy in small:
        copy.start()
    copies = []
    for k in range(3):
        depth = weights[k].shape[0]
        for c in range(4):
            part = pl.ds(c * (depth // 4), depth // 4)
            copies.append(pltpu.make_async_copy(weights[k].at[part], loaded[k].at[part], sems.at[4 * k + c]))
            copies[-1].start()
    for copy in small:
        copy.wait()
    me = lax.axis_index("grp")
    ids = ids_held[...]
    place, group = placing(ids, groups, me, upto(ids.shape[1]))
    scores = 1.0 / (1.0 + jnp.exp(-logits_held[...]))
    expert = lax.broadcasted_iota(jnp.int32, scores.shape, 0)
    chosen = jnp.sum(jnp.where(named(ids, expert) > 0.5, scores, 0.0), axis=0, keepdims=True)
    leading = jnp.zeros(place.shape, F32)
    for g in range(groups):
        leading = jnp.where(group == g, scores[g * GROUP_EXPERTS : g * GROUP_EXPERTS + 1, :], leading)
    weight = (ROUTE_SCALE * leading / chosen).astype(BF16).astype(F32)
    out_ref[...] = jnp.where(place > 0.5, weight, 0.0).astype(BF16)
    for copy in copies:
        copy.wait()


def compact_kernel(groups, slots, *refs):
    arrived, (out_ref, pick_ref) = refs[:groups], refs[groups:]
    rows, features = groups * CAP, out_ref.shape[1]
    live = jnp.concatenate([a[:, features:].astype(F32) for a in arrived], axis=0)
    row = lax.broadcasted_iota(jnp.int32, (rows, rows), 0)
    column = lax.broadcasted_iota(jnp.int32, (rows, rows), 1)
    rank = jnp.dot((column <= row).astype(BF16), live.astype(BF16), preferred_element_type=F32)
    lane = lax.broadcasted_iota(jnp.int32, (rows, LANES), 1).astype(F32)
    pick = jnp.where((live > 0.5) & (rank == lane + 1.0), 1.0, 0.0).astype(BF16)
    pick_ref[...] = pick
    step = 512
    for c in range(features // step):
        part = slice(c * step, (c + 1) * step)
        whole = jnp.concatenate([a[:, part].astype(F32) for a in arrived], axis=0).astype(BF16)
        out_ref[:, part] = lax.dot_general(
            pick[:, :slots], whole, (((0,), (0,)), ((), ())), preferred_element_type=F32
        ).astype(BF16)


def hidden_kernel(columns, *refs):
    blocks, (gate_ref, up_ref, hidden_ref, held) = refs[:columns], refs[columns:]
    slots = blocks[0].shape[0]
    units = gate_ref.shape[1]
    for e in range(columns):
        held[e * slots : (e + 1) * slots, :] = blocks[e][...]
    step = min(256, units)
    for c in range(units // step):
        part = slice(c * step, (c + 1) * step)
        gate = jnp.dot(held[...], gate_ref[:, part], preferred_element_type=F32)
        up = jnp.dot(held[...], up_ref[:, part], preferred_element_type=F32)
        hidden_ref[:, part] = (gate / (1.0 + jnp.exp(-gate)) * up).astype(BF16)


def down_kernel(columns, *refs):
    hiddens, down_ref, outs = refs[:columns], refs[columns], refs[columns + 1 :]
    me = lax.axis_index("ing")
    rows, units = hiddens[0].shape
    slots = rows // columns
    total = jnp.zeros((rows, down_ref.shape[1]), F32)
    for f in range(columns):
        block = jnp.concatenate(
            [hiddens[f][slots * (e ^ f) : slots * ((e ^ f) + 1), :] for e in range(columns)], axis=0
        )
        at = pl.multiple_of((me ^ f) * units, units)
        total += jnp.dot(block, down_ref[pl.ds(at, units), :], preferred_element_type=F32)
    for e in range(columns):
        outs[e][...] = total[e * slots : (e + 1) * slots].astype(BF16)


def spread_kernel(groups, columns, pick_ref, *refs):
    blocks, outs = refs[:columns], refs[columns:]
    for e in range(columns):
        block = blocks[e][...]
        back = jnp.dot(pick_ref[:, : block.shape[0]], block, preferred_element_type=F32)
        for d in range(groups):
            outs[d][e] = back[d * CAP : (d + 1) * CAP].astype(BF16)


def combine_kernel(groups, columns, mixing_ref, *refs):
    backs, (out_ref, held, sems) = refs[:groups], refs[groups:]
    me = lax.axis_index("ing")
    width = backs[0].shape[2]
    copies = []
    for e in range(columns):
        rows = jnp.concatenate([backs[d][e].astype(F32) for d in range(groups)], axis=0)
        value = lax.dot_general(
            mixing_ref[...], rows.astype(BF16), (((0,), (0,)), ((), ())), preferred_element_type=F32
        )
        part = pl.ds(e * width, width)
        held[:, part] = value.astype(BF16)
        there = pl.ds(pl.multiple_of((me ^ e) * width, width), width)
        copies.append(pltpu.make_async_copy(held.at[:, part], out_ref.at[:, there], sems.at[e]))
        copies[-1].start()
    for copy in copies:
        copy.wait()


def swap(x, name, step):
    if step == 0:
        return x
    return lax.ppermute(x, name, [(a, a ^ step) for a in range(lax.axis_size(name))])


def local(tokens, router_logits, expert_ids, w_gate, w_up, w_down):
    groups = lax.axis_size("grp")
    columns = lax.axis_size("ing")
    count, features = tokens.shape
    units, share = w_gate.shape[2], w_down.shape[2]
    slots = groups * CAP // 2
    wide = features + LANES
    ids = pltpu.with_memory_space_constraint(expert_ids.T, pltpu.HBM)
    logits = pltpu.with_memory_space_constraint(router_logits.T, pltpu.HBM)

    outbound = pl.pallas_call(
        functools.partial(dispatch_kernel, groups, 512),
        out_shape=[jax.ShapeDtypeStruct((CAP, wide), BF16)] * groups,
        in_specs=[ANY, ANY],
        out_specs=[VMEM] * groups,
        scratch_shapes=[
            pltpu.VMEM(ids.shape, jnp.int32),
            pltpu.VMEM((count, features), BF16),
            pltpu.VMEM((count, count), BF16),
            pltpu.SemaphoreType.DMA((features // 512 + 1,)),
        ],
        compiler_params=params(2 * count * features),
        name="dispatch",
    )(ids, pltpu.with_memory_space_constraint(tokens, pltpu.HBM))
    arrived = [swap(outbound[d], "grp", d) for d in range(groups)]

    compacted, pick = pl.pallas_call(
        functools.partial(compact_kernel, groups, slots),
        out_shape=[
            jax.ShapeDtypeStruct((slots, features), BF16),
            jax.ShapeDtypeStruct((groups * CAP, LANES), BF16),
        ],
        in_specs=[VMEM] * groups,
        out_specs=[VMEM, VMEM],
        compiler_params=params(2 * (groups * CAP + slots) * wide),
        name="compact",
    )(*arrived)
    blocks = [swap(compacted, "ing", e) for e in range(columns)]

    weights = [w_gate[0], w_up[0], w_down[0]]
    gate, up, down, mixing = pl.pallas_call(
        functools.partial(prepare_kernel, groups),
        out_shape=[pltpu.VMEM(w.shape, BF16) for w in weights]
        + [jax.ShapeDtypeStruct((groups * CAP, count), BF16)],
        in_specs=[ANY] * 6,
        out_specs=[VMEM] * 4,
        scratch_shapes=[
            pltpu.VMEM(ids.shape, jnp.int32),
            pltpu.VMEM(logits.shape, F32),
            pltpu.SemaphoreType.DMA((14,)),
        ],
        compiler_params=params(0),
        name="prepare",
    )(
        pick,
        ids,
        logits,
        *[pltpu.with_memory_space_constraint(w, pltpu.HBM) for w in weights],
    )

    hidden = pl.pallas_call(
        functools.partial(hidden_kernel, columns),
        out_shape=jax.ShapeDtypeStruct((columns * slots, units), BF16),
        in_specs=[VMEM] * (columns + 2),
        out_specs=VMEM,
        scratch_shapes=[pltpu.VMEM((columns * slots, features), BF16)],
        compiler_params=params(2 * columns * slots * (2 * features + units)),
        name="hidden",
    )(*blocks, gate, up)
    hiddens = [swap(hidden, "ing", f) for f in range(columns)]

    results = pl.pallas_call(
        functools.partial(down_kernel, columns),
        out_shape=[jax.ShapeDtypeStruct((slots, share), BF16)] * columns,
        in_specs=[VMEM] * (columns + 1),
        out_specs=[VMEM] * columns,
        compiler_params=params(2 * columns * slots * (columns * units + 4 * share)),
        name="down",
    )(*hiddens, down)
    results = [swap(results[e], "ing", e) for e in range(columns)]

    backs = pl.pallas_call(
        functools.partial(spread_kernel, groups, columns),
        out_shape=[jax.ShapeDtypeStruct((columns, CAP, share), BF16)] * groups,
        in_specs=[VMEM] * (columns + 1),
        out_specs=[VMEM] * groups,
        compiler_params=params(2 * (groups * CAP + slots) * features),
        name="spread",
    )(pick, *results)
    backs = [swap(backs[d], "grp", d) for d in range(groups)]

    if share % LANES:
        me = lax.axis_index("ing")
        rows = jnp.stack(backs)[:, jnp.arange(columns) ^ me]
        rows = rows.transpose(0, 2, 1, 3).reshape(groups * CAP, features)
        return jnp.dot(mixing.T, rows, preferred_element_type=F32).astype(BF16)
    return pl.pallas_call(
        functools.partial(combine_kernel, groups, columns),
        out_shape=jax.ShapeDtypeStruct((count, features), BF16),
        in_specs=[VMEM] * (1 + groups),
        out_specs=ANY,
        scratch_shapes=[pltpu.VMEM((count, features), BF16), pltpu.SemaphoreType.DMA((columns,))],
        compiler_params=params(2 * (count + groups * CAP) * features),
        name="combine",
    )(mixing, *backs)


def solution(mesh):
    placed = (
        P(("rep", "grp", "ing"), None),
        P(("rep", "grp", "ing"), None),
        P(("rep", "grp", "ing"), None),
        P("grp", None, "ing"),
        P("grp", None, "ing"),
        P("grp", None, "ing"),
    )
    return jax.shard_map(
        local, mesh=mesh, in_specs=placed, out_specs=P(("rep", "grp", "ing"), None), check_vma=False
    )
```

```python
import functools

import jax
import jax.numpy as jnp
from jax import lax
from jax.experimental import pallas as pl
from jax.experimental.pallas import tpu as pltpu
from jax.sharding import PartitionSpec as P

GROUP_EXPERTS = 24
CAP = 8
LANES = 128
ROUTE_SCALE = 2.827
MIB = 1024 * 1024

BF16 = jnp.bfloat16
F32 = jnp.float32
VMEM = pl.BlockSpec(memory_space=pltpu.VMEM)
ANY = pl.BlockSpec(memory_space=pl.ANY)


def params(nbytes):
    return pltpu.CompilerParams(vmem_limit_bytes=2 * nbytes + 4 * MIB)


def named(ids, expert):
    hit = jnp.zeros(expert.shape, F32)
    for k in range(ids.shape[0]):
        hit = jnp.where(ids[k : k + 1, :] == expert, 1.0, hit)
    return hit


def upto(count):
    return (
        lax.broadcasted_iota(jnp.int32, (count, count), 0)
        <= lax.broadcasted_iota(jnp.int32, (count, count), 1)
    ).astype(BF16)


def placing(ids, groups, me, before):
    rows, count = groups * CAP, ids.shape[1]
    row = lax.broadcasted_iota(jnp.int32, (rows, count), 0)
    group = (row // CAP) ^ me
    hit = named(ids, group * GROUP_EXPERTS)
    rank = jnp.dot(hit.astype(BF16), before, preferred_element_type=F32)
    slot = lax.rem(row, CAP).astype(F32)
    return jnp.where((hit > 0.5) & (rank == slot + 1.0), 1.0, 0.0), group


def dispatch_kernel(groups, width, ids_ref, tokens_ref, *refs):
    outs, (ids_held, staged, before_ref, sems) = refs[:groups], refs[groups:]
    me = lax.axis_index("grp")
    features = tokens_ref.shape[1]
    first = pltpu.make_async_copy(ids_ref, ids_held, sems.at[features // width])
    first.start()
    copies = []
    for c in range(features // width):
        part = pl.ds(c * width, width)
        copies.append(pltpu.make_async_copy(tokens_ref.at[:, part], staged.at[:, part], sems.at[c]))
        copies[-1].start()
    before_ref[...] = upto(tokens_ref.shape[0])
    first.wait()
    place, _ = placing(ids_held[...], groups, me, before_ref[...])
    live = jnp.sum(place, axis=1, keepdims=True)
    place = place.astype(BF16)
    for d in range(groups):
        outs[d][:, features:] = jnp.broadcast_to(live[d * CAP : (d + 1) * CAP], (CAP, LANES)).astype(BF16)
    for c in range(features // width):
        copies[c].wait()
        part = slice(c * width, (c + 1) * width)
        rows = jnp.dot(place, staged[:, part], preferred_element_type=F32)
        for d in range(groups):
            outs[d][:, part] = rows[d * CAP : (d + 1) * CAP].astype(BF16)


def prepare_kernel(groups, after_ref, ids_ref, logits_ref, *refs):
    del after_ref
    weights, loaded, (out_ref, ids_held, logits_held, sems) = refs[:3], refs[3:6], refs[6:]
    small = [
        pltpu.make_async_copy(ids_ref, ids_held, sems.at[12]),
        pltpu.make_async_copy(logits_ref, logits_held, sems.at[13]),
    ]
    for copy in small:
        copy.start()
    copies = []
    for k in range(3):
        depth = weights[k].shape[0]
        for c in range(4):
            part = pl.ds(c * (depth // 4), depth // 4)
            copies.append(pltpu.make_async_copy(weights[k].at[part], loaded[k].at[part], sems.at[4 * k + c]))
            copies[-1].start()
    for copy in small:
        copy.wait()
    me = lax.axis_index("grp")
    ids = ids_held[...]
    place, group = placing(ids, groups, me, upto(ids.shape[1]))
    scores = 1.0 / (1.0 + jnp.exp(-logits_held[...]))
    expert = lax.broadcasted_iota(jnp.int32, scores.shape, 0)
    chosen = jnp.sum(jnp.where(named(ids, expert) > 0.5, scores, 0.0), axis=0, keepdims=True)
    leading = jnp.zeros(place.shape, F32)
    for g in range(groups):
        leading = jnp.where(group == g, scores[g * GROUP_EXPERTS : g * GROUP_EXPERTS + 1, :], leading)
    weight = (ROUTE_SCALE * leading / chosen).astype(BF16).astype(F32)
    out_ref[...] = jnp.where(place > 0.5, weight, 0.0).T.astype(BF16)
    for copy in copies:
        copy.wait()


def compact_kernel(groups, slots, *refs):
    arrived, (out_ref, pick_ref) = refs[:groups], refs[groups:]
    rows, features = groups * CAP, out_ref.shape[1]
    live = jnp.concatenate([a[:, features:].astype(F32) for a in arrived], axis=0)
    row = lax.broadcasted_iota(jnp.int32, (rows, rows), 0)
    column = lax.broadcasted_iota(jnp.int32, (rows, rows), 1)
    rank = jnp.dot((column <= row).astype(BF16), live.astype(BF16), preferred_element_type=F32)
    lane = lax.broadcasted_iota(jnp.int32, (rows, LANES), 1).astype(F32)
    pick = jnp.where((live > 0.5) & (rank == lane + 1.0), 1.0, 0.0).astype(BF16)
    pick_ref[...] = pick
    step = 512
    for c in range(features // step):
        part = slice(c * step, (c + 1) * step)
        whole = jnp.concatenate([a[:, part].astype(F32) for a in arrived], axis=0).astype(BF16)
        out_ref[:, part] = lax.dot_general(
            pick[:, :slots], whole, (((0,), (0,)), ((), ())), preferred_element_type=F32
        ).astype(BF16)


def hidden_kernel(columns, *refs):
    blocks, (gate_ref, up_ref, hidden_ref, held) = refs[:columns], refs[columns:]
    slots = blocks[0].shape[0]
    units = gate_ref.shape[1]
    for e in range(columns):
        held[e * slots : (e + 1) * slots, :] = blocks[e][...]
    step = min(256, units)
    for c in range(units // step):
        part = slice(c * step, (c + 1) * step)
        gate = jnp.dot(held[...], gate_ref[:, part], preferred_element_type=F32)
        up = jnp.dot(held[...], up_ref[:, part], preferred_element_type=F32)
        hidden_ref[:, part] = (gate / (1.0 + jnp.exp(-gate)) * up).astype(BF16)


def down_kernel(columns, *refs):
    hiddens, down_ref, outs = refs[:columns], refs[columns], refs[columns + 1 :]
    me = lax.axis_index("ing")
    rows, units = hiddens[0].shape
    slots = rows // columns
    total = jnp.zeros((rows, down_ref.shape[1]), F32)
    for f in range(columns):
        block = jnp.concatenate(
            [hiddens[f][slots * (e ^ f) : slots * ((e ^ f) + 1), :] for e in range(columns)], axis=0
        )
        at = pl.multiple_of((me ^ f) * units, units)
        total += jnp.dot(block, down_ref[pl.ds(at, units), :], preferred_element_type=F32)
    for e in range(columns):
        outs[e][...] = total[e * slots : (e + 1) * slots].astype(BF16)


def spread_kernel(groups, columns, pick_ref, *refs):
    blocks, outs = refs[:columns], refs[columns:]
    for e in range(columns):
        block = blocks[e][...]
        back = jnp.dot(pick_ref[:, : block.shape[0]], block, preferred_element_type=F32)
        for d in range(groups):
            outs[d][e] = back[d * CAP : (d + 1) * CAP].astype(BF16)


def combine_kernel(groups, columns, mixing_ref, *refs):
    backs, (out_ref, held, sems) = refs[:groups], refs[groups:]
    me = lax.axis_index("ing")
    width = backs[0].shape[2]
    copies = []
    for e in range(columns):
        rows = jnp.concatenate([backs[d][e].astype(F32) for d in range(groups)], axis=0)
        value = jnp.dot(mixing_ref[...], rows.astype(BF16), preferred_element_type=F32)
        part = pl.ds(e * width, width)
        held[:, part] = value.astype(BF16)
        there = pl.ds(pl.multiple_of((me ^ e) * width, width), width)
        copies.append(pltpu.make_async_copy(held.at[:, part], out_ref.at[:, there], sems.at[e]))
        copies[-1].start()
    for copy in copies:
        copy.wait()


def swap(x, name, step):
    if step == 0:
        return x
    return lax.ppermute(x, name, [(a, a ^ step) for a in range(lax.axis_size(name))])


def swap_all(parts, name):
    got = {k: swap(parts[k], name, k) for k in reversed(range(len(parts)))}
    return [got[k] for k in range(len(parts))]


def local(tokens, router_logits, expert_ids, w_gate, w_up, w_down):
    groups = lax.axis_size("grp")
    columns = lax.axis_size("ing")
    count, features = tokens.shape
    units, share = w_gate.shape[2], w_down.shape[2]
    slots = groups * CAP // 2
    wide = features + LANES
    ids = pltpu.with_memory_space_constraint(expert_ids.T, pltpu.HBM)
    logits = pltpu.with_memory_space_constraint(router_logits.T, pltpu.HBM)

    outbound = pl.pallas_call(
        functools.partial(dispatch_kernel, groups, 512),
        out_shape=[jax.ShapeDtypeStruct((CAP, wide), BF16)] * groups,
        in_specs=[ANY, ANY],
        out_specs=[VMEM] * groups,
        scratch_shapes=[
            pltpu.VMEM(ids.shape, jnp.int32),
            pltpu.VMEM((count, features), BF16),
            pltpu.VMEM((count, count), BF16),
            pltpu.SemaphoreType.DMA((features // 512 + 1,)),
        ],
        compiler_params=params(2 * count * features),
        name="dispatch",
    )(ids, pltpu.with_memory_space_constraint(tokens, pltpu.HBM))
    arrived = swap_all(outbound, "grp")

    compacted, pick = pl.pallas_call(
        functools.partial(compact_kernel, groups, slots),
        out_shape=[
            jax.ShapeDtypeStruct((slots, features), BF16),
            jax.ShapeDtypeStruct((groups * CAP, LANES), BF16),
        ],
        in_specs=[VMEM] * groups,
        out_specs=[VMEM, VMEM],
        compiler_params=params(2 * (groups * CAP + slots) * wide),
        name="compact",
    )(*arrived)
    blocks = [swap(compacted, "ing", e) for e in range(columns)]

    weights = [w_gate[0], w_up[0], w_down[0]]
    gate, up, down, mixing = pl.pallas_call(
        functools.partial(prepare_kernel, groups),
        out_shape=[pltpu.VMEM(w.shape, BF16) for w in weights]
        + [jax.ShapeDtypeStruct((count, groups * CAP), BF16)],
        in_specs=[ANY] * 6,
        out_specs=[VMEM] * 4,
        scratch_shapes=[
            pltpu.VMEM(ids.shape, jnp.int32),
            pltpu.VMEM(logits.shape, F32),
            pltpu.SemaphoreType.DMA((14,)),
        ],
        compiler_params=params(0),
        name="prepare",
    )(
        pick,
        ids,
        logits,
        *[pltpu.with_memory_space_constraint(w, pltpu.HBM) for w in weights],
    )

    hidden = pl.pallas_call(
        functools.partial(hidden_kernel, columns),
        out_shape=jax.ShapeDtypeStruct((columns * slots, units), BF16),
        in_specs=[VMEM] * (columns + 2),
        out_specs=VMEM,
        scratch_shapes=[pltpu.VMEM((columns * slots, features), BF16)],
        compiler_params=params(2 * columns * slots * (2 * features + units)),
        name="hidden",
    )(*blocks, gate, up)
    hiddens = [swap(hidden, "ing", f) for f in range(columns)]

    results = pl.pallas_call(
        functools.partial(down_kernel, columns),
        out_shape=[jax.ShapeDtypeStruct((slots, share), BF16)] * columns,
        in_specs=[VMEM] * (columns + 1),
        out_specs=[VMEM] * columns,
        compiler_params=params(2 * columns * slots * (columns * units + 4 * share)),
        name="down",
    )(*hiddens, down)
    results = swap_all(results, "ing")

    backs = pl.pallas_call(
        functools.partial(spread_kernel, groups, columns),
        out_shape=[jax.ShapeDtypeStruct((columns, CAP, share), BF16)] * groups,
        in_specs=[VMEM] * (columns + 1),
        out_specs=[VMEM] * groups,
        compiler_params=params(2 * (groups * CAP + slots) * features),
        name="spread",
    )(pick, *results)
    backs = swap_all(backs, "grp")

    if share % LANES:
        me = lax.axis_index("ing")
        rows = jnp.stack(backs)[:, jnp.arange(columns) ^ me]
        rows = rows.transpose(0, 2, 1, 3).reshape(groups * CAP, features)
        return jnp.dot(mixing, rows, preferred_element_type=F32).astype(BF16)
    return pl.pallas_call(
        functools.partial(combine_kernel, groups, columns),
        out_shape=jax.ShapeDtypeStruct((count, features), BF16),
        in_specs=[VMEM] * (1 + groups),
        out_specs=ANY,
        scratch_shapes=[pltpu.VMEM((count, features), BF16), pltpu.SemaphoreType.DMA((columns,))],
        compiler_params=params(2 * (count + groups * CAP) * features),
        name="combine",
    )(mixing, *backs)


def solution(mesh):
    placed = (
        P(("rep", "grp", "ing"), None),
        P(("rep", "grp", "ing"), None),
        P(("rep", "grp", "ing"), None),
        P("grp", None, "ing"),
        P("grp", None, "ing"),
        P("grp", None, "ing"),
    )
    return jax.shard_map(
        local, mesh=mesh, in_specs=placed, out_specs=P(("rep", "grp", "ing"), None), check_vma=False
    )
```

```python
import functools

import jax
import jax.numpy as jnp
from jax import lax
from jax.experimental import pallas as pl
from jax.experimental.pallas import tpu as pltpu
from jax.sharding import PartitionSpec as P

GROUP_EXPERTS = 24
CAP = 8
LANES = 128
ROUTE_SCALE = 2.827
MIB = 1024 * 1024

BF16 = jnp.bfloat16
F32 = jnp.float32
VMEM = pl.BlockSpec(memory_space=pltpu.VMEM)
ANY = pl.BlockSpec(memory_space=pl.ANY)


def params(nbytes):
    return pltpu.CompilerParams(vmem_limit_bytes=2 * nbytes + 4 * MIB)


def named(ids, expert):
    hit = jnp.zeros(expert.shape, F32)
    for k in range(ids.shape[0]):
        hit = jnp.where(ids[k : k + 1, :] == expert, 1.0, hit)
    return hit


def upto(count):
    return (
        lax.broadcasted_iota(jnp.int32, (count, count), 0)
        <= lax.broadcasted_iota(jnp.int32, (count, count), 1)
    ).astype(BF16)


def placing(ids, groups, me, before):
    rows, count = groups * CAP, ids.shape[1]
    row = lax.broadcasted_iota(jnp.int32, (rows, count), 0)
    group = (row // CAP) ^ me
    hit = named(ids, group * GROUP_EXPERTS)
    rank = jnp.dot(hit.astype(BF16), before, preferred_element_type=F32)
    slot = lax.rem(row, CAP).astype(F32)
    return jnp.where((hit > 0.5) & (rank == slot + 1.0), 1.0, 0.0), group


def dispatch_kernel(groups, width, ids_ref, tokens_ref, *refs):
    outs, (ids_held, staged, before_ref, sems) = refs[:groups], refs[groups:]
    me = lax.axis_index("grp")
    features = tokens_ref.shape[1]
    first = pltpu.make_async_copy(ids_ref, ids_held, sems.at[features // width])
    first.start()
    copies = []
    for c in range(features // width):
        part = pl.ds(c * width, width)
        copies.append(pltpu.make_async_copy(tokens_ref.at[:, part], staged.at[:, part], sems.at[c]))
        copies[-1].start()
    before_ref[...] = upto(tokens_ref.shape[0])
    first.wait()
    place, _ = placing(ids_held[...], groups, me, before_ref[...])
    live = jnp.sum(place, axis=1, keepdims=True)
    place = place.astype(BF16)
    for d in range(groups):
        outs[d][:, features:] = jnp.broadcast_to(live[d * CAP : (d + 1) * CAP], (CAP, LANES)).astype(BF16)
    for c in range(features // width):
        copies[c].wait()
        part = slice(c * width, (c + 1) * width)
        rows = jnp.dot(place, staged[:, part], preferred_element_type=F32)
        for d in range(groups):
            outs[d][:, part] = rows[d * CAP : (d + 1) * CAP].astype(BF16)


def prepare_kernel(groups, after_ref, ids_ref, logits_ref, *refs):
    del after_ref
    weights, loaded, (out_ref, ids_held, logits_held, sems) = refs[:3], refs[3:6], refs[6:]
    small = [
        pltpu.make_async_copy(ids_ref, ids_held, sems.at[12]),
        pltpu.make_async_copy(logits_ref, logits_held, sems.at[13]),
    ]
    for copy in small:
        copy.start()
    copies = []
    for k in range(3):
        depth = weights[k].shape[0]
        for c in range(4):
            part = pl.ds(c * (depth // 4), depth // 4)
            copies.append(pltpu.make_async_copy(weights[k].at[part], loaded[k].at[part], sems.at[4 * k + c]))
            copies[-1].start()
    for copy in small:
        copy.wait()
    me = lax.axis_index("grp")
    ids = ids_held[...]
    place, group = placing(ids, groups, me, upto(ids.shape[1]))
    scores = 1.0 / (1.0 + jnp.exp(-logits_held[...]))
    expert = lax.broadcasted_iota(jnp.int32, scores.shape, 0)
    chosen = jnp.sum(jnp.where(named(ids, expert) > 0.5, scores, 0.0), axis=0, keepdims=True)
    leading = jnp.zeros(place.shape, F32)
    for g in range(groups):
        leading = jnp.where(group == g, scores[g * GROUP_EXPERTS : g * GROUP_EXPERTS + 1, :], leading)
    weight = (ROUTE_SCALE * leading / chosen).astype(BF16).astype(F32)
    out_ref[...] = jnp.where(place > 0.5, weight, 0.0).T.astype(BF16)
    for copy in copies:
        copy.wait()


def compact_kernel(groups, slots, *refs):
    arrived, (out_ref, pick_ref) = refs[:groups][::-1], refs[groups:]
    rows, features = groups * CAP, out_ref.shape[1]
    live = jnp.concatenate([a[:, features:].astype(F32) for a in arrived], axis=0)
    row = lax.broadcasted_iota(jnp.int32, (rows, rows), 0)
    column = lax.broadcasted_iota(jnp.int32, (rows, rows), 1)
    rank = jnp.dot((column <= row).astype(BF16), live.astype(BF16), preferred_element_type=F32)
    lane = lax.broadcasted_iota(jnp.int32, (rows, LANES), 1).astype(F32)
    pick = jnp.where((live > 0.5) & (rank == lane + 1.0), 1.0, 0.0).astype(BF16)
    pick_ref[...] = pick
    step = 512
    for c in range(features // step):
        part = slice(c * step, (c + 1) * step)
        whole = jnp.concatenate([a[:, part].astype(F32) for a in arrived], axis=0).astype(BF16)
        out_ref[:, part] = lax.dot_general(
            pick[:, :slots], whole, (((0,), (0,)), ((), ())), preferred_element_type=F32
        ).astype(BF16)


def hidden_kernel(columns, *refs):
    blocks, (gate_ref, up_ref, hidden_ref, held) = refs[:columns], refs[columns:]
    slots = blocks[0].shape[0]
    units = gate_ref.shape[1]
    for e in range(columns):
        held[e * slots : (e + 1) * slots, :] = blocks[e][...]
    step = min(256, units)
    for c in range(units // step):
        part = slice(c * step, (c + 1) * step)
        gate = jnp.dot(held[...], gate_ref[:, part], preferred_element_type=F32)
        up = jnp.dot(held[...], up_ref[:, part], preferred_element_type=F32)
        hidden_ref[:, part] = (gate / (1.0 + jnp.exp(-gate)) * up).astype(BF16)


def down_kernel(columns, *refs):
    hiddens, down_ref, outs = refs[:columns], refs[columns], refs[columns + 1 :]
    me = lax.axis_index("ing")
    rows, units = hiddens[0].shape
    slots = rows // columns
    total = jnp.zeros((rows, down_ref.shape[1]), F32)
    for f in range(columns):
        block = jnp.concatenate(
            [hiddens[f][slots * (e ^ f) : slots * ((e ^ f) + 1), :] for e in range(columns)], axis=0
        )
        at = pl.multiple_of((me ^ f) * units, units)
        total += jnp.dot(block, down_ref[pl.ds(at, units), :], preferred_element_type=F32)
    for e in range(columns):
        outs[e][...] = total[e * slots : (e + 1) * slots].astype(BF16)


def spread_kernel(groups, columns, pick_ref, *refs):
    blocks, outs = refs[:columns][::-1], refs[columns:]
    for e in range(columns):
        block = blocks[e][...]
        back = jnp.dot(pick_ref[:, : block.shape[0]], block, preferred_element_type=F32)
        for d in range(groups):
            outs[d][e] = back[d * CAP : (d + 1) * CAP].astype(BF16)


def combine_kernel(groups, columns, mixing_ref, *refs):
    backs, (out_ref, held, sems) = refs[:groups][::-1], refs[groups:]
    me = lax.axis_index("ing")
    width = backs[0].shape[2]
    copies = []
    for e in range(columns):
        rows = jnp.concatenate([backs[d][e].astype(F32) for d in range(groups)], axis=0)
        value = jnp.dot(mixing_ref[...], rows.astype(BF16), preferred_element_type=F32)
        part = pl.ds(e * width, width)
        held[:, part] = value.astype(BF16)
        there = pl.ds(pl.multiple_of((me ^ e) * width, width), width)
        copies.append(pltpu.make_async_copy(held.at[:, part], out_ref.at[:, there], sems.at[e]))
        copies[-1].start()
    for copy in copies:
        copy.wait()


def swap(x, name, step):
    if step == 0:
        return x
    return lax.ppermute(x, name, [(a, a ^ step) for a in range(lax.axis_size(name))])


def swap_all(parts, name):
    return [swap(part, name, k) for k, part in enumerate(parts)][::-1]


def local(tokens, router_logits, expert_ids, w_gate, w_up, w_down):
    groups = lax.axis_size("grp")
    columns = lax.axis_size("ing")
    count, features = tokens.shape
    units, share = w_gate.shape[2], w_down.shape[2]
    slots = groups * CAP // 2
    wide = features + LANES
    ids = pltpu.with_memory_space_constraint(expert_ids.T, pltpu.HBM)
    logits = pltpu.with_memory_space_constraint(router_logits.T, pltpu.HBM)

    outbound = pl.pallas_call(
        functools.partial(dispatch_kernel, groups, 512),
        out_shape=[jax.ShapeDtypeStruct((CAP, wide), BF16)] * groups,
        in_specs=[ANY, ANY],
        out_specs=[VMEM] * groups,
        scratch_shapes=[
            pltpu.VMEM(ids.shape, jnp.int32),
            pltpu.VMEM((count, features), BF16),
            pltpu.VMEM((count, count), BF16),
            pltpu.SemaphoreType.DMA((features // 512 + 1,)),
        ],
        compiler_params=params(2 * count * features),
        name="dispatch",
    )(ids, pltpu.with_memory_space_constraint(tokens, pltpu.HBM))
    arrived = swap_all(outbound, "grp")

    compacted, pick = pl.pallas_call(
        functools.partial(compact_kernel, groups, slots),
        out_shape=[
            jax.ShapeDtypeStruct((slots, features), BF16),
            jax.ShapeDtypeStruct((groups * CAP, LANES), BF16),
        ],
        in_specs=[VMEM] * groups,
        out_specs=[VMEM, VMEM],
        compiler_params=params(2 * (groups * CAP + slots) * wide),
        name="compact",
    )(*arrived)
    blocks = [swap(compacted, "ing", e) for e in range(columns)]

    weights = [w_gate[0], w_up[0], w_down[0]]
    gate, up, down, mixing = pl.pallas_call(
        functools.partial(prepare_kernel, groups),
        out_shape=[pltpu.VMEM(w.shape, BF16) for w in weights]
        + [jax.ShapeDtypeStruct((count, groups * CAP), BF16)],
        in_specs=[ANY] * 6,
        out_specs=[VMEM] * 4,
        scratch_shapes=[
            pltpu.VMEM(ids.shape, jnp.int32),
            pltpu.VMEM(logits.shape, F32),
            pltpu.SemaphoreType.DMA((14,)),
        ],
        compiler_params=params(0),
        name="prepare",
    )(
        pick,
        ids,
        logits,
        *[pltpu.with_memory_space_constraint(w, pltpu.HBM) for w in weights],
    )

    hidden = pl.pallas_call(
        functools.partial(hidden_kernel, columns),
        out_shape=jax.ShapeDtypeStruct((columns * slots, units), BF16),
        in_specs=[VMEM] * (columns + 2),
        out_specs=VMEM,
        scratch_shapes=[pltpu.VMEM((columns * slots, features), BF16)],
        compiler_params=params(2 * columns * slots * (2 * features + units)),
        name="hidden",
    )(*blocks, gate, up)
    hiddens = [swap(hidden, "ing", f) for f in range(columns)]

    results = pl.pallas_call(
        functools.partial(down_kernel, columns),
        out_shape=[jax.ShapeDtypeStruct((slots, share), BF16)] * columns,
        in_specs=[VMEM] * (columns + 1),
        out_specs=[VMEM] * columns,
        compiler_params=params(2 * columns * slots * (columns * units + 4 * share)),
        name="down",
    )(*hiddens, down)
    results = swap_all(results, "ing")

    backs = pl.pallas_call(
        functools.partial(spread_kernel, groups, columns),
        out_shape=[jax.ShapeDtypeStruct((columns, CAP, share), BF16)] * groups,
        in_specs=[VMEM] * (columns + 1),
        out_specs=[VMEM] * groups,
        compiler_params=params(2 * (groups * CAP + slots) * features),
        name="spread",
    )(pick, *results)
    backs = swap_all(backs, "grp")

    if share % LANES:
        me = lax.axis_index("ing")
        rows = jnp.stack(backs[::-1])[:, jnp.arange(columns) ^ me]
        rows = rows.transpose(0, 2, 1, 3).reshape(groups * CAP, features)
        return jnp.dot(mixing, rows, preferred_element_type=F32).astype(BF16)
    return pl.pallas_call(
        functools.partial(combine_kernel, groups, columns),
        out_shape=jax.ShapeDtypeStruct((count, features), BF16),
        in_specs=[VMEM] * (1 + groups),
        out_specs=ANY,
        scratch_shapes=[pltpu.VMEM((count, features), BF16), pltpu.SemaphoreType.DMA((columns,))],
        compiler_params=params(2 * (count + groups * CAP) * features),
        name="combine",
    )(mixing, *backs)


def solution(mesh):
    placed = (
        P(("rep", "grp", "ing"), None),
        P(("rep", "grp", "ing"), None),
        P(("rep", "grp", "ing"), None),
        P("grp", None, "ing"),
        P("grp", None, "ing"),
        P("grp", None, "ing"),
    )
    return jax.shard_map(
        local, mesh=mesh, in_specs=placed, out_specs=P(("rep", "grp", "ing"), None), check_vma=False
    )
```

```python
import functools

import jax
import jax.numpy as jnp
from jax import lax
from jax.experimental import pallas as pl
from jax.experimental.pallas import tpu as pltpu
from jax.sharding import PartitionSpec as P

GROUP_EXPERTS = 24
CAP = 8
LANES = 128
ROUTE_SCALE = 2.827
MIB = 1024 * 1024

BF16 = jnp.bfloat16
F32 = jnp.float32
VMEM = pl.BlockSpec(memory_space=pltpu.VMEM)
ANY = pl.BlockSpec(memory_space=pl.ANY)


def params(nbytes):
    return pltpu.CompilerParams(vmem_limit_bytes=2 * nbytes + 4 * MIB)


def named(ids, expert):
    hit = jnp.zeros(expert.shape, F32)
    for k in range(ids.shape[0]):
        hit = jnp.where(ids[k : k + 1, :] == expert, 1.0, hit)
    return hit


def upto(count):
    return (
        lax.broadcasted_iota(jnp.int32, (count, count), 0)
        <= lax.broadcasted_iota(jnp.int32, (count, count), 1)
    ).astype(BF16)


def placing(ids, groups, me, before):
    rows, count = groups * CAP, ids.shape[1]
    row = lax.broadcasted_iota(jnp.int32, (rows, count), 0)
    group = (row // CAP) ^ me
    hit = named(ids, group * GROUP_EXPERTS)
    rank = jnp.dot(hit.astype(BF16), before, preferred_element_type=F32)
    slot = lax.rem(row, CAP).astype(F32)
    return jnp.where((hit > 0.5) & (rank == slot + 1.0), 1.0, 0.0), group


def dispatch_kernel(groups, width, ids_ref, tokens_ref, *refs):
    outs, (ids_held, staged, before_ref, sems) = refs[:groups], refs[groups:]
    me = lax.axis_index("grp")
    features = tokens_ref.shape[1]
    first = pltpu.make_async_copy(ids_ref, ids_held, sems.at[features // width])
    first.start()
    copies = []
    for c in range(features // width):
        part = pl.ds(c * width, width)
        copies.append(pltpu.make_async_copy(tokens_ref.at[:, part], staged.at[:, part], sems.at[c]))
        copies[-1].start()
    before_ref[...] = upto(tokens_ref.shape[0])
    first.wait()
    place, _ = placing(ids_held[...], groups, me, before_ref[...])
    live = jnp.sum(place, axis=1, keepdims=True)
    place = place.astype(BF16)
    for d in range(groups):
        outs[d][:, features:] = jnp.broadcast_to(live[d * CAP : (d + 1) * CAP], (CAP, LANES)).astype(BF16)
    for c in range(features // width):
        copies[c].wait()
        part = slice(c * width, (c + 1) * width)
        rows = jnp.dot(place, staged[:, part], preferred_element_type=F32)
        for d in range(groups):
            outs[d][:, part] = rows[d * CAP : (d + 1) * CAP].astype(BF16)


def start_loads(weights, loaded, sems):
    copies = []
    for k in range(len(weights)):
        depth = weights[k].shape[0]
        for c in range(4):
            part = pl.ds(c * (depth // 4), depth // 4)
            copies.append(pltpu.make_async_copy(weights[k].at[part], loaded[k].at[part], sems.at[4 * k + c]))
            copies[-1].start()
    return copies


def load_kernel(after_ref, gate_ref, up_ref, gate_out, up_out, sems):
    del after_ref
    for copy in start_loads([gate_ref, up_ref], [gate_out, up_out], sems):
        copy.wait()


def prepare_kernel(groups, after_ref, ids_ref, logits_ref, down_ref, down_out, out_ref, ids_held, logits_held, sems):
    del after_ref
    small = [
        pltpu.make_async_copy(ids_ref, ids_held, sems.at[4]),
        pltpu.make_async_copy(logits_ref, logits_held, sems.at[5]),
    ]
    for copy in small:
        copy.start()
    copies = start_loads([down_ref], [down_out], sems)
    for copy in small:
        copy.wait()
    me = lax.axis_index("grp")
    ids = ids_held[...]
    place, group = placing(ids, groups, me, upto(ids.shape[1]))
    scores = 1.0 / (1.0 + jnp.exp(-logits_held[...]))
    expert = lax.broadcasted_iota(jnp.int32, scores.shape, 0)
    chosen = jnp.sum(jnp.where(named(ids, expert) > 0.5, scores, 0.0), axis=0, keepdims=True)
    leading = jnp.zeros(place.shape, F32)
    for g in range(groups):
        leading = jnp.where(group == g, scores[g * GROUP_EXPERTS : g * GROUP_EXPERTS + 1, :], leading)
    weight = (ROUTE_SCALE * leading / chosen).astype(BF16).astype(F32)
    out_ref[...] = jnp.where(place > 0.5, weight, 0.0).T.astype(BF16)
    for copy in copies:
        copy.wait()


def compact_kernel(groups, slots, after_ref, *refs):
    del after_ref
    arrived, (out_ref, low_ref, high_ref, pick_ref) = refs[:groups][::-1], refs[groups:]
    rows, features = groups * CAP, out_ref.shape[1]
    live = jnp.concatenate([a[:, features:].astype(F32) for a in arrived], axis=0)
    row = lax.broadcasted_iota(jnp.int32, (rows, rows), 0)
    column = lax.broadcasted_iota(jnp.int32, (rows, rows), 1)
    rank = jnp.dot((column <= row).astype(BF16), live.astype(BF16), preferred_element_type=F32)
    lane = lax.broadcasted_iota(jnp.int32, (rows, LANES), 1).astype(F32)
    pick = jnp.where((live > 0.5) & (rank == lane + 1.0), 1.0, 0.0).astype(BF16)
    pick_ref[...] = pick
    half = features // 2
    step = 256
    for c in range(features // step):
        part = slice(c * step, (c + 1) * step)
        whole = jnp.concatenate([a[:, part].astype(F32) for a in arrived], axis=0).astype(BF16)
        moved = lax.dot_general(
            pick[:, :slots], whole, (((0,), (0,)), ((), ())), preferred_element_type=F32
        ).astype(BF16)
        out_ref[:, part] = moved
        if (c + 1) * step <= half:
            low_ref[:, part] = moved
        else:
            high_ref[:, c * step - half : (c + 1) * step - half] = moved


def hidden_kernel(columns, forwarded, *refs):
    if forwarded:
        low, high, near, own, middle, far_low, far_high = refs[:7]
    blocks, (gate_ref, up_ref, hidden_ref, held) = refs[:-4], refs[-4:]
    slots = held.shape[0] // columns
    features, units = gate_ref.shape
    if forwarded:
        half = features // 2
        me = lax.axis_index("ing")
        held[:slots, :] = own[...]
        held[slots : 2 * slots, :] = near[...]
        held[2 * slots : 3 * slots, :half] = low[...]
        held[2 * slots : 3 * slots, half:] = high[...]
        inner = (me == 1) | (me == 2)

        @pl.when(inner)
        def _():
            held[3 * slots :, :] = middle[...]

        @pl.when(jnp.logical_not(inner))
        def _():
            held[3 * slots :, :half] = far_low[...]
            held[3 * slots :, half:] = far_high[...]
    else:
        for e in range(columns):
            held[e * slots : (e + 1) * slots, :] = blocks[e][...]
    step = min(256, units)
    for c in range(units // step):
        part = slice(c * step, (c + 1) * step)
        gate = jnp.dot(held[...], gate_ref[:, part], preferred_element_type=F32)
        up = jnp.dot(held[...], up_ref[:, part], preferred_element_type=F32)
        hidden_ref[:, part] = (gate / (1.0 + jnp.exp(-gate)) * up).astype(BF16)


def down_kernel(columns, *refs):
    hiddens, down_ref, outs = refs[:columns], refs[columns], refs[columns + 1 :]
    me = lax.axis_index("ing")
    rows, units = hiddens[0].shape
    slots = rows // columns
    total = jnp.zeros((rows, down_ref.shape[1]), F32)
    for f in range(columns):
        block = jnp.concatenate(
            [hiddens[f][slots * (e ^ f) : slots * ((e ^ f) + 1), :] for e in range(columns)], axis=0
        )
        at = pl.multiple_of((me ^ f) * units, units)
        total += jnp.dot(block, down_ref[pl.ds(at, units), :], preferred_element_type=F32)
    for e in range(columns):
        outs[e][...] = total[e * slots : (e + 1) * slots].astype(BF16)


def spread_kernel(groups, columns, pick_ref, *refs):
    blocks, outs = refs[:columns][::-1], refs[columns:]
    for e in range(columns):
        block = blocks[e][...]
        back = jnp.dot(pick_ref[:, : block.shape[0]], block, preferred_element_type=F32)
        for d in range(groups):
            outs[d][e] = back[d * CAP : (d + 1) * CAP].astype(BF16)


def combine_kernel(groups, columns, mixing_ref, *refs):
    backs, (out_ref, held, sems) = refs[:groups][::-1], refs[groups:]
    me = lax.axis_index("ing")
    width = backs[0].shape[2]
    copies = []
    for e in range(columns):
        rows = jnp.concatenate([backs[d][e].astype(F32) for d in range(groups)], axis=0)
        value = jnp.dot(mixing_ref[...], rows.astype(BF16), preferred_element_type=F32)
        part = pl.ds(e * width, width)
        held[:, part] = value.astype(BF16)
        there = pl.ds(pl.multiple_of((me ^ e) * width, width), width)
        copies.append(pltpu.make_async_copy(held.at[:, part], out_ref.at[:, there], sems.at[e]))
        copies[-1].start()
    for copy in copies:
        copy.wait()


def swap(x, name, step):
    if step == 0:
        return x
    return lax.ppermute(x, name, [(a, a ^ step) for a in range(lax.axis_size(name))])


def swap_all(parts, name):
    return [swap(part, name, k) for k, part in enumerate(parts)][::-1]


def local(tokens, router_logits, expert_ids, w_gate, w_up, w_down):
    groups = lax.axis_size("grp")
    columns = lax.axis_size("ing")
    count, features = tokens.shape
    units, share = w_gate.shape[2], w_down.shape[2]
    slots = groups * CAP // 2
    wide = features + LANES
    ids = pltpu.with_memory_space_constraint(expert_ids.T, pltpu.HBM)
    logits = pltpu.with_memory_space_constraint(router_logits.T, pltpu.HBM)

    outbound = pl.pallas_call(
        functools.partial(dispatch_kernel, groups, 512),
        out_shape=[jax.ShapeDtypeStruct((CAP, wide), BF16)] * groups,
        in_specs=[ANY, ANY],
        out_specs=[VMEM] * groups,
        scratch_shapes=[
            pltpu.VMEM(ids.shape, jnp.int32),
            pltpu.VMEM((count, features), BF16),
            pltpu.VMEM((count, count), BF16),
            pltpu.SemaphoreType.DMA((features // 512 + 1,)),
        ],
        compiler_params=params(2 * count * features),
        name="dispatch",
    )(ids, pltpu.with_memory_space_constraint(tokens, pltpu.HBM))
    arrived = swap_all(outbound, "grp")

    weights = [w_gate[0], w_up[0], w_down[0]]
    weights = [pltpu.with_memory_space_constraint(w, pltpu.HBM) for w in weights]
    gate, up = pl.pallas_call(
        load_kernel,
        out_shape=[pltpu.VMEM(w.shape, BF16) for w in weights[:2]],
        in_specs=[ANY] * 3,
        out_specs=[VMEM] * 2,
        scratch_shapes=[pltpu.SemaphoreType.DMA((8,))],
        compiler_params=params(0),
        name="load",
    )(outbound[0], *weights[:2])

    compacted, low, high, pick = pl.pallas_call(
        functools.partial(compact_kernel, groups, slots),
        out_shape=[
            jax.ShapeDtypeStruct((slots, features), BF16),
            jax.ShapeDtypeStruct((slots, features // 2), BF16),
            jax.ShapeDtypeStruct((slots, features // 2), BF16),
            jax.ShapeDtypeStruct((groups * CAP, LANES), BF16),
        ],
        in_specs=[ANY] + [VMEM] * groups,
        out_specs=[VMEM] * 4,
        compiler_params=params(2 * (groups * CAP + 2 * slots) * wide),
        name="compact",
    )(gate, *arrived)
    if columns == 4:
        low, high = swap(low, "ing", 2), swap(high, "ing", 2)
        near = swap(compacted, "ing", 1)
        outward = [(1, 0), (2, 3)]
        far_low = lax.ppermute(low, "ing", outward)
        middle = lax.ppermute(compacted, "ing", [(1, 2), (2, 1)])
        far_high = lax.ppermute(high, "ing", outward)
        blocks = [low, high, near, compacted, middle, far_low, far_high]
    else:
        blocks = [swap(compacted, "ing", e) for e in range(columns)]

    hidden = pl.pallas_call(
        functools.partial(hidden_kernel, columns, columns == 4),
        out_shape=jax.ShapeDtypeStruct((columns * slots, units), BF16),
        in_specs=[VMEM] * (len(blocks) + 2),
        out_specs=VMEM,
        scratch_shapes=[pltpu.VMEM((columns * slots, features), BF16)],
        compiler_params=params(2 * columns * slots * (2 * features + units)),
        name="hidden",
    )(*blocks, gate, up)
    down, mixing = pl.pallas_call(
        functools.partial(prepare_kernel, groups),
        out_shape=[
            pltpu.VMEM(w_down.shape[1:], BF16),
            jax.ShapeDtypeStruct((count, groups * CAP), BF16),
        ],
        in_specs=[ANY] * 4,
        out_specs=[VMEM] * 2,
        scratch_shapes=[
            pltpu.VMEM(ids.shape, jnp.int32),
            pltpu.VMEM(logits.shape, F32),
            pltpu.SemaphoreType.DMA((6,)),
        ],
        compiler_params=params(0),
        name="prepare",
    )(hidden, ids, logits, weights[2])
    hiddens = [swap(hidden, "ing", f) for f in range(columns)]

    results = pl.pallas_call(
        functools.partial(down_kernel, columns),
        out_shape=[jax.ShapeDtypeStruct((slots, share), BF16)] * columns,
        in_specs=[VMEM] * (columns + 1),
        out_specs=[VMEM] * columns,
        compiler_params=params(2 * columns * slots * (columns * units + 4 * share)),
        name="down",
    )(*hiddens, down)
    results = swap_all(results, "ing")

    backs = pl.pallas_call(
        functools.partial(spread_kernel, groups, columns),
        out_shape=[jax.ShapeDtypeStruct((columns, CAP, share), BF16)] * groups,
        in_specs=[VMEM] * (columns + 1),
        out_specs=[VMEM] * groups,
        compiler_params=params(2 * (groups * CAP + slots) * features),
        name="spread",
    )(pick, *results)
    backs = swap_all(backs, "grp")

    if share % LANES:
        me = lax.axis_index("ing")
        rows = jnp.stack(backs[::-1])[:, jnp.arange(columns) ^ me]
        rows = rows.transpose(0, 2, 1, 3).reshape(groups * CAP, features)
        return jnp.dot(mixing, rows, preferred_element_type=F32).astype(BF16)
    return pl.pallas_call(
        functools.partial(combine_kernel, groups, columns),
        out_shape=jax.ShapeDtypeStruct((count, features), BF16),
        in_specs=[VMEM] * (1 + groups),
        out_specs=ANY,
        scratch_shapes=[pltpu.VMEM((count, features), BF16), pltpu.SemaphoreType.DMA((columns,))],
        compiler_params=params(2 * (count + groups * CAP) * features),
        name="combine",
    )(mixing, *backs)


def solution(mesh):
    placed = (
        P(("rep", "grp", "ing"), None),
        P(("rep", "grp", "ing"), None),
        P(("rep", "grp", "ing"), None),
        P("grp", None, "ing"),
        P("grp", None, "ing"),
        P("grp", None, "ing"),
    )
    return jax.shard_map(
        local, mesh=mesh, in_specs=placed, out_specs=P(("rep", "grp", "ing"), None), check_vma=False
    )
```

```python
import functools

import jax
import jax.numpy as jnp
from jax import lax
from jax.experimental import pallas as pl
from jax.experimental.pallas import tpu as pltpu
from jax.sharding import PartitionSpec as P

GROUP_EXPERTS = 24
CAP = 8
LANES = 128
ROUTE_SCALE = 2.827
MIB = 1024 * 1024

BF16 = jnp.bfloat16
F32 = jnp.float32
VMEM = pl.BlockSpec(memory_space=pltpu.VMEM)
ANY = pl.BlockSpec(memory_space=pl.ANY)


def params(nbytes):
    return pltpu.CompilerParams(vmem_limit_bytes=2 * nbytes + 4 * MIB)


def named(ids, expert):
    hit = jnp.zeros(expert.shape, F32)
    for k in range(ids.shape[0]):
        hit = jnp.where(ids[k : k + 1, :] == expert, 1.0, hit)
    return hit


def upto(count):
    return (
        lax.broadcasted_iota(jnp.int32, (count, count), 0)
        <= lax.broadcasted_iota(jnp.int32, (count, count), 1)
    ).astype(BF16)


def placing(ids, groups, me, before):
    rows, count = groups * CAP, ids.shape[1]
    row = lax.broadcasted_iota(jnp.int32, (rows, count), 0)
    group = (row // CAP) ^ me
    hit = named(ids, group * GROUP_EXPERTS)
    rank = jnp.dot(hit.astype(BF16), before, preferred_element_type=F32)
    slot = lax.rem(row, CAP).astype(F32)
    return jnp.where((hit > 0.5) & (rank == slot + 1.0), 1.0, 0.0), group


def dispatch_kernel(groups, width, ids_ref, tokens_ref, *refs):
    outs, (ids_held, staged, before_ref, sems) = refs[:groups], refs[groups:]
    me = lax.axis_index("grp")
    features = tokens_ref.shape[1]
    first = pltpu.make_async_copy(ids_ref, ids_held, sems.at[features // width])
    first.start()
    copies = []
    for c in range(features // width):
        part = pl.ds(c * width, width)
        copies.append(pltpu.make_async_copy(tokens_ref.at[:, part], staged.at[:, part], sems.at[c]))
        copies[-1].start()
    before_ref[...] = upto(tokens_ref.shape[0])
    first.wait()
    place, _ = placing(ids_held[...], groups, me, before_ref[...])
    live = jnp.sum(place, axis=1, keepdims=True)
    place = place.astype(BF16)
    for d in range(groups):
        outs[d][:, features:] = jnp.broadcast_to(live[d * CAP : (d + 1) * CAP], (CAP, LANES)).astype(BF16)
    for c in range(features // width):
        copies[c].wait()
        part = slice(c * width, (c + 1) * width)
        rows = jnp.dot(place, staged[:, part], preferred_element_type=F32)
        for d in range(groups):
            outs[d][:, part] = rows[d * CAP : (d + 1) * CAP].astype(BF16)


def prepare_kernel(groups, after_ref, ids_ref, logits_ref, *refs):
    del after_ref
    weights, loaded, (out_ref, ids_held, logits_held, sems) = refs[:3], refs[3:6], refs[6:]
    small = [
        pltpu.make_async_copy(ids_ref, ids_held, sems.at[12]),
        pltpu.make_async_copy(logits_ref, logits_held, sems.at[13]),
    ]
    for copy in small:
        copy.start()
    copies = []
    for k in range(3):
        depth = weights[k].shape[0]
        for c in range(4):
            part = pl.ds(c * (depth // 4), depth // 4)
            copies.append(pltpu.make_async_copy(weights[k].at[part], loaded[k].at[part], sems.at[4 * k + c]))
            copies[-1].start()
    for copy in small:
        copy.wait()
    me = lax.axis_index("grp")
    ids = ids_held[...]
    place, group = placing(ids, groups, me, upto(ids.shape[1]))
    scores = 1.0 / (1.0 + jnp.exp(-logits_held[...]))
    expert = lax.broadcasted_iota(jnp.int32, scores.shape, 0)
    chosen = jnp.sum(jnp.where(named(ids, expert) > 0.5, scores, 0.0), axis=0, keepdims=True)
    leading = jnp.zeros(place.shape, F32)
    for g in range(groups):
        leading = jnp.where(group == g, scores[g * GROUP_EXPERTS : g * GROUP_EXPERTS + 1, :], leading)
    weight = (ROUTE_SCALE * leading / chosen).astype(BF16).astype(F32)
    out_ref[...] = jnp.where(place > 0.5, weight, 0.0).T.astype(BF16)
    for copy in copies:
        copy.wait()


def compact_kernel(groups, slots, *refs):
    arrived, (out_ref, pick_ref) = refs[:groups][::-1], refs[groups:]
    rows, features = groups * CAP, out_ref.shape[1]
    live = jnp.concatenate([a[:, features:].astype(F32) for a in arrived], axis=0)
    row = lax.broadcasted_iota(jnp.int32, (rows, rows), 0)
    column = lax.broadcasted_iota(jnp.int32, (rows, rows), 1)
    rank = jnp.dot((column <= row).astype(BF16), live.astype(BF16), preferred_element_type=F32)
    lane = lax.broadcasted_iota(jnp.int32, (rows, LANES), 1).astype(F32)
    pick = jnp.where((live > 0.5) & (rank == lane + 1.0), 1.0, 0.0).astype(BF16)
    pick_ref[...] = pick
    step = 512
    for c in range(features // step):
        part = slice(c * step, (c + 1) * step)
        whole = jnp.concatenate([a[:, part].astype(F32) for a in arrived], axis=0).astype(BF16)
        out_ref[:, part] = lax.dot_general(
            pick[:, :slots], whole, (((0,), (0,)), ((), ())), preferred_element_type=F32
        ).astype(BF16)


def hidden_kernel(columns, *refs):
    blocks, (gate_ref, up_ref, hidden_ref) = refs[:columns], refs[columns:]
    units = gate_ref.shape[1]
    rows = jnp.concatenate([block[...] for block in blocks], axis=0)
    step = min(256, units)
    for c in range(units // step):
        part = slice(c * step, (c + 1) * step)
        gate = jnp.dot(rows, gate_ref[:, part], preferred_element_type=F32)
        up = jnp.dot(rows, up_ref[:, part], preferred_element_type=F32)
        hidden_ref[:, part] = (gate / (1.0 + jnp.exp(-gate)) * up).astype(BF16)


def down_kernel(columns, *refs):
    hiddens, down_ref, outs = refs[:columns], refs[columns], refs[columns + 1 :]
    me = lax.axis_index("ing")
    rows, units = hiddens[0].shape
    slots = rows // columns
    total = jnp.zeros((rows, down_ref.shape[1]), F32)
    for f in range(columns):
        block = jnp.concatenate(
            [hiddens[f][slots * (e ^ f) : slots * ((e ^ f) + 1), :] for e in range(columns)], axis=0
        )
        at = pl.multiple_of((me ^ f) * units, units)
        total += jnp.dot(block, down_ref[pl.ds(at, units), :], preferred_element_type=F32)
    for e in range(columns):
        outs[e][...] = total[e * slots : (e + 1) * slots].astype(BF16)


def spread_kernel(groups, columns, pick_ref, *refs):
    blocks, outs = refs[:columns][::-1], refs[columns:]
    for e in range(columns):
        block = blocks[e][...]
        back = jnp.dot(pick_ref[:, : block.shape[0]], block, preferred_element_type=F32)
        for d in range(groups):
            outs[d][e] = back[d * CAP : (d + 1) * CAP].astype(BF16)


def combine_kernel(groups, columns, mixing_ref, *refs):
    backs, (out_ref, held, sems) = refs[:groups][::-1], refs[groups:]
    me = lax.axis_index("ing")
    width, half = backs[0].shape[2], held.shape[0] // 2
    copies = []
    for e in range(columns):
        rows = jnp.concatenate([backs[d][e].astype(F32) for d in range(groups)], axis=0)
        rows = rows.astype(BF16)
        part = pl.ds(e * width, width)
        there = pl.ds(pl.multiple_of((me ^ e) * width, width), width)
        for h in range(2):
            mine = pl.ds(h * half, half)
            value = jnp.dot(mixing_ref[mine, :], rows, preferred_element_type=F32)
            held[mine, part] = value.astype(BF16)
            copies.append(
                pltpu.make_async_copy(held.at[mine, part], out_ref.at[mine, there], sems.at[2 * e + h])
            )
            copies[-1].start()
    for copy in copies:
        copy.wait()


def swap(x, name, step):
    if step == 0:
        return x
    return lax.ppermute(x, name, [(a, a ^ step) for a in range(lax.axis_size(name))])


def swap_all(parts, name):
    return [swap(part, name, k) for k, part in enumerate(parts)][::-1]


def local(tokens, router_logits, expert_ids, w_gate, w_up, w_down):
    groups = lax.axis_size("grp")
    columns = lax.axis_size("ing")
    count, features = tokens.shape
    units, share = w_gate.shape[2], w_down.shape[2]
    slots = groups * CAP // 2
    wide = features + LANES
    ids = pltpu.with_memory_space_constraint(expert_ids.T, pltpu.HBM)
    logits = pltpu.with_memory_space_constraint(router_logits.T, pltpu.HBM)

    outbound = pl.pallas_call(
        functools.partial(dispatch_kernel, groups, features // 2),
        out_shape=[jax.ShapeDtypeStruct((CAP, wide), BF16)] * groups,
        in_specs=[ANY, ANY],
        out_specs=[VMEM] * groups,
        scratch_shapes=[
            pltpu.VMEM(ids.shape, jnp.int32),
            pltpu.VMEM((count, features), BF16),
            pltpu.VMEM((count, count), BF16),
            pltpu.SemaphoreType.DMA((3,)),
        ],
        compiler_params=params(2 * count * features),
        name="dispatch",
    )(ids, pltpu.with_memory_space_constraint(tokens, pltpu.HBM))
    arrived = swap_all(outbound, "grp")

    compacted, pick = pl.pallas_call(
        functools.partial(compact_kernel, groups, slots),
        out_shape=[
            jax.ShapeDtypeStruct((slots, features), BF16),
            jax.ShapeDtypeStruct((groups * CAP, LANES), BF16),
        ],
        in_specs=[VMEM] * groups,
        out_specs=[VMEM, VMEM],
        compiler_params=params(2 * (groups * CAP + slots) * wide),
        name="compact",
    )(*arrived)
    blocks = [swap(compacted, "ing", e) for e in range(columns)]

    weights = [w_gate[0], w_up[0], w_down[0]]
    gate, up, down, mixing = pl.pallas_call(
        functools.partial(prepare_kernel, groups),
        out_shape=[pltpu.VMEM(w.shape, BF16) for w in weights]
        + [jax.ShapeDtypeStruct((count, groups * CAP), BF16)],
        in_specs=[ANY] * 6,
        out_specs=[VMEM] * 4,
        scratch_shapes=[
            pltpu.VMEM(ids.shape, jnp.int32),
            pltpu.VMEM(logits.shape, F32),
            pltpu.SemaphoreType.DMA((14,)),
        ],
        compiler_params=params(0),
        name="prepare",
    )(
        pick,
        ids,
        logits,
        *[pltpu.with_memory_space_constraint(w, pltpu.HBM) for w in weights],
    )

    hidden = pl.pallas_call(
        functools.partial(hidden_kernel, columns),
        out_shape=jax.ShapeDtypeStruct((columns * slots, units), BF16),
        in_specs=[VMEM] * (columns + 2),
        out_specs=VMEM,
        compiler_params=params(2 * columns * slots * (2 * features + units)),
        name="hidden",
    )(*blocks, gate, up)
    hiddens = [swap(hidden, "ing", f) for f in range(columns)]

    results = pl.pallas_call(
        functools.partial(down_kernel, columns),
        out_shape=[jax.ShapeDtypeStruct((slots, share), BF16)] * columns,
        in_specs=[VMEM] * (columns + 1),
        out_specs=[VMEM] * columns,
        compiler_params=params(2 * columns * slots * (columns * units + 4 * share)),
        name="down",
    )(*hiddens, down)
    results = swap_all(results, "ing")

    backs = pl.pallas_call(
        functools.partial(spread_kernel, groups, columns),
        out_shape=[jax.ShapeDtypeStruct((columns, CAP, share), BF16)] * groups,
        in_specs=[VMEM] * (columns + 1),
        out_specs=[VMEM] * groups,
        compiler_params=params(2 * (groups * CAP + slots) * features),
        name="spread",
    )(pick, *results)
    backs = swap_all(backs, "grp")

    if share % LANES:
        me = lax.axis_index("ing")
        rows = jnp.stack(backs[::-1])[:, jnp.arange(columns) ^ me]
        rows = rows.transpose(0, 2, 1, 3).reshape(groups * CAP, features)
        return jnp.dot(mixing, rows, preferred_element_type=F32).astype(BF16)
    return pl.pallas_call(
        functools.partial(combine_kernel, groups, columns),
        out_shape=jax.ShapeDtypeStruct((count, features), BF16),
        in_specs=[VMEM] * (1 + groups),
        out_specs=ANY,
        scratch_shapes=[pltpu.VMEM((count, features), BF16), pltpu.SemaphoreType.DMA((2 * columns,))],
        compiler_params=params(2 * (count + groups * CAP) * features),
        name="combine",
    )(mixing, *backs)


def solution(mesh):
    placed = (
        P(("rep", "grp", "ing"), None),
        P(("rep", "grp", "ing"), None),
        P(("rep", "grp", "ing"), None),
        P("grp", None, "ing"),
        P("grp", None, "ing"),
        P("grp", None, "ing"),
    )
    return jax.shard_map(
        local, mesh=mesh, in_specs=placed, out_specs=P(("rep", "grp", "ing"), None), check_vma=False
    )
```

```python
import functools

import jax
import jax.numpy as jnp
from jax import lax
from jax.experimental import pallas as pl
from jax.experimental.pallas import tpu as pltpu
from jax.sharding import PartitionSpec as P

GROUP_EXPERTS = 24
CAP = 8
LANES = 128
ROUTE_SCALE = 2.827
MIB = 1024 * 1024

BF16 = jnp.bfloat16
F32 = jnp.float32
VMEM = pl.BlockSpec(memory_space=pltpu.VMEM)
ANY = pl.BlockSpec(memory_space=pl.ANY)


def params(nbytes):
    return pltpu.CompilerParams(vmem_limit_bytes=2 * nbytes + 4 * MIB)


def named(ids, expert):
    hit = jnp.zeros(expert.shape, F32)
    for k in range(ids.shape[0]):
        hit = jnp.where(ids[k : k + 1, :] == expert, 1.0, hit)
    return hit


def upto(count):
    return (
        lax.broadcasted_iota(jnp.int32, (count, count), 0)
        <= lax.broadcasted_iota(jnp.int32, (count, count), 1)
    ).astype(BF16)


def placing(ids, groups, me, before):
    rows, count = groups * CAP, ids.shape[1]
    row = lax.broadcasted_iota(jnp.int32, (rows, count), 0)
    group = (row // CAP) ^ me
    hit = named(ids, group * GROUP_EXPERTS)
    rank = jnp.dot(hit.astype(BF16), before, preferred_element_type=F32)
    slot = lax.rem(row, CAP).astype(F32)
    return jnp.where((hit > 0.5) & (rank == slot + 1.0), 1.0, 0.0), group


def dispatch_kernel(groups, width, ids_ref, tokens_ref, *refs):
    outs, (ids_held, staged, before_ref, sems) = refs[:groups], refs[groups:]
    me = lax.axis_index("grp")
    features = tokens_ref.shape[1]
    first = pltpu.make_async_copy(ids_ref, ids_held, sems.at[features // width])
    first.start()
    copies = []
    for c in range(features // width):
        part = pl.ds(c * width, width)
        copies.append(pltpu.make_async_copy(tokens_ref.at[:, part], staged.at[:, part], sems.at[c]))
        copies[-1].start()
    before_ref[...] = upto(tokens_ref.shape[0])
    first.wait()
    place, _ = placing(ids_held[...], groups, me, before_ref[...])
    live = jnp.sum(place, axis=1, keepdims=True)
    place = place.astype(BF16)
    for d in range(groups):
        outs[d][:, features:] = jnp.broadcast_to(live[d * CAP : (d + 1) * CAP], (CAP, LANES)).astype(BF16)
    for c in range(features // width):
        copies[c].wait()
        part = slice(c * width, (c + 1) * width)
        rows = jnp.dot(place, staged[:, part], preferred_element_type=F32)
        for d in range(groups):
            outs[d][:, part] = rows[d * CAP : (d + 1) * CAP].astype(BF16)


def prepare_kernel(groups, after_ref, ids_ref, logits_ref, *refs):
    del after_ref
    weights, loaded, (out_ref, ids_held, logits_held, sems) = refs[:3], refs[3:6], refs[6:]
    small = [
        pltpu.make_async_copy(ids_ref, ids_held, sems.at[12]),
        pltpu.make_async_copy(logits_ref, logits_held, sems.at[13]),
    ]
    for copy in small:
        copy.start()
    copies = []
    for k in range(3):
        depth = weights[k].shape[0]
        for c in range(4):
            part = pl.ds(c * (depth // 4), depth // 4)
            copies.append(pltpu.make_async_copy(weights[k].at[part], loaded[k].at[part], sems.at[4 * k + c]))
            copies[-1].start()
    for copy in small:
        copy.wait()
    me = lax.axis_index("grp")
    ids = ids_held[...]
    place, group = placing(ids, groups, me, upto(ids.shape[1]))
    scores = 1.0 / (1.0 + jnp.exp(-logits_held[...]))
    expert = lax.broadcasted_iota(jnp.int32, scores.shape, 0)
    chosen = jnp.sum(jnp.where(named(ids, expert) > 0.5, scores, 0.0), axis=0, keepdims=True)
    leading = jnp.zeros(place.shape, F32)
    for g in range(groups):
        leading = jnp.where(group == g, scores[g * GROUP_EXPERTS : g * GROUP_EXPERTS + 1, :], leading)
    weight = (ROUTE_SCALE * leading / chosen).astype(BF16).astype(F32)
    out_ref[...] = jnp.where(place > 0.5, weight, 0.0).T.astype(BF16)
    for copy in copies:
        copy.wait()


def compact_kernel(groups, slots, *refs):
    arrived, (out_ref, pick_ref) = refs[:groups][::-1], refs[groups:]
    rows, features = groups * CAP, out_ref.shape[1]
    live = jnp.concatenate([a[:, features:].astype(F32) for a in arrived], axis=0)
    row = lax.broadcasted_iota(jnp.int32, (rows, rows), 0)
    column = lax.broadcasted_iota(jnp.int32, (rows, rows), 1)
    rank = jnp.dot((column <= row).astype(BF16), live.astype(BF16), preferred_element_type=F32)
    lane = lax.broadcasted_iota(jnp.int32, (rows, LANES), 1).astype(F32)
    pick = jnp.where((live > 0.5) & (rank == lane + 1.0), 1.0, 0.0).astype(BF16)
    pick_ref[...] = pick
    step = 512
    for c in range(features // step):
        part = slice(c * step, (c + 1) * step)
        whole = jnp.concatenate([a[:, part].astype(F32) for a in arrived], axis=0).astype(BF16)
        out_ref[:, part] = lax.dot_general(
            pick[:, :slots], whole, (((0,), (0,)), ((), ())), preferred_element_type=F32
        ).astype(BF16)


def hidden_kernel(columns, *refs):
    blocks, (gate_ref, up_ref, hidden_ref) = refs[:columns], refs[columns:]
    units = gate_ref.shape[1]
    rows = jnp.concatenate([block[...] for block in blocks], axis=0)
    step = min(256, units)
    for c in range(units // step):
        part = slice(c * step, (c + 1) * step)
        gate = jnp.dot(rows, gate_ref[:, part], preferred_element_type=F32)
        up = jnp.dot(rows, up_ref[:, part], preferred_element_type=F32)
        hidden_ref[:, part] = (gate / (1.0 + jnp.exp(-gate)) * up).astype(BF16)


def down_kernel(columns, shifts, *refs):
    hiddens, down_ref, outs, total_ref = refs[:columns], refs[columns], refs[columns + 1 : -1], refs[-1]
    me = lax.axis_index("ing")
    rows, units = hiddens[0].shape
    slots = rows // columns
    total = jnp.zeros((rows, down_ref.shape[1]), F32)
    for f in range(columns):
        block = jnp.concatenate(
            [hiddens[f][slots * (e ^ f) : slots * ((e ^ f) + 1), :] for e in range(columns)], axis=0
        )
        at = pl.multiple_of((me ^ f) * units, units)
        total += jnp.dot(block, down_ref[pl.ds(at, units), :], preferred_element_type=F32)
    total_ref[...] = total
    for shift, out in zip(shifts, outs):
        other = jnp.clip(me + shift, 0, columns - 1)
        out[...] = total_ref[pl.ds(pl.multiple_of((other ^ me) * slots, slots), slots), :].astype(BF16)


def spread_kernel(groups, columns, shifts, pick_ref, *refs):
    blocks, outs = refs[: len(shifts)], refs[len(shifts) :]
    me = lax.axis_index("ing")
    for (first, last, shift), block in zip(shifts, blocks):

        @pl.when((me >= first) & (me <= last))
        def _():
            back = jnp.dot(pick_ref[:, : block.shape[0]], block[...], preferred_element_type=F32)
            for d in range(groups):
                outs[d][me - shift] = back[d * CAP : (d + 1) * CAP].astype(BF16)


def combine_kernel(groups, columns, mixing_ref, *refs):
    backs, (out_ref, held, sems) = refs[:groups][::-1], refs[groups:]
    width, half = backs[0].shape[2], held.shape[0] // 2
    copies = []
    for e in range(columns):
        rows = jnp.concatenate([backs[d][e].astype(F32) for d in range(groups)], axis=0)
        rows = rows.astype(BF16)
        part = pl.ds(e * width, width)
        for h in range(2):
            mine = pl.ds(h * half, half)
            value = jnp.dot(mixing_ref[mine, :], rows, preferred_element_type=F32)
            held[mine, part] = value.astype(BF16)
            copies.append(
                pltpu.make_async_copy(held.at[mine, part], out_ref.at[mine, part], sems.at[2 * e + h])
            )
            copies[-1].start()
    for copy in copies:
        copy.wait()


def swap(x, name, step):
    if step == 0:
        return x
    return lax.ppermute(x, name, [(a, a ^ step) for a in range(lax.axis_size(name))])


def swap_all(parts, name):
    return [swap(part, name, k) for k, part in enumerate(parts)][::-1]


def local(tokens, router_logits, expert_ids, w_gate, w_up, w_down):
    groups = lax.axis_size("grp")
    columns = lax.axis_size("ing")
    count, features = tokens.shape
    units, share = w_gate.shape[2], w_down.shape[2]
    slots = groups * CAP // 2
    wide = features + LANES
    ids = pltpu.with_memory_space_constraint(expert_ids.T, pltpu.HBM)
    logits = pltpu.with_memory_space_constraint(router_logits.T, pltpu.HBM)

    outbound = pl.pallas_call(
        functools.partial(dispatch_kernel, groups, features // 2),
        out_shape=[jax.ShapeDtypeStruct((CAP, wide), BF16)] * groups,
        in_specs=[ANY, ANY],
        out_specs=[VMEM] * groups,
        scratch_shapes=[
            pltpu.VMEM(ids.shape, jnp.int32),
            pltpu.VMEM((count, features), BF16),
            pltpu.VMEM((count, count), BF16),
            pltpu.SemaphoreType.DMA((3,)),
        ],
        compiler_params=params(2 * count * features),
        name="dispatch",
    )(ids, pltpu.with_memory_space_constraint(tokens, pltpu.HBM))
    arrived = swap_all(outbound, "grp")

    compacted, pick = pl.pallas_call(
        functools.partial(compact_kernel, groups, slots),
        out_shape=[
            jax.ShapeDtypeStruct((slots, features), BF16),
            jax.ShapeDtypeStruct((groups * CAP, LANES), BF16),
        ],
        in_specs=[VMEM] * groups,
        out_specs=[VMEM, VMEM],
        compiler_params=params(2 * (groups * CAP + slots) * wide),
        name="compact",
    )(*arrived)
    blocks = [swap(compacted, "ing", e) for e in range(columns)]

    weights = [w_gate[0], w_up[0], w_down[0]]
    gate, up, down, mixing = pl.pallas_call(
        functools.partial(prepare_kernel, groups),
        out_shape=[pltpu.VMEM(w.shape, BF16) for w in weights]
        + [jax.ShapeDtypeStruct((count, groups * CAP), BF16)],
        in_specs=[ANY] * 6,
        out_specs=[VMEM] * 4,
        scratch_shapes=[
            pltpu.VMEM(ids.shape, jnp.int32),
            pltpu.VMEM(logits.shape, F32),
            pltpu.SemaphoreType.DMA((14,)),
        ],
        compiler_params=params(0),
        name="prepare",
    )(
        pick,
        ids,
        logits,
        *[pltpu.with_memory_space_constraint(w, pltpu.HBM) for w in weights],
    )

    hidden = pl.pallas_call(
        functools.partial(hidden_kernel, columns),
        out_shape=jax.ShapeDtypeStruct((columns * slots, units), BF16),
        in_specs=[VMEM] * (columns + 2),
        out_specs=VMEM,
        compiler_params=params(2 * columns * slots * (2 * features + units)),
        name="hidden",
    )(*blocks, gate, up)
    hiddens = [swap(hidden, "ing", f) for f in range(columns)]

    moves = [(0, columns - 1 + s, s) for s in range(1 - columns, 0)]
    moves += [(1, 1, 1)] + [(s, columns - 1, s) for s in range(2, columns)]
    moves += [(2, columns - 1, 1), (0, columns - 1, 0)]
    shifts = [s for _, _, s in moves]
    results = pl.pallas_call(
        functools.partial(down_kernel, columns, shifts),
        out_shape=[jax.ShapeDtypeStruct((slots, share), BF16)] * len(shifts),
        in_specs=[VMEM] * (columns + 1),
        out_specs=[VMEM] * len(shifts),
        scratch_shapes=[pltpu.VMEM((columns * slots, share), F32)],
        compiler_params=params(2 * columns * slots * (columns * units + 6 * share)),
        name="down",
    )(*hiddens, down)
    returned = [
        lax.ppermute(block, "ing", [(t - s, t) for t in range(first, last + 1)]) if s else block
        for (first, last, s), block in zip(moves, results)
    ]
    backs = pl.pallas_call(
        functools.partial(spread_kernel, groups, columns, moves),
        out_shape=[jax.ShapeDtypeStruct((columns, CAP, share), BF16)] * groups,
        in_specs=[VMEM] * (1 + len(moves)),
        out_specs=[VMEM] * groups,
        compiler_params=params(2 * (groups * CAP + 2 * slots) * features),
        name="spread",
    )(pick, *returned)
    backs = swap_all(backs, "grp")

    if share % LANES:
        rows = jnp.stack(backs[::-1])
        rows = rows.transpose(0, 2, 1, 3).reshape(groups * CAP, features)
        return jnp.dot(mixing, rows, preferred_element_type=F32).astype(BF16)
    return pl.pallas_call(
        functools.partial(combine_kernel, groups, columns),
        out_shape=jax.ShapeDtypeStruct((count, features), BF16),
        in_specs=[VMEM] * (1 + groups),
        out_specs=ANY,
        scratch_shapes=[pltpu.VMEM((count, features), BF16), pltpu.SemaphoreType.DMA((2 * columns,))],
        compiler_params=params(2 * (count + groups * CAP) * features),
        name="combine",
    )(mixing, *backs)


def solution(mesh):
    placed = (
        P(("rep", "grp", "ing"), None),
        P(("rep", "grp", "ing"), None),
        P(("rep", "grp", "ing"), None),
        P("grp", None, "ing"),
        P("grp", None, "ing"),
        P("grp", None, "ing"),
    )
    return jax.shard_map(
        local, mesh=mesh, in_specs=placed, out_specs=P(("rep", "grp", "ing"), None), check_vma=False
    )
```

```python
import functools

import jax
import jax.numpy as jnp
from jax import lax
from jax.experimental import pallas as pl
from jax.experimental.pallas import tpu as pltpu
from jax.sharding import PartitionSpec as P

GROUP_EXPERTS = 24
CAP = 8
LANES = 128
ROUTE_SCALE = 2.827
MIB = 1024 * 1024

BF16 = jnp.bfloat16
F32 = jnp.float32
VMEM = pl.BlockSpec(memory_space=pltpu.VMEM)
ANY = pl.BlockSpec(memory_space=pl.ANY)


def params(nbytes):
    return pltpu.CompilerParams(vmem_limit_bytes=2 * nbytes + 4 * MIB)


def named(ids, expert):
    hit = jnp.zeros(expert.shape, F32)
    for k in range(ids.shape[0]):
        hit = jnp.where(ids[k : k + 1, :] == expert, 1.0, hit)
    return hit


def upto(count):
    return (
        lax.broadcasted_iota(jnp.int32, (count, count), 0)
        <= lax.broadcasted_iota(jnp.int32, (count, count), 1)
    ).astype(BF16)


def placing(ids, groups, me, before):
    rows, count = groups * CAP, ids.shape[1]
    row = lax.broadcasted_iota(jnp.int32, (rows, count), 0)
    group = (row // CAP) ^ me
    hit = named(ids, group * GROUP_EXPERTS)
    rank = jnp.dot(hit.astype(BF16), before, preferred_element_type=F32)
    slot = lax.rem(row, CAP).astype(F32)
    return jnp.where((hit > 0.5) & (rank == slot + 1.0), 1.0, 0.0), group


def dispatch_kernel(groups, width, ids_ref, tokens_ref, *refs):
    outs, (ids_held, staged, before_ref, sems) = refs[:groups], refs[groups:]
    me = lax.axis_index("grp")
    features = tokens_ref.shape[1]
    first = pltpu.make_async_copy(ids_ref, ids_held, sems.at[features // width])
    first.start()
    copies = []
    for c in range(features // width):
        part = pl.ds(c * width, width)
        copies.append(pltpu.make_async_copy(tokens_ref.at[:, part], staged.at[:, part], sems.at[c]))
        copies[-1].start()
    before_ref[...] = upto(tokens_ref.shape[0])
    first.wait()
    place, _ = placing(ids_held[...], groups, me, before_ref[...])
    live = jnp.sum(place, axis=1, keepdims=True)
    place = place.astype(BF16)
    for d in range(groups):
        outs[d][:, features:] = jnp.broadcast_to(live[d * CAP : (d + 1) * CAP], (CAP, LANES)).astype(BF16)
    for c in range(features // width):
        copies[c].wait()
        part = slice(c * width, (c + 1) * width)
        rows = jnp.dot(place, staged[:, part], preferred_element_type=F32)
        for d in range(groups):
            outs[d][:, part] = rows[d * CAP : (d + 1) * CAP].astype(BF16)


def start_loads(weights, loaded, sems):
    copies = []
    for k in range(len(weights)):
        depth = weights[k].shape[0]
        for c in range(4):
            part = pl.ds(c * (depth // 4), depth // 4)
            copies.append(pltpu.make_async_copy(weights[k].at[part], loaded[k].at[part], sems.at[4 * k + c]))
            copies[-1].start()
    return copies


def load_kernel(after_ref, gate_ref, up_ref, gate_out, up_out, sems):
    del after_ref
    for copy in start_loads([gate_ref, up_ref], [gate_out, up_out], sems):
        copy.wait()


def prepare_kernel(groups, after_ref, ids_ref, logits_ref, down_ref, down_out, out_ref, ids_held, logits_held, sems):
    del after_ref
    small = [
        pltpu.make_async_copy(ids_ref, ids_held, sems.at[4]),
        pltpu.make_async_copy(logits_ref, logits_held, sems.at[5]),
    ]
    for copy in small:
        copy.start()
    copies = start_loads([down_ref], [down_out], sems)
    for copy in small:
        copy.wait()
    me = lax.axis_index("grp")
    ids = ids_held[...]
    place, group = placing(ids, groups, me, upto(ids.shape[1]))
    scores = 1.0 / (1.0 + jnp.exp(-logits_held[...]))
    expert = lax.broadcasted_iota(jnp.int32, scores.shape, 0)
    chosen = jnp.sum(jnp.where(named(ids, expert) > 0.5, scores, 0.0), axis=0, keepdims=True)
    leading = jnp.zeros(place.shape, F32)
    for g in range(groups):
        leading = jnp.where(group == g, scores[g * GROUP_EXPERTS : g * GROUP_EXPERTS + 1, :], leading)
    weight = (ROUTE_SCALE * leading / chosen).astype(BF16).astype(F32)
    out_ref[...] = jnp.where(place > 0.5, weight, 0.0).T.astype(BF16)
    for copy in copies:
        copy.wait()


def compact_kernel(groups, slots, after_ref, *refs):
    del after_ref
    arrived, (out_ref, low_ref, high_ref, pick_ref) = refs[:groups][::-1], refs[groups:]
    rows, features = groups * CAP, out_ref.shape[1]
    live = jnp.concatenate([a[:, features:].astype(F32) for a in arrived], axis=0)
    row = lax.broadcasted_iota(jnp.int32, (rows, rows), 0)
    column = lax.broadcasted_iota(jnp.int32, (rows, rows), 1)
    rank = jnp.dot((column <= row).astype(BF16), live.astype(BF16), preferred_element_type=F32)
    lane = lax.broadcasted_iota(jnp.int32, (rows, LANES), 1).astype(F32)
    pick = jnp.where((live > 0.5) & (rank == lane + 1.0), 1.0, 0.0).astype(BF16)
    pick_ref[...] = pick
    half = features // 2
    step = 256
    for c in range(features // step):
        part = slice(c * step, (c + 1) * step)
        whole = jnp.concatenate([a[:, part].astype(F32) for a in arrived], axis=0).astype(BF16)
        moved = lax.dot_general(
            pick[:, :slots], whole, (((0,), (0,)), ((), ())), preferred_element_type=F32
        ).astype(BF16)
        out_ref[:, part] = moved
        if (c + 1) * step <= half:
            low_ref[:, part] = moved
        else:
            high_ref[:, c * step - half : (c + 1) * step - half] = moved


def hidden_kernel(columns, halved, *refs):
    blocks, (gate_ref, up_ref, hidden_ref) = refs[:-3], refs[-3:]
    units = gate_ref.shape[1]
    blocks = [block[...] for block in blocks]
    if halved:
        low, high, near, own, far_low, far_high = blocks
        blocks = [own, near, jnp.concatenate([low, high], axis=1), jnp.concatenate([far_low, far_high], axis=1)]
    rows = jnp.concatenate(blocks, axis=0)
    step = min(256, units)
    for c in range(units // step):
        part = slice(c * step, (c + 1) * step)
        gate = jnp.dot(rows, gate_ref[:, part], preferred_element_type=F32)
        up = jnp.dot(rows, up_ref[:, part], preferred_element_type=F32)
        hidden_ref[:, part] = (gate / (1.0 + jnp.exp(-gate)) * up).astype(BF16)


def down_kernel(columns, *refs):
    hiddens, down_ref, outs = refs[:columns], refs[columns], refs[columns + 1 :]
    me = lax.axis_index("ing")
    rows, units = hiddens[0].shape
    slots = rows // columns
    total = jnp.zeros((rows, down_ref.shape[1]), F32)
    for f in range(columns):
        block = jnp.concatenate(
            [hiddens[f][slots * (e ^ f) : slots * ((e ^ f) + 1), :] for e in range(columns)], axis=0
        )
        at = pl.multiple_of((me ^ f) * units, units)
        total += jnp.dot(block, down_ref[pl.ds(at, units), :], preferred_element_type=F32)
    for e in range(columns):
        outs[e][...] = total[e * slots : (e + 1) * slots].astype(BF16)


def spread_kernel(groups, columns, pick_ref, *refs):
    blocks, outs = refs[:columns][::-1], refs[columns:]
    for e in range(columns):
        block = blocks[e][...]
        back = jnp.dot(pick_ref[:, : block.shape[0]], block, preferred_element_type=F32)
        for d in range(groups):
            outs[d][e] = back[d * CAP : (d + 1) * CAP].astype(BF16)


def combine_kernel(groups, columns, mixing_ref, *refs):
    backs, (out_ref, held, sems) = refs[:groups][::-1], refs[groups:]
    me = lax.axis_index("ing")
    width, half = backs[0].shape[2], held.shape[0] // 2
    copies = []
    for e in range(columns):
        rows = jnp.concatenate([backs[d][e].astype(F32) for d in range(groups)], axis=0)
        rows = rows.astype(BF16)
        part = pl.ds(e * width, width)
        there = pl.ds(pl.multiple_of((me ^ e) * width, width), width)
        for h in range(2):
            mine = pl.ds(h * half, half)
            value = jnp.dot(mixing_ref[mine, :], rows, preferred_element_type=F32)
            held[mine, part] = value.astype(BF16)
            copies.append(
                pltpu.make_async_copy(held.at[mine, part], out_ref.at[mine, there], sems.at[2 * e + h])
            )
            copies[-1].start()
    for copy in copies:
        copy.wait()


def swap(x, name, step):
    if step == 0:
        return x
    return lax.ppermute(x, name, [(a, a ^ step) for a in range(lax.axis_size(name))])


def swap_all(parts, name):
    return [swap(part, name, k) for k, part in enumerate(parts)][::-1]


def local(tokens, router_logits, expert_ids, w_gate, w_up, w_down):
    groups = lax.axis_size("grp")
    columns = lax.axis_size("ing")
    count, features = tokens.shape
    units, share = w_gate.shape[2], w_down.shape[2]
    slots = groups * CAP // 2
    wide = features + LANES
    ids = pltpu.with_memory_space_constraint(expert_ids.T, pltpu.HBM)
    logits = pltpu.with_memory_space_constraint(router_logits.T, pltpu.HBM)

    outbound = pl.pallas_call(
        functools.partial(dispatch_kernel, groups, features // 2),
        out_shape=[jax.ShapeDtypeStruct((CAP, wide), BF16)] * groups,
        in_specs=[ANY, ANY],
        out_specs=[VMEM] * groups,
        scratch_shapes=[
            pltpu.VMEM(ids.shape, jnp.int32),
            pltpu.VMEM((count, features), BF16),
            pltpu.VMEM((count, count), BF16),
            pltpu.SemaphoreType.DMA((3,)),
        ],
        compiler_params=params(2 * count * features),
        name="dispatch",
    )(ids, pltpu.with_memory_space_constraint(tokens, pltpu.HBM))
    arrived = swap_all(outbound, "grp")

    weights = [w_gate[0], w_up[0], w_down[0]]
    weights = [pltpu.with_memory_space_constraint(w, pltpu.HBM) for w in weights]
    gate, up = pl.pallas_call(
        load_kernel,
        out_shape=[pltpu.VMEM(w.shape, BF16) for w in weights[:2]],
        in_specs=[ANY] * 3,
        out_specs=[VMEM] * 2,
        scratch_shapes=[pltpu.SemaphoreType.DMA((8,))],
        compiler_params=params(0),
        name="load",
    )(outbound[0], *weights[:2])

    compacted, low, high, pick = pl.pallas_call(
        functools.partial(compact_kernel, groups, slots),
        out_shape=[
            jax.ShapeDtypeStruct((slots, features), BF16),
            jax.ShapeDtypeStruct((slots, features // 2), BF16),
            jax.ShapeDtypeStruct((slots, features // 2), BF16),
            jax.ShapeDtypeStruct((groups * CAP, LANES), BF16),
        ],
        in_specs=[ANY] + [VMEM] * groups,
        out_specs=[VMEM] * 4,
        compiler_params=params(2 * (groups * CAP + 2 * slots) * wide),
        name="compact",
    )(gate, *arrived)
    if columns == 4:
        low, high = swap(low, "ing", 2), swap(high, "ing", 2)
        near = swap(compacted, "ing", 1)
        blocks = [low, high, near, compacted, swap(low, "ing", 1), swap(high, "ing", 1)]
    else:
        blocks = [swap(compacted, "ing", e) for e in range(columns)]

    hidden = pl.pallas_call(
        functools.partial(hidden_kernel, columns, columns == 4),
        out_shape=jax.ShapeDtypeStruct((columns * slots, units), BF16),
        in_specs=[VMEM] * (len(blocks) + 2),
        out_specs=VMEM,
        compiler_params=params(2 * columns * slots * (2 * features + units)),
        name="hidden",
    )(*blocks, gate, up)
    down, mixing = pl.pallas_call(
        functools.partial(prepare_kernel, groups),
        out_shape=[
            pltpu.VMEM(w_down.shape[1:], BF16),
            jax.ShapeDtypeStruct((count, groups * CAP), BF16),
        ],
        in_specs=[ANY] * 4,
        out_specs=[VMEM] * 2,
        scratch_shapes=[
            pltpu.VMEM(ids.shape, jnp.int32),
            pltpu.VMEM(logits.shape, F32),
            pltpu.SemaphoreType.DMA((6,)),
        ],
        compiler_params=params(0),
        name="prepare",
    )(hidden, ids, logits, weights[2])
    hiddens = [swap(hidden, "ing", f) for f in range(columns)]

    results = pl.pallas_call(
        functools.partial(down_kernel, columns),
        out_shape=[jax.ShapeDtypeStruct((slots, share), BF16)] * columns,
        in_specs=[VMEM] * (columns + 1),
        out_specs=[VMEM] * columns,
        compiler_params=params(2 * columns * slots * (columns * units + 4 * share)),
        name="down",
    )(*hiddens, down)
    results = swap_all(results, "ing")

    backs = pl.pallas_call(
        functools.partial(spread_kernel, groups, columns),
        out_shape=[jax.ShapeDtypeStruct((columns, CAP, share), BF16)] * groups,
        in_specs=[VMEM] * (columns + 1),
        out_specs=[VMEM] * groups,
        compiler_params=params(2 * (groups * CAP + slots) * features),
        name="spread",
    )(pick, *results)
    backs = swap_all(backs, "grp")

    if share % LANES:
        me = lax.axis_index("ing")
        rows = jnp.stack(backs[::-1])[:, jnp.arange(columns) ^ me]
        rows = rows.transpose(0, 2, 1, 3).reshape(groups * CAP, features)
        return jnp.dot(mixing, rows, preferred_element_type=F32).astype(BF16)
    return pl.pallas_call(
        functools.partial(combine_kernel, groups, columns),
        out_shape=jax.ShapeDtypeStruct((count, features), BF16),
        in_specs=[VMEM] * (1 + groups),
        out_specs=ANY,
        scratch_shapes=[pltpu.VMEM((count, features), BF16), pltpu.SemaphoreType.DMA((2 * columns,))],
        compiler_params=params(2 * (count + groups * CAP) * features),
        name="combine",
    )(mixing, *backs)


def solution(mesh):
    placed = (
        P(("rep", "grp", "ing"), None),
        P(("rep", "grp", "ing"), None),
        P(("rep", "grp", "ing"), None),
        P("grp", None, "ing"),
        P("grp", None, "ing"),
        P("grp", None, "ing"),
    )
    return jax.shard_map(
        local, mesh=mesh, in_specs=placed, out_specs=P(("rep", "grp", "ing"), None), check_vma=False
    )
```

```python
import functools

import jax
import jax.numpy as jnp
from jax import lax
from jax.experimental import pallas as pl
from jax.experimental.pallas import tpu as pltpu
from jax.sharding import PartitionSpec as P

GROUP_EXPERTS = 24
CAP = 8
LANES = 128
ROUTE_SCALE = 2.827
MIB = 1024 * 1024

BF16 = jnp.bfloat16
F32 = jnp.float32
VMEM = pl.BlockSpec(memory_space=pltpu.VMEM)
ANY = pl.BlockSpec(memory_space=pl.ANY)


def params(nbytes):
    return pltpu.CompilerParams(vmem_limit_bytes=2 * nbytes + 4 * MIB)


def named(ids, expert):
    hit = jnp.zeros(expert.shape, F32)
    for k in range(ids.shape[0]):
        hit = jnp.where(ids[k : k + 1, :] == expert, 1.0, hit)
    return hit


def upto(count):
    return (
        lax.broadcasted_iota(jnp.int32, (count, count), 0)
        <= lax.broadcasted_iota(jnp.int32, (count, count), 1)
    ).astype(BF16)


def placing(ids, groups, me, before):
    rows, count = groups * CAP, ids.shape[1]
    row = lax.broadcasted_iota(jnp.int32, (rows, count), 0)
    group = (row // CAP) ^ me
    hit = named(ids, group * GROUP_EXPERTS)
    rank = jnp.dot(hit.astype(BF16), before, preferred_element_type=F32)
    slot = lax.rem(row, CAP).astype(F32)
    return jnp.where((hit > 0.5) & (rank == slot + 1.0), 1.0, 0.0), group


def dispatch_kernel(groups, width, ids_ref, tokens_ref, *refs):
    outs, (ids_held, staged, before_ref, sems) = refs[:groups], refs[groups:]
    me = lax.axis_index("grp")
    features = tokens_ref.shape[1]
    first = pltpu.make_async_copy(ids_ref, ids_held, sems.at[features // width])
    first.start()
    copies = []
    for c in range(features // width):
        part = pl.ds(c * width, width)
        copies.append(pltpu.make_async_copy(tokens_ref.at[:, part], staged.at[:, part], sems.at[c]))
        copies[-1].start()
    before_ref[...] = upto(tokens_ref.shape[0])
    first.wait()
    place, _ = placing(ids_held[...], groups, me, before_ref[...])
    live = jnp.sum(place, axis=1, keepdims=True)
    place = place.astype(BF16)
    for d in range(groups):
        outs[d][:, features:] = jnp.broadcast_to(live[d * CAP : (d + 1) * CAP], (CAP, LANES)).astype(BF16)
    for c in range(features // width):
        copies[c].wait()
        part = slice(c * width, (c + 1) * width)
        rows = jnp.dot(place, staged[:, part], preferred_element_type=F32)
        for d in range(groups):
            outs[d][:, part] = rows[d * CAP : (d + 1) * CAP].astype(BF16)


def start_loads(weights, loaded, sems):
    copies = []
    for k in range(len(weights)):
        depth = weights[k].shape[0]
        for c in range(4):
            part = pl.ds(c * (depth // 4), depth // 4)
            copies.append(pltpu.make_async_copy(weights[k].at[part], loaded[k].at[part], sems.at[4 * k + c]))
            copies[-1].start()
    return copies


def load_kernel(after_ref, gate_ref, up_ref, gate_out, up_out, sems):
    del after_ref
    for copy in start_loads([gate_ref, up_ref], [gate_out, up_out], sems):
        copy.wait()


def prepare_kernel(groups, after_ref, ids_ref, logits_ref, down_ref, down_out, out_ref, ids_held, logits_held, sems):
    del after_ref
    small = [
        pltpu.make_async_copy(ids_ref, ids_held, sems.at[4]),
        pltpu.make_async_copy(logits_ref, logits_held, sems.at[5]),
    ]
    for copy in small:
        copy.start()
    copies = start_loads([down_ref], [down_out], sems)
    for copy in small:
        copy.wait()
    me = lax.axis_index("grp")
    ids = ids_held[...]
    place, group = placing(ids, groups, me, upto(ids.shape[1]))
    scores = 1.0 / (1.0 + jnp.exp(-logits_held[...]))
    expert = lax.broadcasted_iota(jnp.int32, scores.shape, 0)
    chosen = jnp.sum(jnp.where(named(ids, expert) > 0.5, scores, 0.0), axis=0, keepdims=True)
    leading = jnp.zeros(place.shape, F32)
    for g in range(groups):
        leading = jnp.where(group == g, scores[g * GROUP_EXPERTS : g * GROUP_EXPERTS + 1, :], leading)
    weight = (ROUTE_SCALE * leading / chosen).astype(BF16).astype(F32)
    out_ref[...] = jnp.where(place > 0.5, weight, 0.0).T.astype(BF16)
    for copy in copies:
        copy.wait()


def compact_kernel(groups, slots, after_ref, *refs):
    del after_ref
    arrived, outs, pick_ref = refs[:groups][::-1], refs[groups:-1], refs[-1]
    rows, part = groups * CAP, outs[0].shape[1]
    features = part * len(outs)
    live = jnp.concatenate([a[:, features:].astype(F32) for a in arrived], axis=0)
    row = lax.broadcasted_iota(jnp.int32, (rows, rows), 0)
    column = lax.broadcasted_iota(jnp.int32, (rows, rows), 1)
    rank = jnp.dot((column <= row).astype(BF16), live.astype(BF16), preferred_element_type=F32)
    lane = lax.broadcasted_iota(jnp.int32, (rows, LANES), 1).astype(F32)
    pick = jnp.where((live > 0.5) & (rank == lane + 1.0), 1.0, 0.0).astype(BF16)
    pick_ref[...] = pick
    step = 256
    for c in range(features // step):
        at = slice(c * step, (c + 1) * step)
        whole = jnp.concatenate([a[:, at].astype(F32) for a in arrived], axis=0).astype(BF16)
        moved = lax.dot_general(pick[:, :slots], whole, (((0,), (0,)), ((), ())), preferred_element_type=F32)
        first = c * step % part
        outs[c * step // part][:, first : first + step] = moved.astype(BF16)


def hidden_kernel(columns, halved, *refs):
    blocks, (gate_ref, up_ref, hidden_ref) = refs[:-3], refs[-3:]
    units = gate_ref.shape[1]
    blocks = [block[...] for block in blocks]
    if halved:
        low, near_low, near_high, high, far_high, far_low, own_low, own_high = blocks
        pairs = [(own_low, own_high), (near_low, near_high), (low, high), (far_low, far_high)]
        blocks = [jnp.concatenate(pair, axis=1) for pair in pairs]
    rows = jnp.concatenate(blocks, axis=0)
    step = min(256, units)
    for c in range(units // step):
        part = slice(c * step, (c + 1) * step)
        gate = jnp.dot(rows, gate_ref[:, part], preferred_element_type=F32)
        up = jnp.dot(rows, up_ref[:, part], preferred_element_type=F32)
        hidden_ref[:, part] = (gate / (1.0 + jnp.exp(-gate)) * up).astype(BF16)


def down_kernel(columns, *refs):
    hiddens, down_ref, outs = refs[:columns], refs[columns], refs[columns + 1 :]
    me = lax.axis_index("ing")
    rows, units = hiddens[0].shape
    slots = rows // columns
    total = jnp.zeros((rows, down_ref.shape[1]), F32)
    for f in range(columns):
        block = jnp.concatenate(
            [hiddens[f][slots * (e ^ f) : slots * ((e ^ f) + 1), :] for e in range(columns)], axis=0
        )
        at = pl.multiple_of((me ^ f) * units, units)
        total += jnp.dot(block, down_ref[pl.ds(at, units), :], preferred_element_type=F32)
    for e in range(columns):
        outs[e][...] = total[e * slots : (e + 1) * slots].astype(BF16)


def spread_kernel(groups, columns, pick_ref, *refs):
    blocks, outs = refs[:columns][::-1], refs[columns:]
    for e in range(columns):
        block = blocks[e][...]
        back = jnp.dot(pick_ref[:, : block.shape[0]], block, preferred_element_type=F32)
        for d in range(groups):
            outs[d][e] = back[d * CAP : (d + 1) * CAP].astype(BF16)


def combine_kernel(groups, columns, mixing_ref, *refs):
    backs, (out_ref, held, sems) = refs[:groups][::-1], refs[groups:]
    me = lax.axis_index("ing")
    width, half = backs[0].shape[2], held.shape[0] // 2
    copies = []
    for e in range(columns):
        rows = jnp.concatenate([backs[d][e].astype(F32) for d in range(groups)], axis=0)
        rows = rows.astype(BF16)
        part = pl.ds(e * width, width)
        there = pl.ds(pl.multiple_of((me ^ e) * width, width), width)
        for h in range(2):
            mine = pl.ds(h * half, half)
            value = jnp.dot(mixing_ref[mine, :], rows, preferred_element_type=F32)
            held[mine, part] = value.astype(BF16)
            copies.append(
                pltpu.make_async_copy(held.at[mine, part], out_ref.at[mine, there], sems.at[2 * e + h])
            )
            copies[-1].start()
    for copy in copies:
        copy.wait()


def swap(x, name, step):
    if step == 0:
        return x
    return lax.ppermute(x, name, [(a, a ^ step) for a in range(lax.axis_size(name))])


def swap_all(parts, name):
    return [swap(part, name, k) for k, part in enumerate(parts)][::-1]


def local(tokens, router_logits, expert_ids, w_gate, w_up, w_down):
    groups = lax.axis_size("grp")
    columns = lax.axis_size("ing")
    count, features = tokens.shape
    units, share = w_gate.shape[2], w_down.shape[2]
    slots = groups * CAP // 2
    wide = features + LANES
    ids = pltpu.with_memory_space_constraint(expert_ids.T, pltpu.HBM)
    logits = pltpu.with_memory_space_constraint(router_logits.T, pltpu.HBM)

    outbound = pl.pallas_call(
        functools.partial(dispatch_kernel, groups, features // 2),
        out_shape=[jax.ShapeDtypeStruct((CAP, wide), BF16)] * groups,
        in_specs=[ANY, ANY],
        out_specs=[VMEM] * groups,
        scratch_shapes=[
            pltpu.VMEM(ids.shape, jnp.int32),
            pltpu.VMEM((count, features), BF16),
            pltpu.VMEM((count, count), BF16),
            pltpu.SemaphoreType.DMA((3,)),
        ],
        compiler_params=params(2 * count * features),
        name="dispatch",
    )(ids, pltpu.with_memory_space_constraint(tokens, pltpu.HBM))
    arrived = swap_all(outbound, "grp")

    weights = [w_gate[0], w_up[0], w_down[0]]
    weights = [pltpu.with_memory_space_constraint(w, pltpu.HBM) for w in weights]
    gate, up = pl.pallas_call(
        load_kernel,
        out_shape=[pltpu.VMEM(w.shape, BF16) for w in weights[:2]],
        in_specs=[ANY] * 3,
        out_specs=[VMEM] * 2,
        scratch_shapes=[pltpu.SemaphoreType.DMA((8,))],
        compiler_params=params(0),
        name="load",
    )(outbound[0], *weights[:2])

    parts = 2 if columns == 4 else 1
    *own, pick = pl.pallas_call(
        functools.partial(compact_kernel, groups, slots),
        out_shape=[jax.ShapeDtypeStruct((slots, features // parts), BF16)] * parts
        + [jax.ShapeDtypeStruct((groups * CAP, LANES), BF16)],
        in_specs=[ANY] + [VMEM] * groups,
        out_specs=[VMEM] * (parts + 1),
        compiler_params=params(2 * (groups * CAP + slots) * wide),
        name="compact",
    )(gate, *arrived)
    if columns == 4:
        near_low, near_high, high, far_high = [swap(part, "ing", e) for part, e in zip(own + own[1:] * 2, (1, 1, 2, 3))]
        low = swap(own[0], "ing", 2)
        far_low = swap(low, "ing", 1)
        blocks = [low, near_low, near_high, high, far_high, far_low] + own
    else:
        blocks = [swap(own[0], "ing", e) for e in range(columns)]

    hidden = pl.pallas_call(
        functools.partial(hidden_kernel, columns, columns == 4),
        out_shape=jax.ShapeDtypeStruct((columns * slots, units), BF16),
        in_specs=[VMEM] * (len(blocks) + 2),
        out_specs=VMEM,
        compiler_params=params(2 * columns * slots * (2 * features + units)),
        name="hidden",
    )(*blocks, gate, up)
    down, mixing = pl.pallas_call(
        functools.partial(prepare_kernel, groups),
        out_shape=[
            pltpu.VMEM(w_down.shape[1:], BF16),
            jax.ShapeDtypeStruct((count, groups * CAP), BF16),
        ],
        in_specs=[ANY] * 4,
        out_specs=[VMEM] * 2,
        scratch_shapes=[
            pltpu.VMEM(ids.shape, jnp.int32),
            pltpu.VMEM(logits.shape, F32),
            pltpu.SemaphoreType.DMA((6,)),
        ],
        compiler_params=params(0),
        name="prepare",
    )(hidden, ids, logits, weights[2])
    hiddens = [swap(hidden, "ing", f) for f in range(columns)]

    results = pl.pallas_call(
        functools.partial(down_kernel, columns),
        out_shape=[jax.ShapeDtypeStruct((slots, share), BF16)] * columns,
        in_specs=[VMEM] * (columns + 1),
        out_specs=[VMEM] * columns,
        compiler_params=params(2 * columns * slots * (columns * units + 4 * share)),
        name="down",
    )(*hiddens, down)
    results = swap_all(results, "ing")

    backs = pl.pallas_call(
        functools.partial(spread_kernel, groups, columns),
        out_shape=[jax.ShapeDtypeStruct((columns, CAP, share), BF16)] * groups,
        in_specs=[VMEM] * (columns + 1),
        out_specs=[VMEM] * groups,
        compiler_params=params(2 * (groups * CAP + slots) * features),
        name="spread",
    )(pick, *results)
    backs = swap_all(backs, "grp")

    if share % LANES:
        me = lax.axis_index("ing")
        rows = jnp.stack(backs[::-1])[:, jnp.arange(columns) ^ me]
        rows = rows.transpose(0, 2, 1, 3).reshape(groups * CAP, features)
        return jnp.dot(mixing, rows, preferred_element_type=F32).astype(BF16)
    return pl.pallas_call(
        functools.partial(combine_kernel, groups, columns),
        out_shape=jax.ShapeDtypeStruct((count, features), BF16),
        in_specs=[VMEM] * (1 + groups),
        out_specs=ANY,
        scratch_shapes=[pltpu.VMEM((count, features), BF16), pltpu.SemaphoreType.DMA((2 * columns,))],
        compiler_params=params(2 * (count + groups * CAP) * features),
        name="combine",
    )(mixing, *backs)


def solution(mesh):
    placed = (
        P(("rep", "grp", "ing"), None),
        P(("rep", "grp", "ing"), None),
        P(("rep", "grp", "ing"), None),
        P("grp", None, "ing"),
        P("grp", None, "ing"),
        P("grp", None, "ing"),
    )
    return jax.shard_map(
        local, mesh=mesh, in_specs=placed, out_specs=P(("rep", "grp", "ing"), None), check_vma=False
    )
```

```python
import functools

import jax
import jax.numpy as jnp
from jax import lax
from jax.experimental import pallas as pl
from jax.experimental.pallas import tpu as pltpu
from jax.sharding import PartitionSpec as P

GROUP_EXPERTS = 24
CAP = 8
LANES = 128
ROUTE_SCALE = 2.827
MIB = 1024 * 1024

BF16 = jnp.bfloat16
F32 = jnp.float32
VMEM = pl.BlockSpec(memory_space=pltpu.VMEM)
ANY = pl.BlockSpec(memory_space=pl.ANY)


def params(nbytes):
    return pltpu.CompilerParams(vmem_limit_bytes=2 * nbytes + 4 * MIB)


def named(ids, expert):
    hit = jnp.zeros(expert.shape, F32)
    for k in range(ids.shape[0]):
        hit = jnp.where(ids[k : k + 1, :] == expert, 1.0, hit)
    return hit


def upto(count):
    return (
        lax.broadcasted_iota(jnp.int32, (count, count), 0)
        <= lax.broadcasted_iota(jnp.int32, (count, count), 1)
    ).astype(BF16)


def placing(ids, groups, me, before):
    rows, count = groups * CAP, ids.shape[1]
    row = lax.broadcasted_iota(jnp.int32, (rows, count), 0)
    group = (row // CAP) ^ me
    hit = named(ids, group * GROUP_EXPERTS)
    rank = jnp.dot(hit.astype(BF16), before, preferred_element_type=F32)
    slot = lax.rem(row, CAP).astype(F32)
    return jnp.where((hit > 0.5) & (rank == slot + 1.0), 1.0, 0.0), group


def dispatch_kernel(groups, width, ids_ref, tokens_ref, *refs):
    outs, (ids_held, staged, before_ref, sems) = refs[:groups], refs[groups:]
    me = lax.axis_index("grp")
    features = tokens_ref.shape[1]
    first = pltpu.make_async_copy(ids_ref, ids_held, sems.at[features // width])
    first.start()
    copies = []
    for c in range(features // width):
        part = pl.ds(c * width, width)
        copies.append(pltpu.make_async_copy(tokens_ref.at[:, part], staged.at[:, part], sems.at[c]))
        copies[-1].start()
    before_ref[...] = upto(tokens_ref.shape[0])
    first.wait()
    place, _ = placing(ids_held[...], groups, me, before_ref[...])
    live = jnp.sum(place, axis=1, keepdims=True)
    place = place.astype(BF16)
    for d in range(groups):
        outs[d][:, features:] = jnp.broadcast_to(live[d * CAP : (d + 1) * CAP], (CAP, LANES)).astype(BF16)
    for c in range(features // width):
        copies[c].wait()
        part = slice(c * width, (c + 1) * width)
        rows = jnp.dot(place, staged[:, part], preferred_element_type=F32)
        for d in range(groups):
            outs[d][:, part] = rows[d * CAP : (d + 1) * CAP].astype(BF16)


def start_loads(weights, loaded, sems):
    copies = []
    for k in range(len(weights)):
        depth = weights[k].shape[0]
        for c in range(4):
            part = pl.ds(c * (depth // 4), depth // 4)
            copies.append(pltpu.make_async_copy(weights[k].at[part], loaded[k].at[part], sems.at[4 * k + c]))
            copies[-1].start()
    return copies


def load_kernel(after_ref, gate_ref, up_ref, gate_out, up_out, sems):
    del after_ref
    for copy in start_loads([gate_ref, up_ref], [gate_out, up_out], sems):
        copy.wait()


def prepare_kernel(groups, after_ref, ids_ref, logits_ref, down_ref, down_out, out_ref, ids_held, logits_held, sems):
    del after_ref
    small = [
        pltpu.make_async_copy(ids_ref, ids_held, sems.at[4]),
        pltpu.make_async_copy(logits_ref, logits_held, sems.at[5]),
    ]
    for copy in small:
        copy.start()
    copies = start_loads([down_ref], [down_out], sems)
    for copy in small:
        copy.wait()
    me = lax.axis_index("grp")
    ids = ids_held[...]
    place, group = placing(ids, groups, me, upto(ids.shape[1]))
    scores = 1.0 / (1.0 + jnp.exp(-logits_held[...]))
    expert = lax.broadcasted_iota(jnp.int32, scores.shape, 0)
    chosen = jnp.sum(jnp.where(named(ids, expert) > 0.5, scores, 0.0), axis=0, keepdims=True)
    leading = jnp.zeros(place.shape, F32)
    for g in range(groups):
        leading = jnp.where(group == g, scores[g * GROUP_EXPERTS : g * GROUP_EXPERTS + 1, :], leading)
    weight = (ROUTE_SCALE * leading / chosen).astype(BF16).astype(F32)
    out_ref[...] = jnp.where(place > 0.5, weight, 0.0).T.astype(BF16)
    for copy in copies:
        copy.wait()


def compact_kernel(groups, slots, parts, after_ref, *refs):
    del after_ref
    arrived, outs, pick_ref = refs[:groups][::-1], refs[groups:-1], refs[-1]
    rows = groups * CAP
    features = arrived[0].shape[1] - LANES
    live = jnp.concatenate([a[:, features:].astype(F32) for a in arrived], axis=0)
    row = lax.broadcasted_iota(jnp.int32, (rows, rows), 0)
    column = lax.broadcasted_iota(jnp.int32, (rows, rows), 1)
    rank = jnp.dot((column <= row).astype(BF16), live.astype(BF16), preferred_element_type=F32)
    lane = lax.broadcasted_iota(jnp.int32, (rows, LANES), 1).astype(F32)
    pick = jnp.where((live > 0.5) & (rank == lane + 1.0), 1.0, 0.0).astype(BF16)
    pick_ref[...] = pick
    step = 256
    for c in range(features // step):
        at = slice(c * step, (c + 1) * step)
        whole = jnp.concatenate([a[:, at].astype(F32) for a in arrived], axis=0).astype(BF16)
        moved = lax.dot_general(pick[:, :slots], whole, (((0,), (0,)), ((), ())), preferred_element_type=F32)
        for (first, last), out in zip(parts, outs):
            if first <= c * step < last:
                out[:, c * step - first : (c + 1) * step - first] = moved.astype(BF16)


def hidden_kernel(columns, halved, *refs):
    blocks, (gate_ref, up_ref, hidden_ref) = refs[:-3], refs[-3:]
    units = gate_ref.shape[1]
    blocks = [block[...] for block in blocks]
    if halved:
        low, near_high, high, far_high, near_low, far_low, own_low, own_high = blocks
        pairs = [(own_low, own_high), (near_low, near_high), (low, high), (far_low, far_high)]
        blocks = [jnp.concatenate(pair, axis=1) for pair in pairs]
    rows = jnp.concatenate(blocks, axis=0)
    step = min(256, units)
    for c in range(units // step):
        part = slice(c * step, (c + 1) * step)
        gate = jnp.dot(rows, gate_ref[:, part], preferred_element_type=F32)
        up = jnp.dot(rows, up_ref[:, part], preferred_element_type=F32)
        hidden_ref[:, part] = (gate / (1.0 + jnp.exp(-gate)) * up).astype(BF16)


def down_kernel(columns, *refs):
    hiddens, down_ref, outs = refs[:columns], refs[columns], refs[columns + 1 :]
    me = lax.axis_index("ing")
    rows, units = hiddens[0].shape
    slots = rows // columns
    total = jnp.zeros((rows, down_ref.shape[1]), F32)
    for f in range(columns):
        block = jnp.concatenate(
            [hiddens[f][slots * (e ^ f) : slots * ((e ^ f) + 1), :] for e in range(columns)], axis=0
        )
        at = pl.multiple_of((me ^ f) * units, units)
        total += jnp.dot(block, down_ref[pl.ds(at, units), :], preferred_element_type=F32)
    for e in range(columns):
        outs[e][...] = total[e * slots : (e + 1) * slots].astype(BF16)


def spread_kernel(groups, columns, pick_ref, *refs):
    blocks, outs = refs[:columns][::-1], refs[columns:]
    for e in range(columns):
        block = blocks[e][...]
        back = jnp.dot(pick_ref[:, : block.shape[0]], block, preferred_element_type=F32)
        for d in range(groups):
            outs[d][e] = back[d * CAP : (d + 1) * CAP].astype(BF16)


def combine_kernel(groups, columns, mixing_ref, *refs):
    backs, (out_ref, held, sems) = refs[:groups][::-1], refs[groups:]
    me = lax.axis_index("ing")
    width, half = backs[0].shape[2], held.shape[0] // 2
    copies = []
    for e in range(columns):
        rows = jnp.concatenate([backs[d][e].astype(F32) for d in range(groups)], axis=0)
        rows = rows.astype(BF16)
        part = pl.ds(e * width, width)
        there = pl.ds(pl.multiple_of((me ^ e) * width, width), width)
        for h in range(2):
            mine = pl.ds(h * half, half)
            value = jnp.dot(mixing_ref[mine, :], rows, preferred_element_type=F32)
            held[mine, part] = value.astype(BF16)
            copies.append(
                pltpu.make_async_copy(held.at[mine, part], out_ref.at[mine, there], sems.at[2 * e + h])
            )
            copies[-1].start()
    for copy in copies:
        copy.wait()


def swap(x, name, step):
    if step == 0:
        return x
    return lax.ppermute(x, name, [(a, a ^ step) for a in range(lax.axis_size(name))])


def swap_all(parts, name):
    return [swap(part, name, k) for k, part in enumerate(parts)][::-1]


def local(tokens, router_logits, expert_ids, w_gate, w_up, w_down):
    groups = lax.axis_size("grp")
    columns = lax.axis_size("ing")
    count, features = tokens.shape
    units, share = w_gate.shape[2], w_down.shape[2]
    slots = groups * CAP // 2
    wide = features + LANES
    ids = pltpu.with_memory_space_constraint(expert_ids.T, pltpu.HBM)
    logits = pltpu.with_memory_space_constraint(router_logits.T, pltpu.HBM)

    outbound = pl.pallas_call(
        functools.partial(dispatch_kernel, groups, features // 2),
        out_shape=[jax.ShapeDtypeStruct((CAP, wide), BF16)] * groups,
        in_specs=[ANY, ANY],
        out_specs=[VMEM] * groups,
        scratch_shapes=[
            pltpu.VMEM(ids.shape, jnp.int32),
            pltpu.VMEM((count, features), BF16),
            pltpu.VMEM((count, count), BF16),
            pltpu.SemaphoreType.DMA((3,)),
        ],
        compiler_params=params(2 * count * features),
        name="dispatch",
    )(ids, pltpu.with_memory_space_constraint(tokens, pltpu.HBM))
    arrived = swap_all(outbound, "grp")

    weights = [w_gate[0], w_up[0], w_down[0]]
    weights = [pltpu.with_memory_space_constraint(w, pltpu.HBM) for w in weights]
    gate, up = pl.pallas_call(
        load_kernel,
        out_shape=[pltpu.VMEM(w.shape, BF16) for w in weights[:2]],
        in_specs=[ANY] * 3,
        out_specs=[VMEM] * 2,
        scratch_shapes=[pltpu.SemaphoreType.DMA((8,))],
        compiler_params=params(0),
        name="load",
    )(outbound[0], *weights[:2])

    cut = features * 3 // 7 // 256 * 256
    parts = [(0, cut), (cut, features), (0, cut)] if columns == 4 else [(0, features)]
    *own, pick = pl.pallas_call(
        functools.partial(compact_kernel, groups, slots, parts),
        out_shape=[jax.ShapeDtypeStruct((slots, last - first), BF16) for first, last in parts]
        + [jax.ShapeDtypeStruct((groups * CAP, LANES), BF16)],
        in_specs=[ANY] + [VMEM] * groups,
        out_specs=[VMEM] * (len(parts) + 1),
        compiler_params=params(2 * (groups * CAP + 2 * slots) * wide),
        name="compact",
    )(gate, *arrived)
    if columns == 4:
        own_low, own_high, own_again = own
        near_high, high, far_high = [swap(own_high, "ing", e) for e in (1, 2, 3)]
        low = swap(own_low, "ing", 2)
        far_low = swap(low, "ing", 1)
        near_low = swap(own_again, "ing", 1)
        blocks = [low, near_high, high, far_high, near_low, far_low, own_low, own_high]
    else:
        blocks = [swap(own[0], "ing", e) for e in range(columns)]

    hidden = pl.pallas_call(
        functools.partial(hidden_kernel, columns, columns == 4),
        out_shape=jax.ShapeDtypeStruct((columns * slots, units), BF16),
        in_specs=[VMEM] * (len(blocks) + 2),
        out_specs=VMEM,
        compiler_params=params(2 * columns * slots * (2 * features + units)),
        name="hidden",
    )(*blocks, gate, up)
    down, mixing = pl.pallas_call(
        functools.partial(prepare_kernel, groups),
        out_shape=[
            pltpu.VMEM(w_down.shape[1:], BF16),
            jax.ShapeDtypeStruct((count, groups * CAP), BF16),
        ],
        in_specs=[ANY] * 4,
        out_specs=[VMEM] * 2,
        scratch_shapes=[
            pltpu.VMEM(ids.shape, jnp.int32),
            pltpu.VMEM(logits.shape, F32),
            pltpu.SemaphoreType.DMA((6,)),
        ],
        compiler_params=params(0),
        name="prepare",
    )(hidden, ids, logits, weights[2])
    hiddens = [swap(hidden, "ing", f) for f in range(columns)]

    results = pl.pallas_call(
        functools.partial(down_kernel, columns),
        out_shape=[jax.ShapeDtypeStruct((slots, share), BF16)] * columns,
        in_specs=[VMEM] * (columns + 1),
        out_specs=[VMEM] * columns,
        compiler_params=params(2 * columns * slots * (columns * units + 4 * share)),
        name="down",
    )(*hiddens, down)
    results = swap_all(results, "ing")

    backs = pl.pallas_call(
        functools.partial(spread_kernel, groups, columns),
        out_shape=[jax.ShapeDtypeStruct((columns, CAP, share), BF16)] * groups,
        in_specs=[VMEM] * (columns + 1),
        out_specs=[VMEM] * groups,
        compiler_params=params(2 * (groups * CAP + slots) * features),
        name="spread",
    )(pick, *results)
    backs = swap_all(backs, "grp")

    if share % LANES:
        me = lax.axis_index("ing")
        rows = jnp.stack(backs[::-1])[:, jnp.arange(columns) ^ me]
        rows = rows.transpose(0, 2, 1, 3).reshape(groups * CAP, features)
        return jnp.dot(mixing, rows, preferred_element_type=F32).astype(BF16)
    return pl.pallas_call(
        functools.partial(combine_kernel, groups, columns),
        out_shape=jax.ShapeDtypeStruct((count, features), BF16),
        in_specs=[VMEM] * (1 + groups),
        out_specs=ANY,
        scratch_shapes=[pltpu.VMEM((count, features), BF16), pltpu.SemaphoreType.DMA((2 * columns,))],
        compiler_params=params(2 * (count + groups * CAP) * features),
        name="combine",
    )(mixing, *backs)


def solution(mesh):
    placed = (
        P(("rep", "grp", "ing"), None),
        P(("rep", "grp", "ing"), None),
        P(("rep", "grp", "ing"), None),
        P("grp", None, "ing"),
        P("grp", None, "ing"),
        P("grp", None, "ing"),
    )
    return jax.shard_map(
        local, mesh=mesh, in_specs=placed, out_specs=P(("rep", "grp", "ing"), None), check_vma=False
    )
```

```python
import functools

import jax
import jax.numpy as jnp
from jax import lax
from jax.experimental import pallas as pl
from jax.experimental.pallas import tpu as pltpu
from jax.sharding import PartitionSpec as P

GROUP_EXPERTS = 24
CAP = 8
LANES = 128
ROUTE_SCALE = 2.827
MIB = 1024 * 1024

BF16 = jnp.bfloat16
F32 = jnp.float32
VMEM = pl.BlockSpec(memory_space=pltpu.VMEM)
ANY = pl.BlockSpec(memory_space=pl.ANY)


def params(nbytes):
    return pltpu.CompilerParams(vmem_limit_bytes=2 * nbytes + 4 * MIB)


def named(ids, expert):
    hit = jnp.zeros(expert.shape, F32)
    for k in range(ids.shape[0]):
        hit = jnp.where(ids[k : k + 1, :] == expert, 1.0, hit)
    return hit


def upto(count):
    return (
        lax.broadcasted_iota(jnp.int32, (count, count), 0)
        <= lax.broadcasted_iota(jnp.int32, (count, count), 1)
    ).astype(BF16)


def placing(ids, groups, me, before):
    rows, count = max(groups, 8), ids.shape[1]
    row = lax.broadcasted_iota(jnp.int32, (rows, count), 0)
    hit = named(ids, jnp.where(row < groups, (row ^ me) * GROUP_EXPERTS, -1))
    rank = jnp.dot(hit.astype(BF16), before, preferred_element_type=F32)
    slot = lax.broadcasted_iota(jnp.int32, (CAP, count), 0).astype(F32) + 1.0
    seat = jnp.where(hit > 0.5, rank, 0.0)
    place = [jnp.where(seat[d : d + 1, :] == slot, 1.0, 0.0) for d in range(groups)]
    return jnp.concatenate(place, axis=0), rank[:, count - 1 :]


def dispatch_kernel(groups, width, ids_ref, tokens_ref, *refs):
    outs, (ids_held, staged, before_ref, sems) = refs[:groups], refs[groups:]
    me = lax.axis_index("grp")
    features = tokens_ref.shape[1]
    first = pltpu.make_async_copy(ids_ref, ids_held, sems.at[features // width])
    first.start()
    copies = []
    for c in range(features // width):
        part = pl.ds(c * width, width)
        copies.append(pltpu.make_async_copy(tokens_ref.at[:, part], staged.at[:, part], sems.at[c]))
        copies[-1].start()
    before_ref[...] = upto(tokens_ref.shape[0])
    first.wait()
    place, counts = placing(ids_held[...], groups, me, before_ref[...])
    place = place.astype(BF16)
    slot = lax.broadcasted_iota(jnp.int32, (CAP, LANES), 0).astype(F32)
    for d in range(groups):
        live = slot < jnp.broadcast_to(counts[d : d + 1, :], (CAP, LANES))
        outs[d][:, features:] = jnp.where(live, 1.0, 0.0).astype(BF16)
    for c in range(features // width):
        copies[c].wait()
        part = slice(c * width, (c + 1) * width)
        rows = jnp.dot(place, staged[:, part], preferred_element_type=F32)
        for d in range(groups):
            outs[d][:, part] = rows[d * CAP : (d + 1) * CAP].astype(BF16)


def start_loads(weights, loaded, sems):
    copies = []
    for k in range(len(weights)):
        depth = weights[k].shape[0]
        for c in range(4):
            part = pl.ds(c * (depth // 4), depth // 4)
            copies.append(pltpu.make_async_copy(weights[k].at[part], loaded[k].at[part], sems.at[4 * k + c]))
            copies[-1].start()
    return copies


def load_kernel(after_ref, gate_ref, up_ref, gate_out, up_out, sems):
    del after_ref
    for copy in start_loads([gate_ref, up_ref], [gate_out, up_out], sems):
        copy.wait()


def prepare_kernel(groups, after_ref, ids_ref, logits_ref, down_ref, down_out, out_ref, ids_held, logits_held, sems):
    del after_ref
    small = [
        pltpu.make_async_copy(ids_ref, ids_held, sems.at[4]),
        pltpu.make_async_copy(logits_ref, logits_held, sems.at[5]),
    ]
    for copy in small:
        copy.start()
    copies = start_loads([down_ref], [down_out], sems)
    for copy in small:
        copy.wait()
    me = lax.axis_index("grp")
    ids = ids_held[...]
    place, _ = placing(ids, groups, me, upto(ids.shape[1]))
    group = (lax.broadcasted_iota(jnp.int32, place.shape, 0) // CAP) ^ me
    scores = 1.0 / (1.0 + jnp.exp(-logits_held[...]))
    expert = lax.broadcasted_iota(jnp.int32, scores.shape, 0)
    chosen = jnp.sum(jnp.where(named(ids, expert) > 0.5, scores, 0.0), axis=0, keepdims=True)
    leading = jnp.zeros(place.shape, F32)
    for g in range(groups):
        leading = jnp.where(group == g, scores[g * GROUP_EXPERTS : g * GROUP_EXPERTS + 1, :], leading)
    weight = (ROUTE_SCALE * leading / chosen).astype(BF16).astype(F32)
    out_ref[...] = jnp.where(place > 0.5, weight, 0.0).T.astype(BF16)
    for copy in copies:
        copy.wait()


def compact_kernel(groups, slots, parts, after_ref, *refs):
    del after_ref
    arrived, outs, pick_ref = refs[:groups][::-1], refs[groups:-1], refs[-1]
    rows = groups * CAP
    features = arrived[0].shape[1] - LANES
    live = jnp.concatenate([a[:, features:].astype(F32) for a in arrived], axis=0)
    row = lax.broadcasted_iota(jnp.int32, (rows, rows), 0)
    column = lax.broadcasted_iota(jnp.int32, (rows, rows), 1)
    rank = jnp.dot((column <= row).astype(BF16), live.astype(BF16), preferred_element_type=F32)
    lane = lax.broadcasted_iota(jnp.int32, (rows, LANES), 1).astype(F32)
    pick = jnp.where((live > 0.5) & (rank == lane + 1.0), 1.0, 0.0).astype(BF16)
    pick_ref[...] = pick
    step = 256
    for c in range(features // step):
        at = slice(c * step, (c + 1) * step)
        whole = jnp.concatenate([a[:, at].astype(F32) for a in arrived], axis=0).astype(BF16)
        moved = lax.dot_general(pick[:, :slots], whole, (((0,), (0,)), ((), ())), preferred_element_type=F32)
        for (first, last), out in zip(parts, outs):
            if first <= c * step < last:
                out[:, c * step - first : (c + 1) * step - first] = moved.astype(BF16)


def hidden_kernel(columns, halved, *refs):
    blocks, (gate_ref, up_ref, hidden_ref) = refs[:-3], refs[-3:]
    units = gate_ref.shape[1]
    blocks = [block[...] for block in blocks]
    if halved:
        low, near_low, near_high, high, far_high, far_low, own_low, own_high = blocks
        pairs = [(own_low, own_high), (near_low, near_high), (low, high), (far_low, far_high)]
        blocks = [jnp.concatenate(pair, axis=1) for pair in pairs]
    rows = jnp.concatenate(blocks, axis=0)
    step = min(256, units)
    for c in range(units // step):
        part = slice(c * step, (c + 1) * step)
        gate = jnp.dot(rows, gate_ref[:, part], preferred_element_type=F32)
        up = jnp.dot(rows, up_ref[:, part], preferred_element_type=F32)
        hidden_ref[:, part] = (gate / (1.0 + jnp.exp(-gate)) * up).astype(BF16)


def down_kernel(columns, *refs):
    hiddens, down_ref, outs = refs[:columns], refs[columns], refs[columns + 1 :]
    me = lax.axis_index("ing")
    rows, units = hiddens[0].shape
    slots = rows // columns
    total = jnp.zeros((rows, down_ref.shape[1]), F32)
    for f in range(columns):
        block = jnp.concatenate(
            [hiddens[f][slots * (e ^ f) : slots * ((e ^ f) + 1), :] for e in range(columns)], axis=0
        )
        at = pl.multiple_of((me ^ f) * units, units)
        total += jnp.dot(block, down_ref[pl.ds(at, units), :], preferred_element_type=F32)
    for e in range(columns):
        outs[e][...] = total[e * slots : (e + 1) * slots].astype(BF16)


def spread_kernel(groups, columns, pick_ref, *refs):
    blocks, outs = refs[:columns][::-1], refs[columns:]
    for e in range(columns):
        block = blocks[e][...]
        back = jnp.dot(pick_ref[:, : block.shape[0]], block, preferred_element_type=F32)
        for d in range(groups):
            outs[d][e] = back[d * CAP : (d + 1) * CAP].astype(BF16)


def combine_kernel(groups, columns, mixing_ref, *refs):
    backs, (out_ref, held, sems) = refs[:groups][::-1], refs[groups:]
    me = lax.axis_index("ing")
    width, half = backs[0].shape[2], held.shape[0] // 2
    copies = []
    for e in range(columns):
        rows = jnp.concatenate([backs[d][e].astype(F32) for d in range(groups)], axis=0)
        rows = rows.astype(BF16)
        part = pl.ds(e * width, width)
        there = pl.ds(pl.multiple_of((me ^ e) * width, width), width)
        for h in range(2):
            mine = pl.ds(h * half, half)
            value = jnp.dot(mixing_ref[mine, :], rows, preferred_element_type=F32)
            held[mine, part] = value.astype(BF16)
            copies.append(
                pltpu.make_async_copy(held.at[mine, part], out_ref.at[mine, there], sems.at[2 * e + h])
            )
            copies[-1].start()
    for copy in copies:
        copy.wait()


def swap(x, name, step):
    if step == 0:
        return x
    return lax.ppermute(x, name, [(a, a ^ step) for a in range(lax.axis_size(name))])


def swap_all(parts, name):
    return [swap(part, name, k) for k, part in enumerate(parts)][::-1]


def local(tokens, router_logits, expert_ids, w_gate, w_up, w_down):
    groups = lax.axis_size("grp")
    columns = lax.axis_size("ing")
    count, features = tokens.shape
    units, share = w_gate.shape[2], w_down.shape[2]
    slots = groups * CAP // 2
    wide = features + LANES
    ids = pltpu.with_memory_space_constraint(expert_ids.T, pltpu.HBM)
    logits = pltpu.with_memory_space_constraint(router_logits.T, pltpu.HBM)

    outbound = pl.pallas_call(
        functools.partial(dispatch_kernel, groups, features // 2),
        out_shape=[jax.ShapeDtypeStruct((CAP, wide), BF16)] * groups,
        in_specs=[ANY, ANY],
        out_specs=[VMEM] * groups,
        scratch_shapes=[
            pltpu.VMEM(ids.shape, jnp.int32),
            pltpu.VMEM((count, features), BF16),
            pltpu.VMEM((count, count), BF16),
            pltpu.SemaphoreType.DMA((3,)),
        ],
        compiler_params=params(2 * count * features),
        name="dispatch",
    )(ids, pltpu.with_memory_space_constraint(tokens, pltpu.HBM))
    arrived = swap_all(outbound, "grp")

    weights = [w_gate[0], w_up[0], w_down[0]]
    weights = [pltpu.with_memory_space_constraint(w, pltpu.HBM) for w in weights]
    gate, up = pl.pallas_call(
        load_kernel,
        out_shape=[pltpu.VMEM(w.shape, BF16) for w in weights[:2]],
        in_specs=[ANY] * 3,
        out_specs=[VMEM] * 2,
        scratch_shapes=[pltpu.SemaphoreType.DMA((8,))],
        compiler_params=params(0),
        name="load",
    )(outbound[0], *weights[:2])

    cut = features // 2
    parts = [(0, cut), (cut, features)] if columns == 4 else [(0, features)]
    *own, pick = pl.pallas_call(
        functools.partial(compact_kernel, groups, slots, parts),
        out_shape=[jax.ShapeDtypeStruct((slots, last - first), BF16) for first, last in parts]
        + [jax.ShapeDtypeStruct((groups * CAP, LANES), BF16)],
        in_specs=[ANY] + [VMEM] * groups,
        out_specs=[VMEM] * (len(parts) + 1),
        compiler_params=params(2 * (groups * CAP + 2 * slots) * wide),
        name="compact",
    )(gate, *arrived)
    if columns == 4:
        near_low, near_high, high, far_high = [swap(part, "ing", e) for part, e in zip(own + own[1:] * 2, (1, 1, 2, 3))]
        low = swap(own[0], "ing", 2)
        far_low = swap(low, "ing", 1)
        blocks = [low, near_low, near_high, high, far_high, far_low] + own
    else:
        blocks = [swap(own[0], "ing", e) for e in range(columns)]

    hidden = pl.pallas_call(
        functools.partial(hidden_kernel, columns, columns == 4),
        out_shape=jax.ShapeDtypeStruct((columns * slots, units), BF16),
        in_specs=[VMEM] * (len(blocks) + 2),
        out_specs=VMEM,
        compiler_params=params(2 * columns * slots * (2 * features + units)),
        name="hidden",
    )(*blocks, gate, up)
    down, mixing = pl.pallas_call(
        functools.partial(prepare_kernel, groups),
        out_shape=[
            pltpu.VMEM(w_down.shape[1:], BF16),
            jax.ShapeDtypeStruct((count, groups * CAP), BF16),
        ],
        in_specs=[ANY] * 4,
        out_specs=[VMEM] * 2,
        scratch_shapes=[
            pltpu.VMEM(ids.shape, jnp.int32),
            pltpu.VMEM(logits.shape, F32),
            pltpu.SemaphoreType.DMA((6,)),
        ],
        compiler_params=params(0),
        name="prepare",
    )(hidden, ids, logits, weights[2])
    hiddens = [swap(hidden, "ing", f) for f in range(columns)]

    results = pl.pallas_call(
        functools.partial(down_kernel, columns),
        out_shape=[jax.ShapeDtypeStruct((slots, share), BF16)] * columns,
        in_specs=[VMEM] * (columns + 1),
        out_specs=[VMEM] * columns,
        compiler_params=params(2 * columns * slots * (columns * units + 4 * share)),
        name="down",
    )(*hiddens, down)
    results = swap_all(results, "ing")

    backs = pl.pallas_call(
        functools.partial(spread_kernel, groups, columns),
        out_shape=[jax.ShapeDtypeStruct((columns, CAP, share), BF16)] * groups,
        in_specs=[VMEM] * (columns + 1),
        out_specs=[VMEM] * groups,
        compiler_params=params(2 * (groups * CAP + slots) * features),
        name="spread",
    )(pick, *results)
    backs = swap_all(backs, "grp")

    if share % LANES:
        me = lax.axis_index("ing")
        rows = jnp.stack(backs[::-1])[:, jnp.arange(columns) ^ me]
        rows = rows.transpose(0, 2, 1, 3).reshape(groups * CAP, features)
        return jnp.dot(mixing, rows, preferred_element_type=F32).astype(BF16)
    return pl.pallas_call(
        functools.partial(combine_kernel, groups, columns),
        out_shape=jax.ShapeDtypeStruct((count, features), BF16),
        in_specs=[VMEM] * (1 + groups),
        out_specs=ANY,
        scratch_shapes=[pltpu.VMEM((count, features), BF16), pltpu.SemaphoreType.DMA((2 * columns,))],
        compiler_params=params(2 * (count + groups * CAP) * features),
        name="combine",
    )(mixing, *backs)


def solution(mesh):
    placed = (
        P(("rep", "grp", "ing"), None),
        P(("rep", "grp", "ing"), None),
        P(("rep", "grp", "ing"), None),
        P("grp", None, "ing"),
        P("grp", None, "ing"),
        P("grp", None, "ing"),
    )
    return jax.shard_map(
        local, mesh=mesh, in_specs=placed, out_specs=P(("rep", "grp", "ing"), None), check_vma=False
    )
```

```python
import functools

import jax
import jax.numpy as jnp
from jax import lax
from jax.experimental import pallas as pl
from jax.experimental.pallas import tpu as pltpu
from jax.sharding import PartitionSpec as P

GROUP_EXPERTS = 24
CAP = 8
LANES = 128
ROUTE_SCALE = 2.827
MIB = 1024 * 1024

BF16 = jnp.bfloat16
F32 = jnp.float32
VMEM = pl.BlockSpec(memory_space=pltpu.VMEM)
ANY = pl.BlockSpec(memory_space=pl.ANY)


def params(nbytes):
    return pltpu.CompilerParams(vmem_limit_bytes=2 * nbytes + 4 * MIB)


def named(ids, expert):
    hit = jnp.zeros(expert.shape, F32)
    for k in range(ids.shape[0]):
        hit = jnp.where(ids[k : k + 1, :] == expert, 1.0, hit)
    return hit


def upto(count):
    return (
        lax.broadcasted_iota(jnp.int32, (count, count), 0)
        <= lax.broadcasted_iota(jnp.int32, (count, count), 1)
    ).astype(BF16)


def placing(ids, groups, me, before):
    rows, count = max(groups, 8), ids.shape[1]
    row = lax.broadcasted_iota(jnp.int32, (rows, count), 0)
    hit = named(ids, jnp.where(row < groups, (row ^ me) * GROUP_EXPERTS, -1))
    rank = jnp.dot(hit.astype(BF16), before, preferred_element_type=F32)
    slot = lax.broadcasted_iota(jnp.int32, (CAP, count), 0).astype(F32) + 1.0
    seat = jnp.where(hit > 0.5, rank, 0.0)
    place = [jnp.where(seat[d : d + 1, :] == slot, 1.0, 0.0) for d in range(groups)]
    return jnp.concatenate(place, axis=0), rank[:, count - 1 :]


def dispatch_kernel(groups, width, ids_ref, tokens_ref, *refs):
    outs, (ids_held, staged, before_ref, sems) = refs[:groups], refs[groups:]
    me = lax.axis_index("grp")
    features = tokens_ref.shape[1]
    first = pltpu.make_async_copy(ids_ref, ids_held, sems.at[features // width])
    first.start()
    copies = []
    for c in range(features // width):
        part = pl.ds(c * width, width)
        copies.append(pltpu.make_async_copy(tokens_ref.at[:, part], staged.at[:, part], sems.at[c]))
        copies[-1].start()
    before_ref[...] = upto(tokens_ref.shape[0])
    first.wait()
    place, counts = placing(ids_held[...], groups, me, before_ref[...])
    place = place.astype(BF16)
    slot = lax.broadcasted_iota(jnp.int32, (CAP, LANES), 0).astype(F32)
    for d in range(groups):
        live = slot < jnp.broadcast_to(counts[d : d + 1, :], (CAP, LANES))
        outs[d][:, features:] = jnp.where(live, 1.0, 0.0).astype(BF16)
    for c in range(features // width):
        copies[c].wait()
        part = slice(c * width, (c + 1) * width)
        rows = jnp.dot(place, staged[:, part], preferred_element_type=F32)
        for d in range(groups):
            outs[d][:, part] = rows[d * CAP : (d + 1) * CAP].astype(BF16)


def start_loads(weights, loaded, sems):
    copies = []
    for k in range(len(weights)):
        depth = weights[k].shape[0]
        for c in range(4):
            part = pl.ds(c * (depth // 4), depth // 4)
            copies.append(pltpu.make_async_copy(weights[k].at[part], loaded[k].at[part], sems.at[4 * k + c]))
            copies[-1].start()
    return copies


def load_kernel(after_ref, gate_ref, up_ref, gate_out, up_out, sems):
    del after_ref
    for copy in start_loads([gate_ref, up_ref], [gate_out, up_out], sems):
        copy.wait()


def prepare_kernel(groups, after_ref, ids_ref, logits_ref, down_ref, down_out, out_ref, ids_held, logits_held, sems):
    del after_ref
    small = [
        pltpu.make_async_copy(ids_ref, ids_held, sems.at[4]),
        pltpu.make_async_copy(logits_ref, logits_held, sems.at[5]),
    ]
    for copy in small:
        copy.start()
    copies = start_loads([down_ref], [down_out], sems)
    for copy in small:
        copy.wait()
    me = lax.axis_index("grp")
    ids = ids_held[...]
    place, _ = placing(ids, groups, me, upto(ids.shape[1]))
    group = (lax.broadcasted_iota(jnp.int32, place.shape, 0) // CAP) ^ me
    scores = 1.0 / (1.0 + jnp.exp(-logits_held[...]))
    expert = lax.broadcasted_iota(jnp.int32, scores.shape, 0)
    chosen = jnp.sum(jnp.where(named(ids, expert) > 0.5, scores, 0.0), axis=0, keepdims=True)
    leading = jnp.zeros(place.shape, F32)
    for g in range(groups):
        leading = jnp.where(group == g, scores[g * GROUP_EXPERTS : g * GROUP_EXPERTS + 1, :], leading)
    weight = (ROUTE_SCALE * leading / chosen).astype(BF16).astype(F32)
    out_ref[...] = jnp.where(place > 0.5, weight, 0.0).T.astype(BF16)
    for copy in copies:
        copy.wait()


def compact_kernel(groups, slots, parts, after_ref, *refs):
    del after_ref
    arrived, outs, pick_ref = refs[:groups][::-1], refs[groups:-1], refs[-1]
    rows = groups * CAP
    features = arrived[0].shape[1] - LANES
    live = jnp.concatenate([a[:, features:].astype(F32) for a in arrived], axis=0)
    row = lax.broadcasted_iota(jnp.int32, (rows, rows), 0)
    column = lax.broadcasted_iota(jnp.int32, (rows, rows), 1)
    rank = jnp.dot((column <= row).astype(BF16), live.astype(BF16), preferred_element_type=F32)
    lane = lax.broadcasted_iota(jnp.int32, (rows, LANES), 1).astype(F32)
    pick = jnp.where((live > 0.5) & (rank == lane + 1.0), 1.0, 0.0).astype(BF16)
    pick_ref[...] = pick
    step = 256
    for c in range(features // step):
        at = slice(c * step, (c + 1) * step)
        whole = jnp.concatenate([a[:, at].astype(F32) for a in arrived], axis=0).astype(BF16)
        moved = lax.dot_general(pick[:, :slots], whole, (((0,), (0,)), ((), ())), preferred_element_type=F32)
        for (first, last), out in zip(parts, outs):
            if first <= c * step < last:
                out[:, c * step - first : (c + 1) * step - first] = moved.astype(BF16)


def ahead_kernel(first, order, *refs):
    blocks, (gate_ref, up_ref, gate_sum, up_sum) = [refs[k] for k in order], refs[len(order) :]
    rows = jnp.concatenate([block[...] for block in blocks], axis=0)
    step = min(256, gate_ref.shape[1])
    for c in range(gate_ref.shape[1] // step):
        part = slice(c * step, (c + 1) * step)
        gate_sum[:, part] = jnp.dot(rows, gate_ref[first:, part], preferred_element_type=F32)
        up_sum[:, part] = jnp.dot(rows, up_ref[first:, part], preferred_element_type=F32)


def hidden_kernel(last, count, *refs):
    blocks, sums, (gate_ref, up_ref, hidden_ref) = refs[:count], refs[count:-3], refs[-3:]
    units = gate_ref.shape[1]
    rows = jnp.concatenate([block[...] for block in blocks], axis=0)
    step = min(256, units)
    for c in range(units // step):
        part = slice(c * step, (c + 1) * step)
        gate = jnp.dot(rows, gate_ref[:last, part], preferred_element_type=F32)
        up = jnp.dot(rows, up_ref[:last, part], preferred_element_type=F32)
        if sums:
            gate, up = gate + sums[0][:, part], up + sums[1][:, part]
        hidden_ref[:, part] = (gate / (1.0 + jnp.exp(-gate)) * up).astype(BF16)


def down_sum(columns, which, hiddens, down_ref):
    me = lax.axis_index("ing")
    rows, units = hiddens[0].shape
    slots = rows // columns
    total = jnp.zeros((rows, down_ref.shape[1]), F32)
    for f, hidden in zip(which, hiddens):
        block = jnp.concatenate(
            [hidden[slots * (e ^ f) : slots * ((e ^ f) + 1), :] for e in range(columns)], axis=0
        )
        at = pl.multiple_of((me ^ f) * units, units)
        total += jnp.dot(block, down_ref[pl.ds(at, units), :], preferred_element_type=F32)
    return total


def begin_kernel(columns, which, *refs):
    refs[-1][...] = down_sum(columns, which, refs[:-2], refs[-2])


def down_kernel(columns, which, *refs):
    count = len(which)
    hiddens, (sum_ref, down_ref), outs = refs[:count], refs[count : count + 2], refs[count + 2 :]
    total = sum_ref[...] + down_sum(columns, which, hiddens, down_ref)
    slots = total.shape[0] // columns
    for e in range(columns):
        outs[e][...] = total[e * slots : (e + 1) * slots].astype(BF16)


def spread_kernel(groups, columns, pick_ref, *refs):
    blocks, outs = refs[:columns][::-1], refs[columns:]
    for e in range(columns):
        block = blocks[e][...]
        back = jnp.dot(pick_ref[:, : block.shape[0]], block, preferred_element_type=F32)
        for d in range(groups):
            outs[d][e] = back[d * CAP : (d + 1) * CAP].astype(BF16)


def combine_kernel(groups, columns, mixing_ref, *refs):
    backs, (out_ref, held, sems) = refs[:groups][::-1], refs[groups:]
    me = lax.axis_index("ing")
    width, half = backs[0].shape[2], held.shape[0] // 2
    copies = []
    for e in range(columns):
        rows = jnp.concatenate([backs[d][e].astype(F32) for d in range(groups)], axis=0)
        rows = rows.astype(BF16)
        part = pl.ds(e * width, width)
        there = pl.ds(pl.multiple_of((me ^ e) * width, width), width)
        for h in range(2):
            mine = pl.ds(h * half, half)
            value = jnp.dot(mixing_ref[mine, :], rows, preferred_element_type=F32)
            held[mine, part] = value.astype(BF16)
            copies.append(
                pltpu.make_async_copy(held.at[mine, part], out_ref.at[mine, there], sems.at[2 * e + h])
            )
            copies[-1].start()
    for copy in copies:
        copy.wait()


def swap(x, name, step):
    if step == 0:
        return x
    return lax.ppermute(x, name, [(a, a ^ step) for a in range(lax.axis_size(name))])


def swap_all(parts, name):
    return [swap(part, name, k) for k, part in enumerate(parts)][::-1]


def local(tokens, router_logits, expert_ids, w_gate, w_up, w_down):
    groups = lax.axis_size("grp")
    columns = lax.axis_size("ing")
    count, features = tokens.shape
    units, share = w_gate.shape[2], w_down.shape[2]
    slots = groups * CAP // 2
    wide = features + LANES
    ids = pltpu.with_memory_space_constraint(expert_ids.T, pltpu.HBM)
    logits = pltpu.with_memory_space_constraint(router_logits.T, pltpu.HBM)

    outbound = pl.pallas_call(
        functools.partial(dispatch_kernel, groups, features // 2),
        out_shape=[jax.ShapeDtypeStruct((CAP, wide), BF16)] * groups,
        in_specs=[ANY, ANY],
        out_specs=[VMEM] * groups,
        scratch_shapes=[
            pltpu.VMEM(ids.shape, jnp.int32),
            pltpu.VMEM((count, features), BF16),
            pltpu.VMEM((count, count), BF16),
            pltpu.SemaphoreType.DMA((3,)),
        ],
        compiler_params=params(2 * count * features),
        name="dispatch",
    )(ids, pltpu.with_memory_space_constraint(tokens, pltpu.HBM))
    arrived = swap_all(outbound, "grp")

    weights = [w_gate[0], w_up[0], w_down[0]]
    weights = [pltpu.with_memory_space_constraint(w, pltpu.HBM) for w in weights]
    gate, up = pl.pallas_call(
        load_kernel,
        out_shape=[pltpu.VMEM(w.shape, BF16) for w in weights[:2]],
        in_specs=[ANY] * 3,
        out_specs=[VMEM] * 2,
        scratch_shapes=[pltpu.SemaphoreType.DMA((8,))],
        compiler_params=params(0),
        name="load",
    )(outbound[0], *weights[:2])

    cut = features // 2
    parts = [(0, cut), (cut, features)] if columns == 4 else [(0, features)]
    *own, pick = pl.pallas_call(
        functools.partial(compact_kernel, groups, slots, parts),
        out_shape=[jax.ShapeDtypeStruct((slots, last - first), BF16) for first, last in parts]
        + [jax.ShapeDtypeStruct((groups * CAP, LANES), BF16)],
        in_specs=[ANY] + [VMEM] * groups,
        out_specs=[VMEM] * (len(parts) + 1),
        compiler_params=params(2 * (groups * CAP + 2 * slots) * wide),
        name="compact",
    )(gate, *arrived)
    if columns == 4:
        near_low, near_high, high, far_high = [swap(part, "ing", e) for part, e in zip(own + own[1:] * 2, (1, 1, 2, 3))]
        low = swap(own[0], "ing", 2)
        far_low = swap(low, "ing", 1)
        sums = pl.pallas_call(
            functools.partial(ahead_kernel, cut, (0, 1, 3, 2)),
            out_shape=[jax.ShapeDtypeStruct((columns * slots, units), F32)] * 2,
            in_specs=[VMEM] * (columns + 2),
            out_specs=[VMEM] * 2,
            compiler_params=params(2 * columns * slots * (features + 4 * units)),
            name="ahead",
        )(own[1], near_high, far_high, high, gate, up)
        blocks = [own[0], near_low, low, far_low]
    else:
        sums, cut = [], features
        blocks = [swap(own[0], "ing", e) for e in range(columns)]

    hidden = pl.pallas_call(
        functools.partial(hidden_kernel, cut, columns),
        out_shape=jax.ShapeDtypeStruct((columns * slots, units), BF16),
        in_specs=[VMEM] * (columns + len(sums) + 2),
        out_specs=VMEM,
        compiler_params=params(2 * columns * slots * (2 * features + 5 * units)),
        name="hidden",
    )(*blocks, *sums, gate, up)
    down, mixing = pl.pallas_call(
        functools.partial(prepare_kernel, groups),
        out_shape=[
            pltpu.VMEM(w_down.shape[1:], BF16),
            jax.ShapeDtypeStruct((count, groups * CAP), BF16),
        ],
        in_specs=[ANY] * 4,
        out_specs=[VMEM] * 2,
        scratch_shapes=[
            pltpu.VMEM(ids.shape, jnp.int32),
            pltpu.VMEM(logits.shape, F32),
            pltpu.SemaphoreType.DMA((6,)),
        ],
        compiler_params=params(0),
        name="prepare",
    )(hidden, ids, logits, weights[2])
    hiddens = [swap(hidden, "ing", f) for f in range(columns)]

    early, late = (0, columns - 1), tuple(range(1, columns - 1))
    begun = pl.pallas_call(
        functools.partial(begin_kernel, columns, early),
        out_shape=jax.ShapeDtypeStruct((columns * slots, share), F32),
        in_specs=[VMEM] * (len(early) + 1),
        out_specs=VMEM,
        compiler_params=params(2 * columns * slots * (2 * units + 4 * share)),
        name="begin",
    )(*[hiddens[f] for f in early], down)
    results = pl.pallas_call(
        functools.partial(down_kernel, columns, late),
        out_shape=[jax.ShapeDtypeStruct((slots, share), BF16)] * columns,
        in_specs=[VMEM] * (len(late) + 2),
        out_specs=[VMEM] * columns,
        compiler_params=params(2 * columns * slots * (columns * units + 6 * share)),
        name="down",
    )(*[hiddens[f] for f in late], begun, down)
    results = swap_all(results, "ing")

    backs = pl.pallas_call(
        functools.partial(spread_kernel, groups, columns),
        out_shape=[jax.ShapeDtypeStruct((columns, CAP, share), BF16)] * groups,
        in_specs=[VMEM] * (columns + 1),
        out_specs=[VMEM] * groups,
        compiler_params=params(2 * (groups * CAP + slots) * features),
        name="spread",
    )(pick, *results)
    backs = swap_all(backs, "grp")

    if share % LANES:
        me = lax.axis_index("ing")
        rows = jnp.stack(backs[::-1])[:, jnp.arange(columns) ^ me]
        rows = rows.transpose(0, 2, 1, 3).reshape(groups * CAP, features)
        return jnp.dot(mixing, rows, preferred_element_type=F32).astype(BF16)
    return pl.pallas_call(
        functools.partial(combine_kernel, groups, columns),
        out_shape=jax.ShapeDtypeStruct((count, features), BF16),
        in_specs=[VMEM] * (1 + groups),
        out_specs=ANY,
        scratch_shapes=[pltpu.VMEM((count, features), BF16), pltpu.SemaphoreType.DMA((2 * columns,))],
        compiler_params=params(2 * (count + groups * CAP) * features),
        name="combine",
    )(mixing, *backs)


def solution(mesh):
    placed = (
        P(("rep", "grp", "ing"), None),
        P(("rep", "grp", "ing"), None),
        P(("rep", "grp", "ing"), None),
        P("grp", None, "ing"),
        P("grp", None, "ing"),
        P("grp", None, "ing"),
    )
    return jax.shard_map(
        local, mesh=mesh, in_specs=placed, out_specs=P(("rep", "grp", "ing"), None), check_vma=False
    )
```

```python
import functools

import jax
import jax.numpy as jnp
from jax import lax
from jax.experimental import pallas as pl
from jax.experimental.pallas import tpu as pltpu
from jax.sharding import PartitionSpec as P

GROUP_EXPERTS = 24
CAP = 8
LANES = 128
ROUTE_SCALE = 2.827
MIB = 1024 * 1024

BF16 = jnp.bfloat16
F32 = jnp.float32
VMEM = pl.BlockSpec(memory_space=pltpu.VMEM)
ANY = pl.BlockSpec(memory_space=pl.ANY)


def params(nbytes):
    return pltpu.CompilerParams(vmem_limit_bytes=2 * nbytes + 4 * MIB)


def named(ids, expert):
    hit = jnp.zeros(expert.shape, F32)
    for k in range(ids.shape[0]):
        hit = jnp.where(ids[k : k + 1, :] == expert, 1.0, hit)
    return hit


def upto(count):
    return (
        lax.broadcasted_iota(jnp.int32, (count, count), 0)
        <= lax.broadcasted_iota(jnp.int32, (count, count), 1)
    ).astype(BF16)


def placing(ids, groups, me, before):
    rows, count = max(groups, 8), ids.shape[1]
    row = lax.broadcasted_iota(jnp.int32, (rows, count), 0)
    hit = named(ids, jnp.where(row < groups, (row ^ me) * GROUP_EXPERTS, -1))
    rank = jnp.dot(hit.astype(BF16), before, preferred_element_type=F32)
    slot = lax.broadcasted_iota(jnp.int32, (CAP, count), 0).astype(F32) + 1.0
    seat = jnp.where(hit > 0.5, rank, 0.0)
    place = [jnp.where(seat[d : d + 1, :] == slot, 1.0, 0.0) for d in range(groups)]
    return jnp.concatenate(place, axis=0), rank[:, count - 1 :]


def dispatch_kernel(groups, width, ids_ref, tokens_ref, *refs):
    outs, (ids_held, staged, before_ref, sems) = refs[:groups], refs[groups:]
    me = lax.axis_index("grp")
    features = tokens_ref.shape[1]
    first = pltpu.make_async_copy(ids_ref, ids_held, sems.at[4 * (features // width)])
    first.start()
    quarter = tokens_ref.shape[0] // 4
    copies = []
    for c in range(features // width):
        for q in range(4):
            part = pl.ds(q * quarter, quarter), pl.ds(c * width, width)
            copies.append(pltpu.make_async_copy(tokens_ref.at[part], staged.at[part], sems.at[4 * c + q]))
            copies[-1].start()
    before_ref[...] = upto(tokens_ref.shape[0])
    first.wait()
    place, counts = placing(ids_held[...], groups, me, before_ref[...])
    place = place.astype(BF16)
    slot = lax.broadcasted_iota(jnp.int32, (CAP, LANES), 0).astype(F32)
    for d in range(groups):
        live = slot < jnp.broadcast_to(counts[d : d + 1, :], (CAP, LANES))
        outs[d][:, features:] = jnp.where(live, 1.0, 0.0).astype(BF16)
    for c in range(features // width):
        for q in range(4):
            copies[4 * c + q].wait()
        part = slice(c * width, (c + 1) * width)
        rows = jnp.dot(place, staged[:, part], preferred_element_type=F32)
        for d in range(groups):
            outs[d][:, part] = rows[d * CAP : (d + 1) * CAP].astype(BF16)


def start_loads(weights, loaded, sems):
    copies = []
    for k in range(len(weights)):
        depth = weights[k].shape[0]
        for c in range(4):
            part = pl.ds(c * (depth // 4), depth // 4)
            copies.append(pltpu.make_async_copy(weights[k].at[part], loaded[k].at[part], sems.at[4 * k + c]))
            copies[-1].start()
    return copies


def load_kernel(after_ref, gate_ref, up_ref, gate_out, up_out, sems):
    del after_ref
    for copy in start_loads([gate_ref, up_ref], [gate_out, up_out], sems):
        copy.wait()


def prepare_kernel(groups, after_ref, ids_ref, logits_ref, down_ref, down_out, out_ref, ids_held, logits_held, sems):
    del after_ref
    small = [
        pltpu.make_async_copy(ids_ref, ids_held, sems.at[4]),
        pltpu.make_async_copy(logits_ref, logits_held, sems.at[5]),
    ]
    for copy in small:
        copy.start()
    copies = start_loads([down_ref], [down_out], sems)
    for copy in small:
        copy.wait()
    me = lax.axis_index("grp")
    ids = ids_held[...]
    place, _ = placing(ids, groups, me, upto(ids.shape[1]))
    group = (lax.broadcasted_iota(jnp.int32, place.shape, 0) // CAP) ^ me
    scores = 1.0 / (1.0 + jnp.exp(-logits_held[...]))
    expert = lax.broadcasted_iota(jnp.int32, scores.shape, 0)
    chosen = jnp.sum(jnp.where(named(ids, expert) > 0.5, scores, 0.0), axis=0, keepdims=True)
    leading = jnp.zeros(place.shape, F32)
    for g in range(groups):
        leading = jnp.where(group == g, scores[g * GROUP_EXPERTS : g * GROUP_EXPERTS + 1, :], leading)
    weight = (ROUTE_SCALE * leading / chosen).astype(BF16).astype(F32)
    out_ref[...] = jnp.where(place > 0.5, weight, 0.0).T.astype(BF16)
    for copy in copies:
        copy.wait()


def compact_kernel(groups, slots, parts, after_ref, *refs):
    del after_ref
    arrived, outs, pick_ref = refs[:groups][::-1], refs[groups:-1], refs[-1]
    rows = groups * CAP
    features = arrived[0].shape[1] - LANES
    live = jnp.concatenate([a[:, features:].astype(F32) for a in arrived], axis=0)
    row = lax.broadcasted_iota(jnp.int32, (rows, rows), 0)
    column = lax.broadcasted_iota(jnp.int32, (rows, rows), 1)
    rank = jnp.dot((column <= row).astype(BF16), live.astype(BF16), preferred_element_type=F32)
    lane = lax.broadcasted_iota(jnp.int32, (rows, LANES), 1).astype(F32)
    pick = jnp.where((live > 0.5) & (rank == lane + 1.0), 1.0, 0.0).astype(BF16)
    pick_ref[...] = pick
    step = 256
    for c in range(features // step):
        at = slice(c * step, (c + 1) * step)
        whole = jnp.concatenate([a[:, at].astype(F32) for a in arrived], axis=0).astype(BF16)
        moved = lax.dot_general(pick[:, :slots], whole, (((0,), (0,)), ((), ())), preferred_element_type=F32)
        for (first, last), out in zip(parts, outs):
            if first <= c * step < last:
                out[:, c * step - first : (c + 1) * step - first] = moved.astype(BF16)


def ahead_kernel(first, order, *refs):
    blocks, (gate_ref, up_ref, gate_sum, up_sum) = [refs[k] for k in order], refs[len(order) :]
    rows = jnp.concatenate([block[...] for block in blocks], axis=0)
    step = min(256, gate_ref.shape[1])
    for c in range(gate_ref.shape[1] // step):
        part = slice(c * step, (c + 1) * step)
        gate_sum[:, part] = jnp.dot(rows, gate_ref[first:, part], preferred_element_type=F32)
        up_sum[:, part] = jnp.dot(rows, up_ref[first:, part], preferred_element_type=F32)


def hidden_kernel(last, count, *refs):
    blocks, sums, (gate_ref, up_ref, hidden_ref) = refs[:count], refs[count:-3], refs[-3:]
    units = gate_ref.shape[1]
    rows = jnp.concatenate([block[...] for block in blocks], axis=0)
    step = min(256, units)
    for c in range(units // step):
        part = slice(c * step, (c + 1) * step)
        gate = jnp.dot(rows, gate_ref[:last, part], preferred_element_type=F32)
        up = jnp.dot(rows, up_ref[:last, part], preferred_element_type=F32)
        if sums:
            gate, up = gate + sums[0][:, part], up + sums[1][:, part]
        hidden_ref[:, part] = (gate / (1.0 + jnp.exp(-gate)) * up).astype(BF16)


def down_sum(columns, which, hiddens, down_ref):
    me = lax.axis_index("ing")
    rows, units = hiddens[0].shape
    slots = rows // columns
    total = jnp.zeros((rows, down_ref.shape[1]), F32)
    for f, hidden in zip(which, hiddens):
        block = jnp.concatenate(
            [hidden[slots * (e ^ f) : slots * ((e ^ f) + 1), :] for e in range(columns)], axis=0
        )
        at = pl.multiple_of((me ^ f) * units, units)
        total += jnp.dot(block, down_ref[pl.ds(at, units), :], preferred_element_type=F32)
    return total


def begin_kernel(columns, which, *refs):
    refs[-1][...] = down_sum(columns, which, refs[:-2], refs[-2])


def down_kernel(columns, which, *refs):
    count = len(which)
    hiddens, (sum_ref, down_ref), outs = refs[:count], refs[count : count + 2], refs[count + 2 :]
    total = sum_ref[...] + down_sum(columns, which, hiddens, down_ref)
    slots = total.shape[0] // columns
    for e in range(columns):
        outs[e][...] = total[e * slots : (e + 1) * slots].astype(BF16)


def spread_kernel(groups, columns, pick_ref, *refs):
    blocks, outs = refs[:columns][::-1], refs[columns:]
    for e in range(columns):
        block = blocks[e][...]
        back = jnp.dot(pick_ref[:, : block.shape[0]], block, preferred_element_type=F32)
        for d in range(groups):
            outs[d][e] = back[d * CAP : (d + 1) * CAP].astype(BF16)


def combine_kernel(groups, columns, mixing_ref, *refs):
    backs, (out_ref, held, sems) = refs[:groups][::-1], refs[groups:]
    me = lax.axis_index("ing")
    width, half = backs[0].shape[2], held.shape[0] // 2
    copies = []
    for e in range(columns):
        rows = jnp.concatenate([backs[d][e].astype(F32) for d in range(groups)], axis=0)
        rows = rows.astype(BF16)
        part = pl.ds(e * width, width)
        there = pl.ds(pl.multiple_of((me ^ e) * width, width), width)
        for h in range(2):
            mine = pl.ds(h * half, half)
            value = jnp.dot(mixing_ref[mine, :], rows, preferred_element_type=F32)
            held[mine, part] = value.astype(BF16)
            copies.append(
                pltpu.make_async_copy(held.at[mine, part], out_ref.at[mine, there], sems.at[2 * e + h])
            )
            copies[-1].start()
    for copy in copies:
        copy.wait()


def swap(x, name, step):
    if step == 0:
        return x
    return lax.ppermute(x, name, [(a, a ^ step) for a in range(lax.axis_size(name))])


def swap_all(parts, name):
    return [swap(part, name, k) for k, part in enumerate(parts)][::-1]


def local(tokens, router_logits, expert_ids, w_gate, w_up, w_down):
    groups = lax.axis_size("grp")
    columns = lax.axis_size("ing")
    count, features = tokens.shape
    units, share = w_gate.shape[2], w_down.shape[2]
    slots = groups * CAP // 2
    wide = features + LANES
    ids = pltpu.with_memory_space_constraint(expert_ids.T, pltpu.HBM)
    logits = pltpu.with_memory_space_constraint(router_logits.T, pltpu.HBM)

    outbound = pl.pallas_call(
        functools.partial(dispatch_kernel, groups, features // 2),
        out_shape=[jax.ShapeDtypeStruct((CAP, wide), BF16)] * groups,
        in_specs=[ANY, ANY],
        out_specs=[VMEM] * groups,
        scratch_shapes=[
            pltpu.VMEM(ids.shape, jnp.int32),
            pltpu.VMEM((count, features), BF16),
            pltpu.VMEM((count, count), BF16),
            pltpu.SemaphoreType.DMA((9,)),
        ],
        compiler_params=params(2 * count * features),
        name="dispatch",
    )(ids, pltpu.with_memory_space_constraint(tokens, pltpu.HBM))
    arrived = swap_all(outbound, "grp")

    weights = [w_gate[0], w_up[0], w_down[0]]
    weights = [pltpu.with_memory_space_constraint(w, pltpu.HBM) for w in weights]
    gate, up = pl.pallas_call(
        load_kernel,
        out_shape=[pltpu.VMEM(w.shape, BF16) for w in weights[:2]],
        in_specs=[ANY] * 3,
        out_specs=[VMEM] * 2,
        scratch_shapes=[pltpu.SemaphoreType.DMA((8,))],
        compiler_params=params(0),
        name="load",
    )(outbound[0], *weights[:2])

    cut = features // 2
    parts = [(0, cut), (cut, features)] if columns == 4 else [(0, features)]
    *own, pick = pl.pallas_call(
        functools.partial(compact_kernel, groups, slots, parts),
        out_shape=[jax.ShapeDtypeStruct((slots, last - first), BF16) for first, last in parts]
        + [jax.ShapeDtypeStruct((groups * CAP, LANES), BF16)],
        in_specs=[ANY] + [VMEM] * groups,
        out_specs=[VMEM] * (len(parts) + 1),
        compiler_params=params(2 * (groups * CAP + 2 * slots) * wide),
        name="compact",
    )(gate, *arrived)
    if columns == 4:
        near_low, near_high, high, far_high = [swap(part, "ing", e) for part, e in zip(own + own[1:] * 2, (1, 1, 2, 3))]
        low = swap(own[0], "ing", 2)
        far_low = swap(low, "ing", 1)
        sums = pl.pallas_call(
            functools.partial(ahead_kernel, cut, (0, 1, 3, 2)),
            out_shape=[jax.ShapeDtypeStruct((columns * slots, units), F32)] * 2,
            in_specs=[VMEM] * (columns + 2),
            out_specs=[VMEM] * 2,
            compiler_params=params(2 * columns * slots * (features + 4 * units)),
            name="ahead",
        )(own[1], near_high, far_high, high, gate, up)
        blocks = [own[0], near_low, low, far_low]
    else:
        sums, cut = [], features
        blocks = [swap(own[0], "ing", e) for e in range(columns)]

    hidden = pl.pallas_call(
        functools.partial(hidden_kernel, cut, columns),
        out_shape=jax.ShapeDtypeStruct((columns * slots, units), BF16),
        in_specs=[VMEM] * (columns + len(sums) + 2),
        out_specs=VMEM,
        compiler_params=params(2 * columns * slots * (2 * features + 5 * units)),
        name="hidden",
    )(*blocks, *sums, gate, up)
    down, mixing = pl.pallas_call(
        functools.partial(prepare_kernel, groups),
        out_shape=[
            pltpu.VMEM(w_down.shape[1:], BF16),
            jax.ShapeDtypeStruct((count, groups * CAP), BF16),
        ],
        in_specs=[ANY] * 4,
        out_specs=[VMEM] * 2,
        scratch_shapes=[
            pltpu.VMEM(ids.shape, jnp.int32),
            pltpu.VMEM(logits.shape, F32),
            pltpu.SemaphoreType.DMA((6,)),
        ],
        compiler_params=params(0),
        name="prepare",
    )(hidden, ids, logits, weights[2])
    hiddens = [swap(hidden, "ing", f) for f in range(columns)]

    early, late = (0, columns - 1), tuple(range(1, columns - 1))
    begun = pl.pallas_call(
        functools.partial(begin_kernel, columns, early),
        out_shape=jax.ShapeDtypeStruct((columns * slots, share), F32),
        in_specs=[VMEM] * (len(early) + 1),
        out_specs=VMEM,
        compiler_params=params(2 * columns * slots * (2 * units + 4 * share)),
        name="begin",
    )(*[hiddens[f] for f in early], down)
    results = pl.pallas_call(
        functools.partial(down_kernel, columns, late),
        out_shape=[jax.ShapeDtypeStruct((slots, share), BF16)] * columns,
        in_specs=[VMEM] * (len(late) + 2),
        out_specs=[VMEM] * columns,
        compiler_params=params(2 * columns * slots * (columns * units + 6 * share)),
        name="down",
    )(*[hiddens[f] for f in late], begun, down)
    results = swap_all(results, "ing")

    backs = pl.pallas_call(
        functools.partial(spread_kernel, groups, columns),
        out_shape=[jax.ShapeDtypeStruct((columns, CAP, share), BF16)] * groups,
        in_specs=[VMEM] * (columns + 1),
        out_specs=[VMEM] * groups,
        compiler_params=params(2 * (groups * CAP + slots) * features),
        name="spread",
    )(pick, *results)
    backs = swap_all(backs, "grp")

    if share % LANES:
        me = lax.axis_index("ing")
        rows = jnp.stack(backs[::-1])[:, jnp.arange(columns) ^ me]
        rows = rows.transpose(0, 2, 1, 3).reshape(groups * CAP, features)
        return jnp.dot(mixing, rows, preferred_element_type=F32).astype(BF16)
    return pl.pallas_call(
        functools.partial(combine_kernel, groups, columns),
        out_shape=jax.ShapeDtypeStruct((count, features), BF16),
        in_specs=[VMEM] * (1 + groups),
        out_specs=ANY,
        scratch_shapes=[pltpu.VMEM((count, features), BF16), pltpu.SemaphoreType.DMA((2 * columns,))],
        compiler_params=params(2 * (count + groups * CAP) * features),
        name="combine",
    )(mixing, *backs)


def solution(mesh):
    placed = (
        P(("rep", "grp", "ing"), None),
        P(("rep", "grp", "ing"), None),
        P(("rep", "grp", "ing"), None),
        P("grp", None, "ing"),
        P("grp", None, "ing"),
        P("grp", None, "ing"),
    )
    return jax.shard_map(
        local, mesh=mesh, in_specs=placed, out_specs=P(("rep", "grp", "ing"), None), check_vma=False
    )
```

```python
import functools

import jax
import jax.numpy as jnp
from jax import lax
from jax.experimental import pallas as pl
from jax.experimental.pallas import tpu as pltpu
from jax.sharding import PartitionSpec as P

GROUP_EXPERTS = 24
CAP = 8
LANES = 128
ROUTE_SCALE = 2.827
MIB = 1024 * 1024

BF16 = jnp.bfloat16
F32 = jnp.float32
VMEM = pl.BlockSpec(memory_space=pltpu.VMEM)
ANY = pl.BlockSpec(memory_space=pl.ANY)


def params(nbytes):
    return pltpu.CompilerParams(vmem_limit_bytes=2 * nbytes + 4 * MIB)


def named(ids, expert):
    hit = jnp.zeros(expert.shape, F32)
    for k in range(ids.shape[0]):
        hit = jnp.where(ids[k : k + 1, :] == expert, 1.0, hit)
    return hit


def upto(count):
    return (
        lax.broadcasted_iota(jnp.int32, (count, count), 0)
        <= lax.broadcasted_iota(jnp.int32, (count, count), 1)
    ).astype(BF16)


def placing(ids, groups, me, before):
    rows, count = max(groups, 8), ids.shape[1]
    row = lax.broadcasted_iota(jnp.int32, (rows, count), 0)
    hit = named(ids, jnp.where(row < groups, (row ^ me) * GROUP_EXPERTS, -1))
    rank = jnp.dot(hit.astype(BF16), before, preferred_element_type=F32)
    slot = lax.broadcasted_iota(jnp.int32, (CAP, count), 0).astype(F32) + 1.0
    seat = jnp.where(hit > 0.5, rank, 0.0)
    place = [jnp.where(seat[d : d + 1, :] == slot, 1.0, 0.0) for d in range(groups)]
    return jnp.concatenate(place, axis=0), rank[:, count - 1 :]


def dispatch_kernel(groups, width, ids_ref, tokens_ref, *refs):
    outs, (ids_held, staged, before_ref, sems) = refs[:groups], refs[groups:]
    me = lax.axis_index("grp")
    features = tokens_ref.shape[1]
    first = pltpu.make_async_copy(ids_ref, ids_held, sems.at[features // width])
    first.start()
    copies = []
    for c in range(features // width):
        part = pl.ds(c * width, width)
        copies.append(pltpu.make_async_copy(tokens_ref.at[:, part], staged.at[:, part], sems.at[c]))
        copies[-1].start()
    before_ref[...] = upto(tokens_ref.shape[0])
    first.wait()
    place, counts = placing(ids_held[...], groups, me, before_ref[...])
    place = place.astype(BF16)
    slot = lax.broadcasted_iota(jnp.int32, (CAP, LANES), 0).astype(F32)
    for d in range(groups):
        live = slot < jnp.broadcast_to(counts[d : d + 1, :], (CAP, LANES))
        outs[d][:, features:] = jnp.where(live, 1.0, 0.0).astype(BF16)
    for c in range(features // width):
        copies[c].wait()
        part = slice(c * width, (c + 1) * width)
        rows = jnp.dot(place, staged[:, part], preferred_element_type=F32)
        for d in range(groups):
            outs[d][:, part] = rows[d * CAP : (d + 1) * CAP].astype(BF16)


def start_loads(weights, loaded, sems):
    copies = []
    for k in range(len(weights)):
        depth = weights[k].shape[0]
        for c in range(4):
            part = pl.ds(c * (depth // 4), depth // 4)
            copies.append(pltpu.make_async_copy(weights[k].at[part], loaded[k].at[part], sems.at[4 * k + c]))
            copies[-1].start()
    return copies


def load_kernel(after_ref, gate_ref, up_ref, gate_out, up_out, sems):
    del after_ref
    for copy in start_loads([gate_ref, up_ref], [gate_out, up_out], sems):
        copy.wait()


def prepare_kernel(groups, after_ref, ids_ref, logits_ref, down_ref, down_out, out_ref, ids_held, logits_held, sems):
    del after_ref
    small = [
        pltpu.make_async_copy(ids_ref, ids_held, sems.at[4]),
        pltpu.make_async_copy(logits_ref, logits_held, sems.at[5]),
    ]
    for copy in small:
        copy.start()
    copies = start_loads([down_ref], [down_out], sems)
    for copy in small:
        copy.wait()
    me = lax.axis_index("grp")
    ids = ids_held[...]
    place, _ = placing(ids, groups, me, upto(ids.shape[1]))
    group = (lax.broadcasted_iota(jnp.int32, place.shape, 0) // CAP) ^ me
    scores = 1.0 / (1.0 + jnp.exp(-logits_held[...]))
    expert = lax.broadcasted_iota(jnp.int32, scores.shape, 0)
    chosen = jnp.sum(jnp.where(named(ids, expert) > 0.5, scores, 0.0), axis=0, keepdims=True)
    leading = jnp.zeros(place.shape, F32)
    for g in range(groups):
        leading = jnp.where(group == g, scores[g * GROUP_EXPERTS : g * GROUP_EXPERTS + 1, :], leading)
    weight = (ROUTE_SCALE * leading / chosen).astype(BF16).astype(F32)
    out_ref[...] = jnp.where(place > 0.5, weight, 0.0).T.astype(BF16)
    for copy in copies:
        copy.wait()


def compact_kernel(groups, slots, parts, after_ref, *refs):
    del after_ref
    arrived, outs, pick_ref = refs[:groups][::-1], refs[groups:-1], refs[-1]
    rows = groups * CAP
    features = arrived[0].shape[1] - LANES
    live = jnp.concatenate([a[:, features:].astype(F32) for a in arrived], axis=0)
    row = lax.broadcasted_iota(jnp.int32, (rows, rows), 0)
    column = lax.broadcasted_iota(jnp.int32, (rows, rows), 1)
    rank = jnp.dot((column <= row).astype(BF16), live.astype(BF16), preferred_element_type=F32)
    lane = lax.broadcasted_iota(jnp.int32, (rows, LANES), 1).astype(F32)
    pick = jnp.where((live > 0.5) & (rank == lane + 1.0), 1.0, 0.0).astype(BF16)
    pick_ref[...] = pick
    step = 256
    for c in range(features // step):
        at = slice(c * step, (c + 1) * step)
        whole = jnp.concatenate([a[:, at].astype(F32) for a in arrived], axis=0).astype(BF16)
        moved = lax.dot_general(pick[:, :slots], whole, (((0,), (0,)), ((), ())), preferred_element_type=F32)
        for (first, last), out in zip(parts, outs):
            if first <= c * step < last:
                out[:, c * step - first : (c + 1) * step - first] = moved.astype(BF16)


def ahead_kernel(first, order, *refs):
    blocks, (gate_ref, up_ref, gate_sum, up_sum) = [refs[k] for k in order], refs[len(order) :]
    rows = jnp.concatenate([block[...] for block in blocks], axis=0)
    step = min(256, gate_ref.shape[1])
    for c in range(gate_ref.shape[1] // step):
        part = slice(c * step, (c + 1) * step)
        gate_sum[:, part] = jnp.dot(rows, gate_ref[first:, part], preferred_element_type=F32)
        up_sum[:, part] = jnp.dot(rows, up_ref[first:, part], preferred_element_type=F32)


def hidden_kernel(last, count, *refs):
    blocks, sums, (gate_ref, up_ref, hidden_ref) = refs[:count], refs[count:-3], refs[-3:]
    units = gate_ref.shape[1]
    rows = jnp.concatenate([block[...] for block in blocks], axis=0)
    step = min(256, units)
    for c in range(units // step):
        part = slice(c * step, (c + 1) * step)
        gate = jnp.dot(rows, gate_ref[:last, part], preferred_element_type=F32)
        up = jnp.dot(rows, up_ref[:last, part], preferred_element_type=F32)
        if sums:
            gate, up = gate + sums[0][:, part], up + sums[1][:, part]
        hidden_ref[:, part] = (gate / (1.0 + jnp.exp(-gate)) * up).astype(BF16)


def down_sum(columns, which, hiddens, down_ref):
    me = lax.axis_index("ing")
    rows, units = hiddens[0].shape
    slots = rows // columns
    total = jnp.zeros((rows, down_ref.shape[1]), F32)
    for f, hidden in zip(which, hiddens):
        block = jnp.concatenate(
            [hidden[slots * (e ^ f) : slots * ((e ^ f) + 1), :] for e in range(columns)], axis=0
        )
        at = pl.multiple_of((me ^ f) * units, units)
        total += jnp.dot(block, down_ref[pl.ds(at, units), :], preferred_element_type=F32)
    return total


def begin_kernel(columns, which, *refs):
    refs[-1][...] = down_sum(columns, which, refs[:-2], refs[-2])


def down_kernel(columns, which, *refs):
    count = len(which)
    hiddens, (sum_ref, down_ref), outs = refs[:count], refs[count : count + 2], refs[count + 2 :]
    total = sum_ref[...] + down_sum(columns, which, hiddens, down_ref)
    slots = total.shape[0] // columns
    for e in range(columns):
        outs[e][...] = total[e * slots : (e + 1) * slots].astype(BF16)


def spread_kernel(groups, columns, pick_ref, *refs):
    blocks, outs = refs[:columns][::-1], refs[columns:]
    for e in range(columns):
        block = blocks[e][...]
        back = jnp.dot(pick_ref[:, : block.shape[0]], block, preferred_element_type=F32)
        for d in range(groups):
            outs[d][e] = back[d * CAP : (d + 1) * CAP].astype(BF16)


def combine_kernel(groups, columns, mixing_ref, *refs):
    backs, (out_ref, rows_ref, held, sems) = refs[:groups][::-1], refs[groups:]
    me = lax.axis_index("ing")
    width, quarter = backs[0].shape[2], held.shape[0] // 4
    for e in range(columns):
        rows = jnp.concatenate([backs[d][e].astype(F32) for d in range(groups)], axis=0)
        rows_ref[:, pl.ds(pl.multiple_of((me ^ e) * width, width), width)] = rows.astype(BF16)
    copies = []
    for q in range(4):
        mine = pl.ds(q * quarter, quarter)
        held[mine, :] = jnp.dot(mixing_ref[mine, :], rows_ref[...], preferred_element_type=F32).astype(BF16)
        copies.append(pltpu.make_async_copy(held.at[mine], out_ref.at[mine], sems.at[q]))
        copies[-1].start()
    for copy in copies:
        copy.wait()


def swap(x, name, step):
    if step == 0:
        return x
    return lax.ppermute(x, name, [(a, a ^ step) for a in range(lax.axis_size(name))])


def swap_all(parts, name):
    return [swap(part, name, k) for k, part in enumerate(parts)][::-1]


def local(tokens, router_logits, expert_ids, w_gate, w_up, w_down):
    groups = lax.axis_size("grp")
    columns = lax.axis_size("ing")
    count, features = tokens.shape
    units, share = w_gate.shape[2], w_down.shape[2]
    slots = groups * CAP // 2
    wide = features + LANES
    ids = pltpu.with_memory_space_constraint(expert_ids.T, pltpu.HBM)
    logits = pltpu.with_memory_space_constraint(router_logits.T, pltpu.HBM)

    outbound = pl.pallas_call(
        functools.partial(dispatch_kernel, groups, features),
        out_shape=[jax.ShapeDtypeStruct((CAP, wide), BF16)] * groups,
        in_specs=[ANY, ANY],
        out_specs=[VMEM] * groups,
        scratch_shapes=[
            pltpu.VMEM(ids.shape, jnp.int32),
            pltpu.VMEM((count, features), BF16),
            pltpu.VMEM((count, count), BF16),
            pltpu.SemaphoreType.DMA((2,)),
        ],
        compiler_params=params(2 * count * features),
        name="dispatch",
    )(ids, pltpu.with_memory_space_constraint(tokens, pltpu.HBM))
    arrived = swap_all(outbound, "grp")

    weights = [w_gate[0], w_up[0], w_down[0]]
    weights = [pltpu.with_memory_space_constraint(w, pltpu.HBM) for w in weights]
    gate, up = pl.pallas_call(
        load_kernel,
        out_shape=[pltpu.VMEM(w.shape, BF16) for w in weights[:2]],
        in_specs=[ANY] * 3,
        out_specs=[VMEM] * 2,
        scratch_shapes=[pltpu.SemaphoreType.DMA((8,))],
        compiler_params=params(0),
        name="load",
    )(outbound[0], *weights[:2])

    cut = features // 2
    parts = [(0, cut), (cut, features)] if columns == 4 else [(0, features)]
    *own, pick = pl.pallas_call(
        functools.partial(compact_kernel, groups, slots, parts),
        out_shape=[jax.ShapeDtypeStruct((slots, last - first), BF16) for first, last in parts]
        + [jax.ShapeDtypeStruct((groups * CAP, LANES), BF16)],
        in_specs=[ANY] + [VMEM] * groups,
        out_specs=[VMEM] * (len(parts) + 1),
        compiler_params=params(2 * (groups * CAP + 2 * slots) * wide),
        name="compact",
    )(gate, *arrived)
    if columns == 4:
        near_low, near_high, high, far_high = [swap(part, "ing", e) for part, e in zip(own + own[1:] * 2, (1, 1, 2, 3))]
        low = swap(own[0], "ing", 2)
        far_low = swap(low, "ing", 1)
        sums = pl.pallas_call(
            functools.partial(ahead_kernel, cut, (0, 1, 3, 2)),
            out_shape=[jax.ShapeDtypeStruct((columns * slots, units), F32)] * 2,
            in_specs=[VMEM] * (columns + 2),
            out_specs=[VMEM] * 2,
            compiler_params=params(2 * columns * slots * (features + 4 * units)),
            name="ahead",
        )(own[1], near_high, far_high, high, gate, up)
        blocks = [own[0], near_low, low, far_low]
    else:
        sums, cut = [], features
        blocks = [swap(own[0], "ing", e) for e in range(columns)]

    hidden = pl.pallas_call(
        functools.partial(hidden_kernel, cut, columns),
        out_shape=jax.ShapeDtypeStruct((columns * slots, units), BF16),
        in_specs=[VMEM] * (columns + len(sums) + 2),
        out_specs=VMEM,
        compiler_params=params(2 * columns * slots * (2 * features + 5 * units)),
        name="hidden",
    )(*blocks, *sums, gate, up)
    down, mixing = pl.pallas_call(
        functools.partial(prepare_kernel, groups),
        out_shape=[
            pltpu.VMEM(w_down.shape[1:], BF16),
            jax.ShapeDtypeStruct((count, groups * CAP), BF16),
        ],
        in_specs=[ANY] * 4,
        out_specs=[VMEM] * 2,
        scratch_shapes=[
            pltpu.VMEM(ids.shape, jnp.int32),
            pltpu.VMEM(logits.shape, F32),
            pltpu.SemaphoreType.DMA((6,)),
        ],
        compiler_params=params(0),
        name="prepare",
    )(hidden, ids, logits, weights[2])
    hiddens = [swap(hidden, "ing", f) for f in range(columns)]

    early, late = (0, columns - 1), tuple(range(1, columns - 1))
    begun = pl.pallas_call(
        functools.partial(begin_kernel, columns, early),
        out_shape=jax.ShapeDtypeStruct((columns * slots, share), F32),
        in_specs=[VMEM] * (len(early) + 1),
        out_specs=VMEM,
        compiler_params=params(2 * columns * slots * (2 * units + 4 * share)),
        name="begin",
    )(*[hiddens[f] for f in early], down)
    results = pl.pallas_call(
        functools.partial(down_kernel, columns, late),
        out_shape=[jax.ShapeDtypeStruct((slots, share), BF16)] * columns,
        in_specs=[VMEM] * (len(late) + 2),
        out_specs=[VMEM] * columns,
        compiler_params=params(2 * columns * slots * (columns * units + 6 * share)),
        name="down",
    )(*[hiddens[f] for f in late], begun, down)
    results = swap_all(results, "ing")

    backs = pl.pallas_call(
        functools.partial(spread_kernel, groups, columns),
        out_shape=[jax.ShapeDtypeStruct((columns, CAP, share), BF16)] * groups,
        in_specs=[VMEM] * (columns + 1),
        out_specs=[VMEM] * groups,
        compiler_params=params(2 * (groups * CAP + slots) * features),
        name="spread",
    )(pick, *results)
    backs = swap_all(backs, "grp")

    if share % LANES:
        me = lax.axis_index("ing")
        rows = jnp.stack(backs[::-1])[:, jnp.arange(columns) ^ me]
        rows = rows.transpose(0, 2, 1, 3).reshape(groups * CAP, features)
        return jnp.dot(mixing, rows, preferred_element_type=F32).astype(BF16)
    return pl.pallas_call(
        functools.partial(combine_kernel, groups, columns),
        out_shape=jax.ShapeDtypeStruct((count, features), BF16),
        in_specs=[VMEM] * (1 + groups),
        out_specs=ANY,
        scratch_shapes=[
            pltpu.VMEM((groups * CAP, features), BF16),
            pltpu.VMEM((count, features), BF16),
            pltpu.SemaphoreType.DMA((4,)),
        ],
        compiler_params=params(2 * (count + groups * CAP) * features),
        name="combine",
    )(mixing, *backs)


def solution(mesh):
    placed = (
        P(("rep", "grp", "ing"), None),
        P(("rep", "grp", "ing"), None),
        P(("rep", "grp", "ing"), None),
        P("grp", None, "ing"),
        P("grp", None, "ing"),
        P("grp", None, "ing"),
    )
    return jax.shard_map(
        local, mesh=mesh, in_specs=placed, out_specs=P(("rep", "grp", "ing"), None), check_vma=False
    )
```

```python
import functools

import jax
import jax.numpy as jnp
from jax import lax
from jax.experimental import pallas as pl
from jax.experimental.pallas import tpu as pltpu
from jax.sharding import PartitionSpec as P

GROUP_EXPERTS = 24
CAP = 8
LANES = 128
ROUTE_SCALE = 2.827
MIB = 1024 * 1024

BF16 = jnp.bfloat16
F32 = jnp.float32
VMEM = pl.BlockSpec(memory_space=pltpu.VMEM)
ANY = pl.BlockSpec(memory_space=pl.ANY)


def params(nbytes):
    return pltpu.CompilerParams(vmem_limit_bytes=2 * nbytes + 4 * MIB)


def named(ids, expert):
    hit = jnp.zeros(expert.shape, F32)
    for k in range(ids.shape[0]):
        hit = jnp.where(ids[k : k + 1, :] == expert, 1.0, hit)
    return hit


def upto(count):
    return (
        lax.broadcasted_iota(jnp.int32, (count, count), 0)
        <= lax.broadcasted_iota(jnp.int32, (count, count), 1)
    ).astype(BF16)


def placing(ids, groups, me, before):
    rows, count = max(groups, 8), ids.shape[1]
    row = lax.broadcasted_iota(jnp.int32, (rows, count), 0)
    hit = named(ids, jnp.where(row < groups, (row ^ me) * GROUP_EXPERTS, -1))
    rank = jnp.dot(hit.astype(BF16), before, preferred_element_type=F32)
    slot = lax.broadcasted_iota(jnp.int32, (CAP, count), 0).astype(F32) + 1.0
    seat = jnp.where(hit > 0.5, rank, 0.0)
    place = [jnp.where(seat[d : d + 1, :] == slot, 1.0, 0.0) for d in range(groups)]
    return jnp.concatenate(place, axis=0), rank[:, count - 1 :]


def dispatch_kernel(groups, width, ids_ref, tokens_ref, *refs):
    outs, (ids_held, staged, before_ref, sems) = refs[:groups], refs[groups:]
    me = lax.axis_index("grp")
    features = tokens_ref.shape[1]
    first = pltpu.make_async_copy(ids_ref, ids_held, sems.at[features // width])
    first.start()
    copies = []
    for c in range(features // width):
        part = pl.ds(c * width, width)
        copies.append(pltpu.make_async_copy(tokens_ref.at[:, part], staged.at[:, part], sems.at[c]))
        copies[-1].start()
    before_ref[...] = upto(tokens_ref.shape[0])
    first.wait()
    place, counts = placing(ids_held[...], groups, me, before_ref[...])
    place = place.astype(BF16)
    slot = lax.broadcasted_iota(jnp.int32, (CAP, LANES), 0).astype(F32)
    for d in range(groups):
        live = slot < jnp.broadcast_to(counts[d : d + 1, :], (CAP, LANES))
        outs[d][:, features:] = jnp.where(live, 1.0, 0.0).astype(BF16)
    for c in range(features // width):
        copies[c].wait()
        part = slice(c * width, (c + 1) * width)
        rows = jnp.dot(place, staged[:, part], preferred_element_type=F32)
        for d in range(groups):
            outs[d][:, part] = rows[d * CAP : (d + 1) * CAP].astype(BF16)


def start_loads(weights, loaded, sems):
    copies = []
    for k in range(len(weights)):
        depth = weights[k].shape[0]
        for c in range(4):
            part = pl.ds(c * (depth // 4), depth // 4)
            copies.append(pltpu.make_async_copy(weights[k].at[part], loaded[k].at[part], sems.at[4 * k + c]))
            copies[-1].start()
    return copies


def load_kernel(after_ref, gate_ref, up_ref, gate_out, up_out, sems):
    del after_ref
    for copy in start_loads([gate_ref, up_ref], [gate_out, up_out], sems):
        copy.wait()


def prepare_kernel(groups, after_ref, ids_ref, logits_ref, down_ref, down_out, out_ref, ids_held, logits_held, sems):
    del after_ref
    small = [
        pltpu.make_async_copy(ids_ref, ids_held, sems.at[4]),
        pltpu.make_async_copy(logits_ref, logits_held, sems.at[5]),
    ]
    for copy in small:
        copy.start()
    copies = start_loads([down_ref], [down_out], sems)
    for copy in small:
        copy.wait()
    me = lax.axis_index("grp")
    ids = ids_held[...]
    place, _ = placing(ids, groups, me, upto(ids.shape[1]))
    group = (lax.broadcasted_iota(jnp.int32, place.shape, 0) // CAP) ^ me
    scores = 1.0 / (1.0 + jnp.exp(-logits_held[...]))
    expert = lax.broadcasted_iota(jnp.int32, scores.shape, 0)
    chosen = jnp.sum(jnp.where(named(ids, expert) > 0.5, scores, 0.0), axis=0, keepdims=True)
    leading = jnp.zeros(place.shape, F32)
    for g in range(groups):
        leading = jnp.where(group == g, scores[g * GROUP_EXPERTS : g * GROUP_EXPERTS + 1, :], leading)
    weight = (ROUTE_SCALE * leading / chosen).astype(BF16).astype(F32)
    out_ref[...] = jnp.where(place > 0.5, weight, 0.0).T.astype(BF16)
    for copy in copies:
        copy.wait()


def compact_kernel(groups, slots, parts, after_ref, *refs):
    del after_ref
    arrived, outs, pick_ref = refs[:groups][::-1], refs[groups:-1], refs[-1]
    rows = groups * CAP
    features = arrived[0].shape[1] - LANES
    live = jnp.concatenate([a[:, features:].astype(F32) for a in arrived], axis=0)
    row = lax.broadcasted_iota(jnp.int32, (rows, rows), 0)
    column = lax.broadcasted_iota(jnp.int32, (rows, rows), 1)
    rank = jnp.dot((column <= row).astype(BF16), live.astype(BF16), preferred_element_type=F32)
    lane = lax.broadcasted_iota(jnp.int32, (rows, LANES), 1).astype(F32)
    pick = jnp.where((live > 0.5) & (rank == lane + 1.0), 1.0, 0.0).astype(BF16)
    pick_ref[...] = pick
    step = 256
    for c in range(features // step):
        at = slice(c * step, (c + 1) * step)
        whole = jnp.concatenate([a[:, at].astype(F32) for a in arrived], axis=0).astype(BF16)
        moved = lax.dot_general(pick[:, :slots], whole, (((0,), (0,)), ((), ())), preferred_element_type=F32)
        for (first, last), out in zip(parts, outs):
            if first <= c * step < last:
                out[:, c * step - first : (c + 1) * step - first] = moved.astype(BF16)


def ahead_kernel(first, order, *refs):
    blocks, (gate_ref, up_ref, gate_sum, up_sum) = [refs[k] for k in order], refs[len(order) :]
    rows = jnp.concatenate([block[...] for block in blocks], axis=0)
    step = min(256, gate_ref.shape[1])
    for c in range(gate_ref.shape[1] // step):
        part = slice(c * step, (c + 1) * step)
        gate_sum[:, part] = jnp.dot(rows, gate_ref[first:, part], preferred_element_type=F32)
        up_sum[:, part] = jnp.dot(rows, up_ref[first:, part], preferred_element_type=F32)


def hidden_kernel(last, count, *refs):
    blocks, sums, (gate_ref, up_ref, hidden_ref) = refs[:count], refs[count:-3], refs[-3:]
    units = gate_ref.shape[1]
    rows = jnp.concatenate([block[...] for block in blocks], axis=0)
    step = min(256, units)
    for c in range(units // step):
        part = slice(c * step, (c + 1) * step)
        gate = jnp.dot(rows, gate_ref[:last, part], preferred_element_type=F32)
        up = jnp.dot(rows, up_ref[:last, part], preferred_element_type=F32)
        if sums:
            gate, up = gate + sums[0][:, part], up + sums[1][:, part]
        hidden_ref[:, part] = (gate / (1.0 + jnp.exp(-gate)) * up).astype(BF16)


def down_sum(columns, which, hiddens, down_ref):
    me = lax.axis_index("ing")
    rows, units = hiddens[0].shape
    slots = rows // columns
    total = jnp.zeros((rows, down_ref.shape[1]), F32)
    for f, hidden in zip(which, hiddens):
        block = jnp.concatenate(
            [hidden[slots * (e ^ f) : slots * ((e ^ f) + 1), :] for e in range(columns)], axis=0
        )
        at = pl.multiple_of((me ^ f) * units, units)
        total += jnp.dot(block, down_ref[pl.ds(at, units), :], preferred_element_type=F32)
    return total


def begin_kernel(columns, which, *refs):
    refs[-1][...] = down_sum(columns, which, refs[:-2], refs[-2])


def down_kernel(columns, which, *refs):
    count = len(which)
    hiddens, (sum_ref, down_ref) = refs[:count], refs[count : count + 2]
    outs, total_ref = refs[count + 2 : -1], refs[-1]
    me = lax.axis_index("ing")
    total_ref[...] = sum_ref[...] + down_sum(columns, which, hiddens, down_ref)
    slots = total_ref.shape[0] // columns
    for s in range(columns):
        at = pl.multiple_of((lax.rem(me + s, columns) ^ me) * slots, slots)
        outs[s][...] = total_ref[pl.ds(at, slots), :].astype(BF16)


def spread_kernel(groups, columns, pick_ref, *refs):
    blocks, outs = refs[:columns], refs[columns:]
    me = lax.axis_index("ing")
    for k in range(columns):
        block = blocks[k][...]
        place = lax.rem(me + columns - (k + 1), columns) ^ me
        back = jnp.dot(pick_ref[:, : block.shape[0]], block, preferred_element_type=F32)
        for d in range(groups):
            outs[d][place] = back[d * CAP : (d + 1) * CAP].astype(BF16)


def combine_kernel(groups, columns, mixing_ref, *refs):
    backs, (out_ref, held, sems) = refs[:groups][::-1], refs[groups:]
    me = lax.axis_index("ing")
    width, half = backs[0].shape[2], held.shape[0] // 2
    copies = []
    for e in range(columns):
        rows = jnp.concatenate([backs[d][e].astype(F32) for d in range(groups)], axis=0)
        rows = rows.astype(BF16)
        part = pl.ds(e * width, width)
        there = pl.ds(pl.multiple_of((me ^ e) * width, width), width)
        for h in range(2):
            mine = pl.ds(h * half, half)
            value = jnp.dot(mixing_ref[mine, :], rows, preferred_element_type=F32)
            held[mine, part] = value.astype(BF16)
            copies.append(
                pltpu.make_async_copy(held.at[mine, part], out_ref.at[mine, there], sems.at[2 * e + h])
            )
            copies[-1].start()
    for copy in copies:
        copy.wait()


def swap(x, name, step):
    if step == 0:
        return x
    return lax.ppermute(x, name, [(a, a ^ step) for a in range(lax.axis_size(name))])


def swap_all(parts, name):
    return [swap(part, name, k) for k, part in enumerate(parts)][::-1]


def local(tokens, router_logits, expert_ids, w_gate, w_up, w_down):
    groups = lax.axis_size("grp")
    columns = lax.axis_size("ing")
    count, features = tokens.shape
    units, share = w_gate.shape[2], w_down.shape[2]
    slots = groups * CAP // 2
    wide = features + LANES
    ids = pltpu.with_memory_space_constraint(expert_ids.T, pltpu.HBM)
    logits = pltpu.with_memory_space_constraint(router_logits.T, pltpu.HBM)

    outbound = pl.pallas_call(
        functools.partial(dispatch_kernel, groups, features // 2),
        out_shape=[jax.ShapeDtypeStruct((CAP, wide), BF16)] * groups,
        in_specs=[ANY, ANY],
        out_specs=[VMEM] * groups,
        scratch_shapes=[
            pltpu.VMEM(ids.shape, jnp.int32),
            pltpu.VMEM((count, features), BF16),
            pltpu.VMEM((count, count), BF16),
            pltpu.SemaphoreType.DMA((3,)),
        ],
        compiler_params=params(2 * count * features),
        name="dispatch",
    )(ids, pltpu.with_memory_space_constraint(tokens, pltpu.HBM))
    arrived = swap_all(outbound, "grp")

    weights = [w_gate[0], w_up[0], w_down[0]]
    weights = [pltpu.with_memory_space_constraint(w, pltpu.HBM) for w in weights]
    gate, up = pl.pallas_call(
        load_kernel,
        out_shape=[pltpu.VMEM(w.shape, BF16) for w in weights[:2]],
        in_specs=[ANY] * 3,
        out_specs=[VMEM] * 2,
        scratch_shapes=[pltpu.SemaphoreType.DMA((8,))],
        compiler_params=params(0),
        name="load",
    )(outbound[0], *weights[:2])

    cut = features // 2
    parts = [(0, cut), (cut, features)] if columns == 4 else [(0, features)]
    *own, pick = pl.pallas_call(
        functools.partial(compact_kernel, groups, slots, parts),
        out_shape=[jax.ShapeDtypeStruct((slots, last - first), BF16) for first, last in parts]
        + [jax.ShapeDtypeStruct((groups * CAP, LANES), BF16)],
        in_specs=[ANY] + [VMEM] * groups,
        out_specs=[VMEM] * (len(parts) + 1),
        compiler_params=params(2 * (groups * CAP + 2 * slots) * wide),
        name="compact",
    )(gate, *arrived)
    if columns == 4:
        near_low, near_high, high, far_high = [swap(part, "ing", e) for part, e in zip(own + own[1:] * 2, (1, 1, 2, 3))]
        low = swap(own[0], "ing", 2)
        far_low = swap(low, "ing", 1)
        sums = pl.pallas_call(
            functools.partial(ahead_kernel, cut, (0, 1, 3, 2)),
            out_shape=[jax.ShapeDtypeStruct((columns * slots, units), F32)] * 2,
            in_specs=[VMEM] * (columns + 2),
            out_specs=[VMEM] * 2,
            compiler_params=params(2 * columns * slots * (features + 4 * units)),
            name="ahead",
        )(own[1], near_high, far_high, high, gate, up)
        blocks = [own[0], near_low, low, far_low]
    else:
        sums, cut = [], features
        blocks = [swap(own[0], "ing", e) for e in range(columns)]

    hidden = pl.pallas_call(
        functools.partial(hidden_kernel, cut, columns),
        out_shape=jax.ShapeDtypeStruct((columns * slots, units), BF16),
        in_specs=[VMEM] * (columns + len(sums) + 2),
        out_specs=VMEM,
        compiler_params=params(2 * columns * slots * (2 * features + 5 * units)),
        name="hidden",
    )(*blocks, *sums, gate, up)
    down, mixing = pl.pallas_call(
        functools.partial(prepare_kernel, groups),
        out_shape=[
            pltpu.VMEM(w_down.shape[1:], BF16),
            jax.ShapeDtypeStruct((count, groups * CAP), BF16),
        ],
        in_specs=[ANY] * 4,
        out_specs=[VMEM] * 2,
        scratch_shapes=[
            pltpu.VMEM(ids.shape, jnp.int32),
            pltpu.VMEM(logits.shape, F32),
            pltpu.SemaphoreType.DMA((6,)),
        ],
        compiler_params=params(0),
        name="prepare",
    )(hidden, ids, logits, weights[2])
    hiddens = [swap(hidden, "ing", f) for f in range(columns)]

    early, late = (0, columns - 1), tuple(range(1, columns - 1))
    begun = pl.pallas_call(
        functools.partial(begin_kernel, columns, early),
        out_shape=jax.ShapeDtypeStruct((columns * slots, share), F32),
        in_specs=[VMEM] * (len(early) + 1),
        out_specs=VMEM,
        compiler_params=params(2 * columns * slots * (2 * units + 4 * share)),
        name="begin",
    )(*[hiddens[f] for f in early], down)
    results = pl.pallas_call(
        functools.partial(down_kernel, columns, late),
        out_shape=[jax.ShapeDtypeStruct((slots, share), BF16)] * columns,
        in_specs=[VMEM] * (len(late) + 2),
        out_specs=[VMEM] * columns,
        scratch_shapes=[pltpu.VMEM((columns * slots, share), F32)],
        compiler_params=params(2 * columns * slots * (columns * units + 8 * share)),
        name="down",
    )(*[hiddens[f] for f in late], begun, down)
    results = [
        lax.ppermute(results[s], "ing", [(a, (a + s) % columns) for a in range(columns)]) for s in range(1, columns)
    ] + [results[0]]

    backs = pl.pallas_call(
        functools.partial(spread_kernel, groups, columns),
        out_shape=[jax.ShapeDtypeStruct((columns, CAP, share), BF16)] * groups,
        in_specs=[VMEM] * (columns + 1),
        out_specs=[VMEM] * groups,
        compiler_params=params(2 * (groups * CAP + slots) * features),
        name="spread",
    )(pick, *results)
    backs = swap_all(backs, "grp")

    if share % LANES:
        me = lax.axis_index("ing")
        rows = jnp.stack(backs[::-1])[:, jnp.arange(columns) ^ me]
        rows = rows.transpose(0, 2, 1, 3).reshape(groups * CAP, features)
        return jnp.dot(mixing, rows, preferred_element_type=F32).astype(BF16)
    return pl.pallas_call(
        functools.partial(combine_kernel, groups, columns),
        out_shape=jax.ShapeDtypeStruct((count, features), BF16),
        in_specs=[VMEM] * (1 + groups),
        out_specs=ANY,
        scratch_shapes=[pltpu.VMEM((count, features), BF16), pltpu.SemaphoreType.DMA((2 * columns,))],
        compiler_params=params(2 * (count + groups * CAP) * features),
        name="combine",
    )(mixing, *backs)


def solution(mesh):
    placed = (
        P(("rep", "grp", "ing"), None),
        P(("rep", "grp", "ing"), None),
        P(("rep", "grp", "ing"), None),
        P("grp", None, "ing"),
        P("grp", None, "ing"),
        P("grp", None, "ing"),
    )
    return jax.shard_map(
        local, mesh=mesh, in_specs=placed, out_specs=P(("rep", "grp", "ing"), None), check_vma=False
    )
```

```python
import functools

import jax
import jax.numpy as jnp
from jax import lax
from jax.experimental import pallas as pl
from jax.experimental.pallas import tpu as pltpu
from jax.sharding import PartitionSpec as P

GROUP_EXPERTS = 24
CAP = 8
LANES = 128
ROUTE_SCALE = 2.827
MIB = 1024 * 1024

BF16 = jnp.bfloat16
F32 = jnp.float32
VMEM = pl.BlockSpec(memory_space=pltpu.VMEM)
ANY = pl.BlockSpec(memory_space=pl.ANY)


def params(nbytes):
    return pltpu.CompilerParams(vmem_limit_bytes=2 * nbytes + 4 * MIB)


def named(ids, expert):
    hit = jnp.zeros(expert.shape, F32)
    for k in range(ids.shape[0]):
        hit = jnp.where(ids[k : k + 1, :] == expert, 1.0, hit)
    return hit


def upto(count):
    return (
        lax.broadcasted_iota(jnp.int32, (count, count), 0)
        <= lax.broadcasted_iota(jnp.int32, (count, count), 1)
    ).astype(BF16)


def placing(ids, groups, me, before):
    rows, count = max(groups, 8), ids.shape[1]
    row = lax.broadcasted_iota(jnp.int32, (rows, count), 0)
    hit = named(ids, jnp.where(row < groups, (row ^ me) * GROUP_EXPERTS, -1))
    rank = jnp.dot(hit.astype(BF16), before, preferred_element_type=F32)
    slot = lax.broadcasted_iota(jnp.int32, (CAP, count), 0).astype(F32) + 1.0
    seat = jnp.where(hit > 0.5, rank, 0.0)
    place = [jnp.where(seat[d : d + 1, :] == slot, 1.0, 0.0) for d in range(groups)]
    return jnp.concatenate(place, axis=0), rank[:, count - 1 :]


def dispatch_kernel(groups, cut, ids_ref, tokens_ref, *refs):
    outs, (ids_held, staged, before_ref, sems) = refs[:groups], refs[groups:]
    me = lax.axis_index("grp")
    features = tokens_ref.shape[1]
    first = pltpu.make_async_copy(ids_ref, ids_held, sems.at[2])
    first.start()
    copies = []
    parts = (0, cut), (cut, features)
    for c, (begin, end) in enumerate(parts):
        part = pl.ds(begin, end - begin)
        copies.append(pltpu.make_async_copy(tokens_ref.at[:, part], staged.at[:, part], sems.at[c]))
        copies[-1].start()
    before_ref[...] = upto(tokens_ref.shape[0])
    first.wait()
    place, counts = placing(ids_held[...], groups, me, before_ref[...])
    place = place.astype(BF16)
    slot = lax.broadcasted_iota(jnp.int32, (CAP, LANES), 0).astype(F32)
    for d in range(groups):
        live = slot < jnp.broadcast_to(counts[d : d + 1, :], (CAP, LANES))
        outs[d][:, features:] = jnp.where(live, 1.0, 0.0).astype(BF16)
    for copy, (begin, end) in zip(copies, parts):
        copy.wait()
        part = slice(begin, end)
        rows = jnp.dot(place, staged[:, part], preferred_element_type=F32)
        for d in range(groups):
            outs[d][:, part] = rows[d * CAP : (d + 1) * CAP].astype(BF16)


def start_loads(weights, loaded, sems):
    copies = []
    for k in range(len(weights)):
        depth = weights[k].shape[0]
        for c in range(4):
            part = pl.ds(c * (depth // 4), depth // 4)
            copies.append(pltpu.make_async_copy(weights[k].at[part], loaded[k].at[part], sems.at[4 * k + c]))
            copies[-1].start()
    return copies


def load_kernel(after_ref, gate_ref, up_ref, gate_out, up_out, sems):
    del after_ref
    for copy in start_loads([gate_ref, up_ref], [gate_out, up_out], sems):
        copy.wait()


def prepare_kernel(groups, after_ref, ids_ref, logits_ref, down_ref, down_out, out_ref, ids_held, logits_held, sems):
    del after_ref
    small = [
        pltpu.make_async_copy(ids_ref, ids_held, sems.at[4]),
        pltpu.make_async_copy(logits_ref, logits_held, sems.at[5]),
    ]
    for copy in small:
        copy.start()
    copies = start_loads([down_ref], [down_out], sems)
    for copy in small:
        copy.wait()
    me = lax.axis_index("grp")
    ids = ids_held[...]
    place, _ = placing(ids, groups, me, upto(ids.shape[1]))
    group = (lax.broadcasted_iota(jnp.int32, place.shape, 0) // CAP) ^ me
    scores = 1.0 / (1.0 + jnp.exp(-logits_held[...]))
    expert = lax.broadcasted_iota(jnp.int32, scores.shape, 0)
    chosen = jnp.sum(jnp.where(named(ids, expert) > 0.5, scores, 0.0), axis=0, keepdims=True)
    leading = jnp.zeros(place.shape, F32)
    for g in range(groups):
        leading = jnp.where(group == g, scores[g * GROUP_EXPERTS : g * GROUP_EXPERTS + 1, :], leading)
    weight = (ROUTE_SCALE * leading / chosen).astype(BF16).astype(F32)
    out_ref[...] = jnp.where(place > 0.5, weight, 0.0).T.astype(BF16)
    for copy in copies:
        copy.wait()


def compact_kernel(groups, slots, parts, after_ref, *refs):
    del after_ref
    arrived, outs, pick_ref = refs[:groups][::-1], refs[groups:-1], refs[-1]
    rows = groups * CAP
    features = arrived[0].shape[1] - LANES
    live = jnp.concatenate([a[:, features:].astype(F32) for a in arrived], axis=0)
    row = lax.broadcasted_iota(jnp.int32, (rows, rows), 0)
    column = lax.broadcasted_iota(jnp.int32, (rows, rows), 1)
    rank = jnp.dot((column <= row).astype(BF16), live.astype(BF16), preferred_element_type=F32)
    lane = lax.broadcasted_iota(jnp.int32, (rows, LANES), 1).astype(F32)
    pick = jnp.where((live > 0.5) & (rank == lane + 1.0), 1.0, 0.0).astype(BF16)
    pick_ref[...] = pick
    step = 256
    for c in range(features // step):
        at = slice(c * step, (c + 1) * step)
        whole = jnp.concatenate([a[:, at].astype(F32) for a in arrived], axis=0).astype(BF16)
        moved = lax.dot_general(pick[:, :slots], whole, (((0,), (0,)), ((), ())), preferred_element_type=F32)
        for (first, last), out in zip(parts, outs):
            if first <= c * step < last:
                out[:, c * step - first : (c + 1) * step - first] = moved.astype(BF16)


def ahead_kernel(first, order, *refs):
    blocks, (gate_ref, up_ref, gate_sum, up_sum) = [refs[k] for k in order], refs[len(order) :]
    rows = jnp.concatenate([block[...] for block in blocks], axis=0)
    step = min(256, gate_ref.shape[1])
    for c in range(gate_ref.shape[1] // step):
        part = slice(c * step, (c + 1) * step)
        gate_sum[:, part] = jnp.dot(rows, gate_ref[first:, part], preferred_element_type=F32)
        up_sum[:, part] = jnp.dot(rows, up_ref[first:, part], preferred_element_type=F32)


def hidden_kernel(last, count, *refs):
    blocks, sums, (gate_ref, up_ref, hidden_ref) = refs[:count], refs[count:-3], refs[-3:]
    units = gate_ref.shape[1]
    rows = jnp.concatenate([block[...] for block in blocks], axis=0)
    step = min(256, units)
    for c in range(units // step):
        part = slice(c * step, (c + 1) * step)
        gate = jnp.dot(rows, gate_ref[:last, part], preferred_element_type=F32)
        up = jnp.dot(rows, up_ref[:last, part], preferred_element_type=F32)
        if sums:
            gate, up = gate + sums[0][:, part], up + sums[1][:, part]
        hidden_ref[:, part] = (gate / (1.0 + jnp.exp(-gate)) * up).astype(BF16)


def down_sum(columns, which, hiddens, down_ref):
    me = lax.axis_index("ing")
    rows, units = hiddens[0].shape
    slots = rows // columns
    total = jnp.zeros((rows, down_ref.shape[1]), F32)
    for f, hidden in zip(which, hiddens):
        block = jnp.concatenate(
            [hidden[slots * (e ^ f) : slots * ((e ^ f) + 1), :] for e in range(columns)], axis=0
        )
        at = pl.multiple_of((me ^ f) * units, units)
        total += jnp.dot(block, down_ref[pl.ds(at, units), :], preferred_element_type=F32)
    return total


def begin_kernel(columns, which, *refs):
    refs[-1][...] = down_sum(columns, which, refs[:-2], refs[-2])


def down_kernel(columns, which, *refs):
    count = len(which)
    hiddens, (sum_ref, down_ref) = refs[:count], refs[count : count + 2]
    outs, total_ref = refs[count + 2 : -1], refs[-1]
    me = lax.axis_index("ing")
    total_ref[...] = sum_ref[...] + down_sum(columns, which, hiddens, down_ref)
    slots = total_ref.shape[0] // columns
    for s in range(columns):
        at = pl.multiple_of((lax.rem(me + s, columns) ^ me) * slots, slots)
        outs[s][...] = total_ref[pl.ds(at, slots), :].astype(BF16)


def spread_kernel(groups, columns, pick_ref, *refs):
    blocks, outs = refs[:columns], refs[columns:]
    me = lax.axis_index("ing")
    for k in range(columns):
        block = blocks[k][...]
        place = lax.rem(me + columns - (k + 1), columns) ^ me
        back = jnp.dot(pick_ref[:, : block.shape[0]], block, preferred_element_type=F32)
        for d in range(groups):
            outs[d][place] = back[d * CAP : (d + 1) * CAP].astype(BF16)


def combine_kernel(groups, columns, mixing_ref, *refs):
    backs, (out_ref, held, sems) = refs[:groups][::-1], refs[groups:]
    me = lax.axis_index("ing")
    width, half = backs[0].shape[2], held.shape[0] // 2
    copies = []
    for e in range(columns):
        rows = jnp.concatenate([backs[d][e].astype(F32) for d in range(groups)], axis=0)
        rows = rows.astype(BF16)
        part = pl.ds(e * width, width)
        there = pl.ds(pl.multiple_of((me ^ e) * width, width), width)
        for h in range(2):
            mine = pl.ds(h * half, half)
            value = jnp.dot(mixing_ref[mine, :], rows, preferred_element_type=F32)
            held[mine, part] = value.astype(BF16)
            copies.append(
                pltpu.make_async_copy(held.at[mine, part], out_ref.at[mine, there], sems.at[2 * e + h])
            )
            copies[-1].start()
    for copy in copies:
        copy.wait()


def swap(x, name, step):
    if step == 0:
        return x
    return lax.ppermute(x, name, [(a, a ^ step) for a in range(lax.axis_size(name))])


def swap_all(parts, name):
    return [swap(part, name, k) for k, part in enumerate(parts)][::-1]


def local(tokens, router_logits, expert_ids, w_gate, w_up, w_down):
    groups = lax.axis_size("grp")
    columns = lax.axis_size("ing")
    count, features = tokens.shape
    units, share = w_gate.shape[2], w_down.shape[2]
    slots = groups * CAP // 2
    wide = features + LANES
    ids = pltpu.with_memory_space_constraint(expert_ids.T, pltpu.HBM)
    logits = pltpu.with_memory_space_constraint(router_logits.T, pltpu.HBM)

    outbound = pl.pallas_call(
        functools.partial(dispatch_kernel, groups, features * 5 // 7),
        out_shape=[jax.ShapeDtypeStruct((CAP, wide), BF16)] * groups,
        in_specs=[ANY, ANY],
        out_specs=[VMEM] * groups,
        scratch_shapes=[
            pltpu.VMEM(ids.shape, jnp.int32),
            pltpu.VMEM((count, features), BF16),
            pltpu.VMEM((count, count), BF16),
            pltpu.SemaphoreType.DMA((3,)),
        ],
        compiler_params=params(2 * count * features),
        name="dispatch",
    )(ids, pltpu.with_memory_space_constraint(tokens, pltpu.HBM))
    arrived = swap_all(outbound, "grp")

    weights = [w_gate[0], w_up[0], w_down[0]]
    weights = [pltpu.with_memory_space_constraint(w, pltpu.HBM) for w in weights]
    gate, up = pl.pallas_call(
        load_kernel,
        out_shape=[pltpu.VMEM(w.shape, BF16) for w in weights[:2]],
        in_specs=[ANY] * 3,
        out_specs=[VMEM] * 2,
        scratch_shapes=[pltpu.SemaphoreType.DMA((8,))],
        compiler_params=params(0),
        name="load",
    )(outbound[0], *weights[:2])

    cut = features // 2
    parts = [(0, cut), (cut, features)] if columns == 4 else [(0, features)]
    *own, pick = pl.pallas_call(
        functools.partial(compact_kernel, groups, slots, parts),
        out_shape=[jax.ShapeDtypeStruct((slots, last - first), BF16) for first, last in parts]
        + [jax.ShapeDtypeStruct((groups * CAP, LANES), BF16)],
        in_specs=[ANY] + [VMEM] * groups,
        out_specs=[VMEM] * (len(parts) + 1),
        compiler_params=params(2 * (groups * CAP + 2 * slots) * wide),
        name="compact",
    )(gate, *arrived)
    if columns == 4:
        near_low, near_high, high, far_high = [swap(part, "ing", e) for part, e in zip(own + own[1:] * 2, (1, 1, 2, 3))]
        low = swap(own[0], "ing", 2)
        far_low = swap(low, "ing", 1)
        sums = pl.pallas_call(
            functools.partial(ahead_kernel, cut, (0, 1, 3, 2)),
            out_shape=[jax.ShapeDtypeStruct((columns * slots, units), F32)] * 2,
            in_specs=[VMEM] * (columns + 2),
            out_specs=[VMEM] * 2,
            compiler_params=params(2 * columns * slots * (features + 4 * units)),
            name="ahead",
        )(own[1], near_high, far_high, high, gate, up)
        blocks = [own[0], near_low, low, far_low]
    else:
        sums, cut = [], features
        blocks = [swap(own[0], "ing", e) for e in range(columns)]

    hidden = pl.pallas_call(
        functools.partial(hidden_kernel, cut, columns),
        out_shape=jax.ShapeDtypeStruct((columns * slots, units), BF16),
        in_specs=[VMEM] * (columns + len(sums) + 2),
        out_specs=VMEM,
        compiler_params=params(2 * columns * slots * (2 * features + 5 * units)),
        name="hidden",
    )(*blocks, *sums, gate, up)
    down, mixing = pl.pallas_call(
        functools.partial(prepare_kernel, groups),
        out_shape=[
            pltpu.VMEM(w_down.shape[1:], BF16),
            jax.ShapeDtypeStruct((count, groups * CAP), BF16),
        ],
        in_specs=[ANY] * 4,
        out_specs=[VMEM] * 2,
        scratch_shapes=[
            pltpu.VMEM(ids.shape, jnp.int32),
            pltpu.VMEM(logits.shape, F32),
            pltpu.SemaphoreType.DMA((6,)),
        ],
        compiler_params=params(0),
        name="prepare",
    )(hidden, ids, logits, weights[2])
    hiddens = [swap(hidden, "ing", f) for f in range(columns)]

    early, late = (0, columns - 1), tuple(range(1, columns - 1))
    begun = pl.pallas_call(
        functools.partial(begin_kernel, columns, early),
        out_shape=jax.ShapeDtypeStruct((columns * slots, share), F32),
        in_specs=[VMEM] * (len(early) + 1),
        out_specs=VMEM,
        compiler_params=params(2 * columns * slots * (2 * units + 4 * share)),
        name="begin",
    )(*[hiddens[f] for f in early], down)
    results = pl.pallas_call(
        functools.partial(down_kernel, columns, late),
        out_shape=[jax.ShapeDtypeStruct((slots, share), BF16)] * columns,
        in_specs=[VMEM] * (len(late) + 2),
        out_specs=[VMEM] * columns,
        scratch_shapes=[pltpu.VMEM((columns * slots, share), F32)],
        compiler_params=params(2 * columns * slots * (columns * units + 8 * share)),
        name="down",
    )(*[hiddens[f] for f in late], begun, down)
    results = [
        lax.ppermute(results[s], "ing", [(a, (a + s) % columns) for a in range(columns)]) for s in range(1, columns)
    ] + [results[0]]

    backs = pl.pallas_call(
        functools.partial(spread_kernel, groups, columns),
        out_shape=[jax.ShapeDtypeStruct((columns, CAP, share), BF16)] * groups,
        in_specs=[VMEM] * (columns + 1),
        out_specs=[VMEM] * groups,
        compiler_params=params(2 * (groups * CAP + slots) * features),
        name="spread",
    )(pick, *results)
    backs = swap_all(backs, "grp")

    if share % LANES:
        me = lax.axis_index("ing")
        rows = jnp.stack(backs[::-1])[:, jnp.arange(columns) ^ me]
        rows = rows.transpose(0, 2, 1, 3).reshape(groups * CAP, features)
        return jnp.dot(mixing, rows, preferred_element_type=F32).astype(BF16)
    return pl.pallas_call(
        functools.partial(combine_kernel, groups, columns),
        out_shape=jax.ShapeDtypeStruct((count, features), BF16),
        in_specs=[VMEM] * (1 + groups),
        out_specs=ANY,
        scratch_shapes=[pltpu.VMEM((count, features), BF16), pltpu.SemaphoreType.DMA((2 * columns,))],
        compiler_params=params(2 * (count + groups * CAP) * features),
        name="combine",
    )(mixing, *backs)


def solution(mesh):
    placed = (
        P(("rep", "grp", "ing"), None),
        P(("rep", "grp", "ing"), None),
        P(("rep", "grp", "ing"), None),
        P("grp", None, "ing"),
        P("grp", None, "ing"),
        P("grp", None, "ing"),
    )
    return jax.shard_map(
        local, mesh=mesh, in_specs=placed, out_specs=P(("rep", "grp", "ing"), None), check_vma=False
    )
```

```python
import functools

import jax
import jax.numpy as jnp
from jax import lax
from jax.experimental import pallas as pl
from jax.experimental.pallas import tpu as pltpu
from jax.sharding import PartitionSpec as P

GROUP_EXPERTS = 24
CAP = 8
LANES = 128
ROUTE_SCALE = 2.827
MIB = 1024 * 1024

BF16 = jnp.bfloat16
F32 = jnp.float32
VMEM = pl.BlockSpec(memory_space=pltpu.VMEM)
ANY = pl.BlockSpec(memory_space=pl.ANY)


def params(nbytes):
    return pltpu.CompilerParams(vmem_limit_bytes=2 * nbytes + 4 * MIB)


def named(ids, expert):
    hit = jnp.zeros(expert.shape, F32)
    for k in range(ids.shape[0]):
        hit = jnp.where(ids[k : k + 1, :] == expert, 1.0, hit)
    return hit


def upto(count):
    return (
        lax.broadcasted_iota(jnp.int32, (count, count), 0)
        <= lax.broadcasted_iota(jnp.int32, (count, count), 1)
    ).astype(BF16)


def placing(ids, groups, me, before):
    rows, count = max(groups, 8), ids.shape[1]
    row = lax.broadcasted_iota(jnp.int32, (rows, count), 0)
    hit = named(ids, jnp.where(row < groups, (row ^ me) * GROUP_EXPERTS, -1))
    rank = jnp.dot(hit.astype(BF16), before, preferred_element_type=F32)
    slot = lax.broadcasted_iota(jnp.int32, (CAP, count), 0).astype(F32) + 1.0
    seat = jnp.where(hit > 0.5, rank, 0.0)
    place = [jnp.where(seat[d : d + 1, :] == slot, 1.0, 0.0) for d in range(groups)]
    return jnp.concatenate(place, axis=0), rank[:, count - 1 :]


def dispatch_kernel(groups, width, ids_ref, tokens_ref, *refs):
    outs, (ids_held, staged, before_ref, sems) = refs[:groups], refs[groups:]
    me = lax.axis_index("grp")
    features = tokens_ref.shape[1]
    first = pltpu.make_async_copy(ids_ref, ids_held, sems.at[features // width])
    first.start()
    copies = []
    for c in range(features // width):
        part = pl.ds(c * width, width)
        copies.append(pltpu.make_async_copy(tokens_ref.at[:, part], staged.at[:, part], sems.at[c]))
        copies[-1].start()
    before_ref[...] = upto(tokens_ref.shape[0])
    first.wait()
    place, counts = placing(ids_held[...], groups, me, before_ref[...])
    place = place.astype(BF16)
    slot = lax.broadcasted_iota(jnp.int32, (CAP, LANES), 0).astype(F32)
    for d in range(groups):
        live = slot < jnp.broadcast_to(counts[d : d + 1, :], (CAP, LANES))
        outs[d][:, features:] = jnp.where(live, 1.0, 0.0).astype(BF16)
    for c in range(features // width):
        copies[c].wait()
        part = slice(c * width, (c + 1) * width)
        rows = jnp.dot(place, staged[:, part], preferred_element_type=F32)
        for d in range(groups):
            outs[d][:, part] = rows[d * CAP : (d + 1) * CAP].astype(BF16)


def start_loads(weights, loaded, sems):
    copies = []
    for k in range(len(weights)):
        depth = weights[k].shape[0]
        for c in range(4):
            part = pl.ds(c * (depth // 4), depth // 4)
            copies.append(pltpu.make_async_copy(weights[k].at[part], loaded[k].at[part], sems.at[4 * k + c]))
            copies[-1].start()
    return copies


def load_kernel(after_ref, gate_ref, up_ref, gate_out, up_out, sems):
    del after_ref
    for copy in start_loads([gate_ref, up_ref], [gate_out, up_out], sems):
        copy.wait()


def prepare_kernel(groups, after_ref, ids_ref, logits_ref, down_ref, down_out, out_ref, ids_held, logits_held, sems):
    del after_ref
    small = [
        pltpu.make_async_copy(ids_ref, ids_held, sems.at[4]),
        pltpu.make_async_copy(logits_ref, logits_held, sems.at[5]),
    ]
    for copy in small:
        copy.start()
    copies = start_loads([down_ref], [down_out], sems)
    for copy in small:
        copy.wait()
    me = lax.axis_index("grp")
    ids = ids_held[...]
    place, _ = placing(ids, groups, me, upto(ids.shape[1]))
    group = (lax.broadcasted_iota(jnp.int32, place.shape, 0) // CAP) ^ me
    scores = 1.0 / (1.0 + jnp.exp(-logits_held[...]))
    expert = lax.broadcasted_iota(jnp.int32, scores.shape, 0)
    chosen = jnp.sum(jnp.where(named(ids, expert) > 0.5, scores, 0.0), axis=0, keepdims=True)
    leading = jnp.zeros(place.shape, F32)
    for g in range(groups):
        leading = jnp.where(group == g, scores[g * GROUP_EXPERTS : g * GROUP_EXPERTS + 1, :], leading)
    weight = (ROUTE_SCALE * leading / chosen).astype(BF16).astype(F32)
    out_ref[...] = jnp.where(place > 0.5, weight, 0.0).T.astype(BF16)
    for copy in copies:
        copy.wait()


def compact_kernel(groups, slots, parts, after_ref, *refs):
    del after_ref
    arrived, outs, pick_ref = refs[:groups][::-1], refs[groups:-1], refs[-1]
    rows = groups * CAP
    features = arrived[0].shape[1] - LANES
    live = jnp.concatenate([a[:, features:].astype(F32) for a in arrived], axis=0)
    row = lax.broadcasted_iota(jnp.int32, (rows, rows), 0)
    column = lax.broadcasted_iota(jnp.int32, (rows, rows), 1)
    rank = jnp.dot((column <= row).astype(BF16), live.astype(BF16), preferred_element_type=F32)
    lane = lax.broadcasted_iota(jnp.int32, (rows, LANES), 1).astype(F32)
    pick = jnp.where((live > 0.5) & (rank == lane + 1.0), 1.0, 0.0).astype(BF16)
    pick_ref[...] = pick
    step = 256
    for c in range(features // step):
        at = slice(c * step, (c + 1) * step)
        whole = jnp.concatenate([a[:, at].astype(F32) for a in arrived], axis=0).astype(BF16)
        moved = lax.dot_general(pick[:, :slots], whole, (((0,), (0,)), ((), ())), preferred_element_type=F32)
        for (first, last), out in zip(parts, outs):
            if first <= c * step < last:
                out[:, c * step - first : (c + 1) * step - first] = moved.astype(BF16)


def ahead_kernel(first, order, *refs):
    blocks, (gate_ref, up_ref, gate_sum, up_sum) = [refs[k] for k in order], refs[len(order) :]
    rows = jnp.concatenate([block[...] for block in blocks], axis=0)
    step = min(256, gate_ref.shape[1])
    for c in range(gate_ref.shape[1] // step):
        part = slice(c * step, (c + 1) * step)
        gate_sum[:, part] = jnp.dot(rows, gate_ref[first:, part], preferred_element_type=F32)
        up_sum[:, part] = jnp.dot(rows, up_ref[first:, part], preferred_element_type=F32)


def hidden_kernel(last, count, *refs):
    blocks, sums, (gate_ref, up_ref, hidden_ref) = refs[:count], refs[count:-3], refs[-3:]
    units = gate_ref.shape[1]
    rows = jnp.concatenate([block[...] for block in blocks], axis=0)
    step = min(256, units)
    for c in range(units // step):
        part = slice(c * step, (c + 1) * step)
        gate = jnp.dot(rows, gate_ref[:last, part], preferred_element_type=F32)
        up = jnp.dot(rows, up_ref[:last, part], preferred_element_type=F32)
        if sums:
            gate, up = gate + sums[0][:, part], up + sums[1][:, part]
        hidden_ref[:, part] = (gate / (1.0 + jnp.exp(-gate)) * up).astype(BF16)


def down_sum(columns, which, hiddens, down_ref):
    me = lax.axis_index("ing")
    rows, units = hiddens[0].shape
    slots = rows // columns
    total = jnp.zeros((rows, down_ref.shape[1]), F32)
    for f, hidden in zip(which, hiddens):
        block = jnp.concatenate(
            [hidden[slots * (e ^ f) : slots * ((e ^ f) + 1), :] for e in range(columns)], axis=0
        )
        at = pl.multiple_of((me ^ f) * units, units)
        total += jnp.dot(block, down_ref[pl.ds(at, units), :], preferred_element_type=F32)
    return total


def begin_kernel(columns, which, *refs):
    refs[-1][...] = down_sum(columns, which, refs[:-2], refs[-2])


def down_kernel(columns, which, *refs):
    count = len(which)
    hiddens, (sum_ref, down_ref) = refs[:count], refs[count : count + 2]
    outs, total_ref = refs[count + 2 : -1], refs[-1]
    me = lax.axis_index("ing")
    total_ref[...] = sum_ref[...] + down_sum(columns, which, hiddens, down_ref)
    slots = total_ref.shape[0] // columns
    for s in range(columns):
        at = pl.multiple_of((lax.rem(me + s, columns) ^ me) * slots, slots)
        outs[s][...] = total_ref[pl.ds(at, slots), :].astype(BF16)


def spread_kernel(groups, columns, pick_ref, *refs):
    blocks, outs = refs[:columns], refs[columns:]
    me = lax.axis_index("ing")
    for k in range(columns):
        block = blocks[k][...]
        place = lax.rem(me + columns - (k + 1), columns) ^ me
        back = jnp.dot(pick_ref[:, : block.shape[0]], block, preferred_element_type=F32)
        for d in range(groups):
            outs[d][place] = back[d * CAP : (d + 1) * CAP].astype(BF16)


def combine_kernel(groups, columns, mixing_ref, *refs):
    backs, (out_ref, held, sems) = refs[:groups][::-1], refs[groups:]
    me = lax.axis_index("ing")
    width, half = backs[0].shape[2], held.shape[0] // 2
    copies = []
    for e in range(columns):
        rows = jnp.concatenate([backs[d][e].astype(F32) for d in range(groups)], axis=0)
        rows = rows.astype(BF16)
        part = pl.ds(e * width, width)
        there = pl.ds(pl.multiple_of((me ^ e) * width, width), width)
        for h in range(2):
            mine = pl.ds(h * half, half)
            value = jnp.dot(mixing_ref[mine, :], rows, preferred_element_type=F32)
            held[mine, part] = value.astype(BF16)
            copies.append(
                pltpu.make_async_copy(held.at[mine, part], out_ref.at[mine, there], sems.at[2 * e + h])
            )
            copies[-1].start()
    for copy in copies:
        copy.wait()


def swap(x, name, step):
    if step == 0:
        return x
    return lax.ppermute(x, name, [(a, a ^ step) for a in range(lax.axis_size(name))])


def swap_all(parts, name):
    return [swap(part, name, k) for k, part in enumerate(parts)][::-1]


def local(tokens, router_logits, expert_ids, w_gate, w_up, w_down):
    groups = lax.axis_size("grp")
    columns = lax.axis_size("ing")
    count, features = tokens.shape
    units, share = w_gate.shape[2], w_down.shape[2]
    slots = groups * CAP // 2
    wide = features + LANES
    ids = pltpu.with_memory_space_constraint(expert_ids.T, pltpu.HBM)
    logits = pltpu.with_memory_space_constraint(router_logits.T, pltpu.HBM)

    outbound = pl.pallas_call(
        functools.partial(dispatch_kernel, groups, features // 4),
        out_shape=[jax.ShapeDtypeStruct((CAP, wide), BF16)] * groups,
        in_specs=[ANY, ANY],
        out_specs=[VMEM] * groups,
        scratch_shapes=[
            pltpu.VMEM(ids.shape, jnp.int32),
            pltpu.VMEM((count, features), BF16),
            pltpu.VMEM((count, count), BF16),
            pltpu.SemaphoreType.DMA((5,)),
        ],
        compiler_params=params(2 * count * features),
        name="dispatch",
    )(ids, pltpu.with_memory_space_constraint(tokens, pltpu.HBM))
    arrived = swap_all(outbound, "grp")

    weights = [w_gate[0], w_up[0], w_down[0]]
    weights = [pltpu.with_memory_space_constraint(w, pltpu.HBM) for w in weights]
    gate, up = pl.pallas_call(
        load_kernel,
        out_shape=[pltpu.VMEM(w.shape, BF16) for w in weights[:2]],
        in_specs=[ANY] * 3,
        out_specs=[VMEM] * 2,
        scratch_shapes=[pltpu.SemaphoreType.DMA((8,))],
        compiler_params=params(0),
        name="load",
    )(outbound[0], *weights[:2])

    cut = features // 2
    parts = [(0, cut), (cut, features)] if columns == 4 else [(0, features)]
    *own, pick = pl.pallas_call(
        functools.partial(compact_kernel, groups, slots, parts),
        out_shape=[jax.ShapeDtypeStruct((slots, last - first), BF16) for first, last in parts]
        + [jax.ShapeDtypeStruct((groups * CAP, LANES), BF16)],
        in_specs=[ANY] + [VMEM] * groups,
        out_specs=[VMEM] * (len(parts) + 1),
        compiler_params=params(2 * (groups * CAP + 2 * slots) * wide),
        name="compact",
    )(gate, *arrived)
    if columns == 4:
        near_low, near_high, high, far_high = [swap(part, "ing", e) for part, e in zip(own + own[1:] * 2, (1, 1, 2, 3))]
        low = swap(own[0], "ing", 2)
        far_low = swap(low, "ing", 1)
        sums = pl.pallas_call(
            functools.partial(ahead_kernel, cut, (0, 1, 3, 2)),
            out_shape=[jax.ShapeDtypeStruct((columns * slots, units), F32)] * 2,
            in_specs=[VMEM] * (columns + 2),
            out_specs=[VMEM] * 2,
            compiler_params=params(2 * columns * slots * (features + 4 * units)),
            name="ahead",
        )(own[1], near_high, far_high, high, gate, up)
        blocks = [own[0], near_low, low, far_low]
    else:
        sums, cut = [], features
        blocks = [swap(own[0], "ing", e) for e in range(columns)]

    hidden = pl.pallas_call(
        functools.partial(hidden_kernel, cut, columns),
        out_shape=jax.ShapeDtypeStruct((columns * slots, units), BF16),
        in_specs=[VMEM] * (columns + len(sums) + 2),
        out_specs=VMEM,
        compiler_params=params(2 * columns * slots * (2 * features + 5 * units)),
        name="hidden",
    )(*blocks, *sums, gate, up)
    down, mixing = pl.pallas_call(
        functools.partial(prepare_kernel, groups),
        out_shape=[
            pltpu.VMEM(w_down.shape[1:], BF16),
            jax.ShapeDtypeStruct((count, groups * CAP), BF16),
        ],
        in_specs=[ANY] * 4,
        out_specs=[VMEM] * 2,
        scratch_shapes=[
            pltpu.VMEM(ids.shape, jnp.int32),
            pltpu.VMEM(logits.shape, F32),
            pltpu.SemaphoreType.DMA((6,)),
        ],
        compiler_params=params(0),
        name="prepare",
    )(hidden, ids, logits, weights[2])
    hiddens = [swap(hidden, "ing", f) for f in range(columns)]

    early, late = (0, columns - 1), tuple(range(1, columns - 1))
    begun = pl.pallas_call(
        functools.partial(begin_kernel, columns, early),
        out_shape=jax.ShapeDtypeStruct((columns * slots, share), F32),
        in_specs=[VMEM] * (len(early) + 1),
        out_specs=VMEM,
        compiler_params=params(2 * columns * slots * (2 * units + 4 * share)),
        name="begin",
    )(*[hiddens[f] for f in early], down)
    results = pl.pallas_call(
        functools.partial(down_kernel, columns, late),
        out_shape=[jax.ShapeDtypeStruct((slots, share), BF16)] * columns,
        in_specs=[VMEM] * (len(late) + 2),
        out_specs=[VMEM] * columns,
        scratch_shapes=[pltpu.VMEM((columns * slots, share), F32)],
        compiler_params=params(2 * columns * slots * (columns * units + 8 * share)),
        name="down",
    )(*[hiddens[f] for f in late], begun, down)
    results = [
        lax.ppermute(results[s], "ing", [(a, (a + s) % columns) for a in range(columns)]) for s in range(1, columns)
    ] + [results[0]]

    backs = pl.pallas_call(
        functools.partial(spread_kernel, groups, columns),
        out_shape=[jax.ShapeDtypeStruct((columns, CAP, share), BF16)] * groups,
        in_specs=[VMEM] * (columns + 1),
        out_specs=[VMEM] * groups,
        compiler_params=params(2 * (groups * CAP + slots) * features),
        name="spread",
    )(pick, *results)
    backs = swap_all(backs, "grp")

    if share % LANES:
        me = lax.axis_index("ing")
        rows = jnp.stack(backs[::-1])[:, jnp.arange(columns) ^ me]
        rows = rows.transpose(0, 2, 1, 3).reshape(groups * CAP, features)
        return jnp.dot(mixing, rows, preferred_element_type=F32).astype(BF16)
    return pl.pallas_call(
        functools.partial(combine_kernel, groups, columns),
        out_shape=jax.ShapeDtypeStruct((count, features), BF16),
        in_specs=[VMEM] * (1 + groups),
        out_specs=ANY,
        scratch_shapes=[pltpu.VMEM((count, features), BF16), pltpu.SemaphoreType.DMA((2 * columns,))],
        compiler_params=params(2 * (count + groups * CAP) * features),
        name="combine",
    )(mixing, *backs)


def solution(mesh):
    placed = (
        P(("rep", "grp", "ing"), None),
        P(("rep", "grp", "ing"), None),
        P(("rep", "grp", "ing"), None),
        P("grp", None, "ing"),
        P("grp", None, "ing"),
        P("grp", None, "ing"),
    )
    return jax.shard_map(
        local, mesh=mesh, in_specs=placed, out_specs=P(("rep", "grp", "ing"), None), check_vma=False
    )
```

```python
import functools

import jax
import jax.numpy as jnp
from jax import lax
from jax.experimental import pallas as pl
from jax.experimental.pallas import tpu as pltpu
from jax.sharding import PartitionSpec as P

GROUP_EXPERTS = 24
CAP = 8
LANES = 128
ROUTE_SCALE = 2.827
MIB = 1024 * 1024

BF16 = jnp.bfloat16
F32 = jnp.float32
VMEM = pl.BlockSpec(memory_space=pltpu.VMEM)
ANY = pl.BlockSpec(memory_space=pl.ANY)


def params(nbytes):
    return pltpu.CompilerParams(vmem_limit_bytes=2 * nbytes + 4 * MIB)


def named(ids, expert):
    hit = jnp.zeros(expert.shape, F32)
    for k in range(ids.shape[0]):
        hit = jnp.where(ids[k : k + 1, :] == expert, 1.0, hit)
    return hit


def upto(count):
    return (
        lax.broadcasted_iota(jnp.int32, (count, count), 0)
        <= lax.broadcasted_iota(jnp.int32, (count, count), 1)
    ).astype(BF16)


def placing(ids, groups, me, before):
    rows, count = max(groups, 8), ids.shape[1]
    row = lax.broadcasted_iota(jnp.int32, (rows, count), 0)
    hit = named(ids, jnp.where(row < groups, (row ^ me) * GROUP_EXPERTS, -1))
    rank = jnp.dot(hit.astype(BF16), before, preferred_element_type=F32)
    slot = lax.broadcasted_iota(jnp.int32, (CAP, count), 0).astype(F32) + 1.0
    seat = jnp.where(hit > 0.5, rank, 0.0)
    place = [jnp.where(seat[d : d + 1, :] == slot, 1.0, 0.0) for d in range(groups)]
    return jnp.concatenate(place, axis=0), rank[:, count - 1 :]


def dispatch_kernel(groups, width, ids_ref, tokens_ref, *refs):
    outs, (ids_held, staged, before_ref, sems) = refs[:groups], refs[groups:]
    me = lax.axis_index("grp")
    features = tokens_ref.shape[1]
    first = pltpu.make_async_copy(ids_ref, ids_held, sems.at[features // width])
    first.start()
    copies = []
    for c in range(features // width):
        part = pl.ds(c * width, width)
        copies.append(pltpu.make_async_copy(tokens_ref.at[:, part], staged.at[:, part], sems.at[c]))
        copies[-1].start()
    before_ref[...] = upto(tokens_ref.shape[0])
    first.wait()
    place, counts = placing(ids_held[...], groups, me, before_ref[...])
    place = place.astype(BF16)
    slot = lax.broadcasted_iota(jnp.int32, (CAP, LANES), 0).astype(F32)
    for d in range(groups):
        live = slot < jnp.broadcast_to(counts[d : d + 1, :], (CAP, LANES))
        outs[d][:, features:] = jnp.where(live, 1.0, 0.0).astype(BF16)
    for c in range(features // width):
        copies[c].wait()
        part = slice(c * width, (c + 1) * width)
        rows = jnp.dot(place, staged[:, part], preferred_element_type=F32)
        for d in range(groups):
            outs[d][:, part] = rows[d * CAP : (d + 1) * CAP].astype(BF16)


def start_loads(weights, loaded, sems):
    copies = []
    for k in range(len(weights)):
        depth = weights[k].shape[0]
        for c in range(4):
            part = pl.ds(c * (depth // 4), depth // 4)
            copies.append(pltpu.make_async_copy(weights[k].at[part], loaded[k].at[part], sems.at[4 * k + c]))
            copies[-1].start()
    return copies


def load_kernel(after_ref, gate_ref, up_ref, gate_out, up_out, sems):
    del after_ref
    for copy in start_loads([gate_ref, up_ref], [gate_out, up_out], sems):
        copy.wait()


def prepare_kernel(groups, after_ref, ids_ref, logits_ref, down_ref, down_out, out_ref, ids_held, logits_held, sems):
    del after_ref
    small = [
        pltpu.make_async_copy(ids_ref, ids_held, sems.at[4]),
        pltpu.make_async_copy(logits_ref, logits_held, sems.at[5]),
    ]
    for copy in small:
        copy.start()
    copies = start_loads([down_ref], [down_out], sems)
    for copy in small:
        copy.wait()
    me = lax.axis_index("grp")
    ids = ids_held[...]
    place, _ = placing(ids, groups, me, upto(ids.shape[1]))
    group = (lax.broadcasted_iota(jnp.int32, place.shape, 0) // CAP) ^ me
    scores = 1.0 / (1.0 + jnp.exp(-logits_held[...]))
    expert = lax.broadcasted_iota(jnp.int32, scores.shape, 0)
    chosen = jnp.sum(jnp.where(named(ids, expert) > 0.5, scores, 0.0), axis=0, keepdims=True)
    leading = jnp.zeros(place.shape, F32)
    for g in range(groups):
        leading = jnp.where(group == g, scores[g * GROUP_EXPERTS : g * GROUP_EXPERTS + 1, :], leading)
    weight = (ROUTE_SCALE * leading / chosen).astype(BF16).astype(F32)
    out_ref[...] = jnp.where(place > 0.5, weight, 0.0).T.astype(BF16)
    for copy in copies:
        copy.wait()


def compact_kernel(groups, slots, parts, after_ref, *refs):
    del after_ref
    arrived, outs, pick_ref = refs[:groups][::-1], refs[groups:-1], refs[-1]
    rows = groups * CAP
    features = arrived[0].shape[1] - LANES
    live = jnp.concatenate([a[:, features:].astype(F32) for a in arrived], axis=0)
    row = lax.broadcasted_iota(jnp.int32, (rows, rows), 0)
    column = lax.broadcasted_iota(jnp.int32, (rows, rows), 1)
    rank = jnp.dot((column <= row).astype(BF16), live.astype(BF16), preferred_element_type=F32)
    lane = lax.broadcasted_iota(jnp.int32, (rows, LANES), 1).astype(F32)
    pick = jnp.where((live > 0.5) & (rank == lane + 1.0), 1.0, 0.0).astype(BF16)
    pick_ref[...] = pick
    step = 256
    for c in range(features // step):
        at = slice(c * step, (c + 1) * step)
        whole = jnp.concatenate([a[:, at].astype(F32) for a in arrived], axis=0).astype(BF16)
        moved = lax.dot_general(pick[:, :slots], whole, (((0,), (0,)), ((), ())), preferred_element_type=F32)
        for (first, last), out in zip(parts, outs):
            if first <= c * step < last:
                out[:, c * step - first : (c + 1) * step - first] = moved.astype(BF16)


def ahead_kernel(first, order, *refs):
    blocks, (gate_ref, up_ref, gate_sum, up_sum) = [refs[k] for k in order], refs[len(order) :]
    rows = jnp.concatenate([block[...] for block in blocks], axis=0)
    step = min(512, gate_ref.shape[1])
    for c in range(gate_ref.shape[1] // step):
        part = slice(c * step, (c + 1) * step)
        gate_sum[:, part] = jnp.dot(rows, gate_ref[first:, part], preferred_element_type=F32)
        up_sum[:, part] = jnp.dot(rows, up_ref[first:, part], preferred_element_type=F32)


def hidden_kernel(last, count, *refs):
    blocks, sums, (gate_ref, up_ref, hidden_ref) = refs[:count], refs[count:-3], refs[-3:]
    units = gate_ref.shape[1]
    rows = jnp.concatenate([block[...] for block in blocks], axis=0)
    step = min(512, units)
    for c in range(units // step):
        part = slice(c * step, (c + 1) * step)
        gate = jnp.dot(rows, gate_ref[:last, part], preferred_element_type=F32)
        up = jnp.dot(rows, up_ref[:last, part], preferred_element_type=F32)
        if sums:
            gate, up = gate + sums[0][:, part], up + sums[1][:, part]
        hidden_ref[:, part] = (gate / (1.0 + jnp.exp(-gate)) * up).astype(BF16)


def down_sum(columns, which, hiddens, down_ref):
    me = lax.axis_index("ing")
    rows, units = hiddens[0].shape
    slots = rows // columns
    total = jnp.zeros((rows, down_ref.shape[1]), F32)
    for f, hidden in zip(which, hiddens):
        block = jnp.concatenate(
            [hidden[slots * (e ^ f) : slots * ((e ^ f) + 1), :] for e in range(columns)], axis=0
        )
        at = pl.multiple_of((me ^ f) * units, units)
        total += jnp.dot(block, down_ref[pl.ds(at, units), :], preferred_element_type=F32)
    return total


def begin_kernel(columns, which, *refs):
    refs[-1][...] = down_sum(columns, which, refs[:-2], refs[-2])


def down_kernel(columns, which, *refs):
    count = len(which)
    hiddens, (sum_ref, down_ref) = refs[:count], refs[count : count + 2]
    outs, total_ref = refs[count + 2 : -1], refs[-1]
    me = lax.axis_index("ing")
    total_ref[...] = sum_ref[...] + down_sum(columns, which, hiddens, down_ref)
    slots = total_ref.shape[0] // columns
    for s in range(columns):
        at = pl.multiple_of((lax.rem(me + s, columns) ^ me) * slots, slots)
        outs[s][...] = total_ref[pl.ds(at, slots), :].astype(BF16)


def spread_kernel(groups, columns, pick_ref, *refs):
    blocks, outs = refs[:columns], refs[columns:]
    me = lax.axis_index("ing")
    for k in range(columns):
        block = blocks[k][...]
        place = lax.rem(me + columns - (k + 1), columns) ^ me
        back = jnp.dot(pick_ref[:, : block.shape[0]], block, preferred_element_type=F32)
        for d in range(groups):
            outs[d][place] = back[d * CAP : (d + 1) * CAP].astype(BF16)


def combine_kernel(groups, columns, mixing_ref, *refs):
    backs, (out_ref, held, sems) = refs[:groups][::-1], refs[groups:]
    me = lax.axis_index("ing")
    width, half = backs[0].shape[2], held.shape[0] // 2
    copies = []
    for e in range(columns):
        rows = jnp.concatenate([backs[d][e].astype(F32) for d in range(groups)], axis=0)
        rows = rows.astype(BF16)
        part = pl.ds(e * width, width)
        there = pl.ds(pl.multiple_of((me ^ e) * width, width), width)
        for h in range(2):
            mine = pl.ds(h * half, half)
            value = jnp.dot(mixing_ref[mine, :], rows, preferred_element_type=F32)
            held[mine, part] = value.astype(BF16)
            copies.append(
                pltpu.make_async_copy(held.at[mine, part], out_ref.at[mine, there], sems.at[2 * e + h])
            )
            copies[-1].start()
    for copy in copies:
        copy.wait()


def swap(x, name, step):
    if step == 0:
        return x
    return lax.ppermute(x, name, [(a, a ^ step) for a in range(lax.axis_size(name))])


def swap_all(parts, name):
    return [swap(part, name, k) for k, part in enumerate(parts)][::-1]


def local(tokens, router_logits, expert_ids, w_gate, w_up, w_down):
    groups = lax.axis_size("grp")
    columns = lax.axis_size("ing")
    count, features = tokens.shape
    units, share = w_gate.shape[2], w_down.shape[2]
    slots = groups * CAP // 2
    wide = features + LANES
    ids = pltpu.with_memory_space_constraint(expert_ids.T, pltpu.HBM)
    logits = pltpu.with_memory_space_constraint(router_logits.T, pltpu.HBM)

    outbound = pl.pallas_call(
        functools.partial(dispatch_kernel, groups, features // 4),
        out_shape=[jax.ShapeDtypeStruct((CAP, wide), BF16)] * groups,
        in_specs=[ANY, ANY],
        out_specs=[VMEM] * groups,
        scratch_shapes=[
            pltpu.VMEM(ids.shape, jnp.int32),
            pltpu.VMEM((count, features), BF16),
            pltpu.VMEM((count, count), BF16),
            pltpu.SemaphoreType.DMA((5,)),
        ],
        compiler_params=params(2 * count * features),
        name="dispatch",
    )(ids, pltpu.with_memory_space_constraint(tokens, pltpu.HBM))
    arrived = swap_all(outbound, "grp")

    weights = [w_gate[0], w_up[0], w_down[0]]
    weights = [pltpu.with_memory_space_constraint(w, pltpu.HBM) for w in weights]
    gate, up = pl.pallas_call(
        load_kernel,
        out_shape=[pltpu.VMEM(w.shape, BF16) for w in weights[:2]],
        in_specs=[ANY] * 3,
        out_specs=[VMEM] * 2,
        scratch_shapes=[pltpu.SemaphoreType.DMA((8,))],
        compiler_params=params(0),
        name="load",
    )(outbound[0], *weights[:2])

    cut = features // 2
    parts = [(0, cut), (cut, features)] if columns == 4 else [(0, features)]
    *own, pick = pl.pallas_call(
        functools.partial(compact_kernel, groups, slots, parts),
        out_shape=[jax.ShapeDtypeStruct((slots, last - first), BF16) for first, last in parts]
        + [jax.ShapeDtypeStruct((groups * CAP, LANES), BF16)],
        in_specs=[ANY] + [VMEM] * groups,
        out_specs=[VMEM] * (len(parts) + 1),
        compiler_params=params(2 * (groups * CAP + 2 * slots) * wide),
        name="compact",
    )(gate, *arrived)
    if columns == 4:
        near_low, near_high, high, far_high = [swap(part, "ing", e) for part, e in zip(own + own[1:] * 2, (1, 1, 2, 3))]
        low = swap(own[0], "ing", 2)
        far_low = swap(low, "ing", 1)
        sums = pl.pallas_call(
            functools.partial(ahead_kernel, cut, (0, 1, 3, 2)),
            out_shape=[jax.ShapeDtypeStruct((columns * slots, units), F32)] * 2,
            in_specs=[VMEM] * (columns + 2),
            out_specs=[VMEM] * 2,
            compiler_params=params(2 * columns * slots * (features + 4 * units)),
            name="ahead",
        )(own[1], near_high, far_high, high, gate, up)
        blocks = [own[0], near_low, low, far_low]
    else:
        sums, cut = [], features
        blocks = [swap(own[0], "ing", e) for e in range(columns)]

    hidden = pl.pallas_call(
        functools.partial(hidden_kernel, cut, columns),
        out_shape=jax.ShapeDtypeStruct((columns * slots, units), BF16),
        in_specs=[VMEM] * (columns + len(sums) + 2),
        out_specs=VMEM,
        compiler_params=params(2 * columns * slots * (2 * features + 5 * units)),
        name="hidden",
    )(*blocks, *sums, gate, up)
    down, mixing = pl.pallas_call(
        functools.partial(prepare_kernel, groups),
        out_shape=[
            pltpu.VMEM(w_down.shape[1:], BF16),
            jax.ShapeDtypeStruct((count, groups * CAP), BF16),
        ],
        in_specs=[ANY] * 4,
        out_specs=[VMEM] * 2,
        scratch_shapes=[
            pltpu.VMEM(ids.shape, jnp.int32),
            pltpu.VMEM(logits.shape, F32),
            pltpu.SemaphoreType.DMA((6,)),
        ],
        compiler_params=params(0),
        name="prepare",
    )(hidden, ids, logits, weights[2])
    hiddens = [swap(hidden, "ing", f) for f in range(columns)]

    early, late = (0, columns - 1), tuple(range(1, columns - 1))
    begun = pl.pallas_call(
        functools.partial(begin_kernel, columns, early),
        out_shape=jax.ShapeDtypeStruct((columns * slots, share), F32),
        in_specs=[VMEM] * (len(early) + 1),
        out_specs=VMEM,
        compiler_params=params(2 * columns * slots * (2 * units + 4 * share)),
        name="begin",
    )(*[hiddens[f] for f in early], down)
    results = pl.pallas_call(
        functools.partial(down_kernel, columns, late),
        out_shape=[jax.ShapeDtypeStruct((slots, share), BF16)] * columns,
        in_specs=[VMEM] * (len(late) + 2),
        out_specs=[VMEM] * columns,
        scratch_shapes=[pltpu.VMEM((columns * slots, share), F32)],
        compiler_params=params(2 * columns * slots * (columns * units + 8 * share)),
        name="down",
    )(*[hiddens[f] for f in late], begun, down)
    results = [
        lax.ppermute(results[s], "ing", [(a, (a + s) % columns) for a in range(columns)]) for s in range(1, columns)
    ] + [results[0]]

    backs = pl.pallas_call(
        functools.partial(spread_kernel, groups, columns),
        out_shape=[jax.ShapeDtypeStruct((columns, CAP, share), BF16)] * groups,
        in_specs=[VMEM] * (columns + 1),
        out_specs=[VMEM] * groups,
        compiler_params=params(2 * (groups * CAP + slots) * features),
        name="spread",
    )(pick, *results)
    backs = swap_all(backs, "grp")

    if share % LANES:
        me = lax.axis_index("ing")
        rows = jnp.stack(backs[::-1])[:, jnp.arange(columns) ^ me]
        rows = rows.transpose(0, 2, 1, 3).reshape(groups * CAP, features)
        return jnp.dot(mixing, rows, preferred_element_type=F32).astype(BF16)
    return pl.pallas_call(
        functools.partial(combine_kernel, groups, columns),
        out_shape=jax.ShapeDtypeStruct((count, features), BF16),
        in_specs=[VMEM] * (1 + groups),
        out_specs=ANY,
        scratch_shapes=[pltpu.VMEM((count, features), BF16), pltpu.SemaphoreType.DMA((2 * columns,))],
        compiler_params=params(2 * (count + groups * CAP) * features),
        name="combine",
    )(mixing, *backs)


def solution(mesh):
    placed = (
        P(("rep", "grp", "ing"), None),
        P(("rep", "grp", "ing"), None),
        P(("rep", "grp", "ing"), None),
        P("grp", None, "ing"),
        P("grp", None, "ing"),
        P("grp", None, "ing"),
    )
    return jax.shard_map(
        local, mesh=mesh, in_specs=placed, out_specs=P(("rep", "grp", "ing"), None), check_vma=False
    )
```

```python
import functools

import jax
import jax.numpy as jnp
from jax import lax
from jax.experimental import pallas as pl
from jax.experimental.pallas import tpu as pltpu
from jax.sharding import PartitionSpec as P

GROUP_EXPERTS = 24
CAP = 8
LANES = 128
ROUTE_SCALE = 2.827
MIB = 1024 * 1024

BF16 = jnp.bfloat16
F32 = jnp.float32
VMEM = pl.BlockSpec(memory_space=pltpu.VMEM)
ANY = pl.BlockSpec(memory_space=pl.ANY)


def params(nbytes):
    return pltpu.CompilerParams(vmem_limit_bytes=2 * nbytes + 4 * MIB)


def named(ids, expert):
    hit = jnp.zeros(expert.shape, F32)
    for k in range(ids.shape[0]):
        hit = jnp.where(ids[k : k + 1, :] == expert, 1.0, hit)
    return hit


def upto(count):
    return (
        lax.broadcasted_iota(jnp.int32, (count, count), 0)
        <= lax.broadcasted_iota(jnp.int32, (count, count), 1)
    ).astype(BF16)


def placing(ids, groups, me, before):
    rows, count = max(groups, 8), ids.shape[1]
    row = lax.broadcasted_iota(jnp.int32, (rows, count), 0)
    hit = named(ids, jnp.where(row < groups, (row ^ me) * GROUP_EXPERTS, -1))
    rank = jnp.dot(hit.astype(BF16), before, preferred_element_type=F32)
    slot = lax.broadcasted_iota(jnp.int32, (CAP, count), 0).astype(F32) + 1.0
    seat = jnp.where(hit > 0.5, rank, 0.0)
    place = [jnp.where(seat[d : d + 1, :] == slot, 1.0, 0.0) for d in range(groups)]
    return jnp.concatenate(place, axis=0), rank[:, count - 1 :]


def dispatch_kernel(groups, width, ids_ref, tokens_ref, *refs):
    outs, (ids_held, staged, before_ref, sems) = refs[:groups], refs[groups:]
    me = lax.axis_index("grp")
    features = tokens_ref.shape[1]
    first = pltpu.make_async_copy(ids_ref, ids_held, sems.at[features // width])
    first.start()
    copies = []
    for c in range(features // width):
        part = pl.ds(c * width, width)
        copies.append(pltpu.make_async_copy(tokens_ref.at[:, part], staged.at[:, part], sems.at[c]))
        copies[-1].start()
    before_ref[...] = upto(tokens_ref.shape[0])
    first.wait()
    place, counts = placing(ids_held[...], groups, me, before_ref[...])
    place = place.astype(BF16)
    slot = lax.broadcasted_iota(jnp.int32, (CAP, LANES), 0).astype(F32)
    for d in range(groups):
        live = slot < jnp.broadcast_to(counts[d : d + 1, :], (CAP, LANES))
        outs[d][:, features:] = jnp.where(live, 1.0, 0.0).astype(BF16)
    for c in range(features // width):
        copies[c].wait()
        part = slice(c * width, (c + 1) * width)
        rows = jnp.dot(place, staged[:, part], preferred_element_type=F32)
        for d in range(groups):
            outs[d][:, part] = rows[d * CAP : (d + 1) * CAP].astype(BF16)


def start_loads(weights, loaded, sems):
    copies = []
    for k in range(len(weights)):
        depth = weights[k].shape[0]
        for c in range(4):
            part = pl.ds(c * (depth // 4), depth // 4)
            copies.append(pltpu.make_async_copy(weights[k].at[part], loaded[k].at[part], sems.at[4 * k + c]))
            copies[-1].start()
    return copies


def load_kernel(after_ref, gate_ref, up_ref, gate_out, up_out, sems):
    del after_ref
    for copy in start_loads([gate_ref, up_ref], [gate_out, up_out], sems):
        copy.wait()


def prepare_kernel(groups, after_ref, ids_ref, logits_ref, down_ref, down_out, out_ref, ids_held, logits_held, sems):
    del after_ref
    small = [
        pltpu.make_async_copy(ids_ref, ids_held, sems.at[4]),
        pltpu.make_async_copy(logits_ref, logits_held, sems.at[5]),
    ]
    for copy in small:
        copy.start()
    copies = start_loads([down_ref], [down_out], sems)
    for copy in small:
        copy.wait()
    me = lax.axis_index("grp")
    ids = ids_held[...]
    place, _ = placing(ids, groups, me, upto(ids.shape[1]))
    group = (lax.broadcasted_iota(jnp.int32, place.shape, 0) // CAP) ^ me
    scores = 1.0 / (1.0 + jnp.exp(-logits_held[...]))
    expert = lax.broadcasted_iota(jnp.int32, scores.shape, 0)
    chosen = jnp.sum(jnp.where(named(ids, expert) > 0.5, scores, 0.0), axis=0, keepdims=True)
    leading = jnp.zeros(place.shape, F32)
    for g in range(groups):
        leading = jnp.where(group == g, scores[g * GROUP_EXPERTS : g * GROUP_EXPERTS + 1, :], leading)
    weight = (ROUTE_SCALE * leading / chosen).astype(BF16).astype(F32)
    out_ref[...] = jnp.where(place > 0.5, weight, 0.0).T.astype(BF16)
    for copy in copies:
        copy.wait()


def compact_kernel(groups, slots, parts, after_ref, *refs):
    del after_ref
    arrived, outs, pick_ref = refs[:groups][::-1], refs[groups:-1], refs[-1]
    rows = groups * CAP
    features = arrived[0].shape[1] - LANES
    live = jnp.concatenate([a[:, features:].astype(F32) for a in arrived], axis=0)
    row = lax.broadcasted_iota(jnp.int32, (rows, rows), 0)
    column = lax.broadcasted_iota(jnp.int32, (rows, rows), 1)
    rank = jnp.dot((column <= row).astype(BF16), live.astype(BF16), preferred_element_type=F32)
    lane = lax.broadcasted_iota(jnp.int32, (rows, LANES), 1).astype(F32)
    pick = jnp.where((live > 0.5) & (rank == lane + 1.0), 1.0, 0.0).astype(BF16)
    pick_ref[...] = pick
    step = 256
    for c in range(features // step):
        at = slice(c * step, (c + 1) * step)
        whole = jnp.concatenate([a[:, at].astype(F32) for a in arrived], axis=0).astype(BF16)
        moved = lax.dot_general(pick[:, :slots], whole, (((0,), (0,)), ((), ())), preferred_element_type=F32)
        for (first, last), out in zip(parts, outs):
            if first <= c * step < last:
                out[:, c * step - first : (c + 1) * step - first] = moved.astype(BF16)


def ahead_kernel(first, order, *refs):
    blocks, (gate_ref, up_ref, gate_sum, up_sum) = [refs[k] for k in order], refs[len(order) :]
    rows = jnp.concatenate([block[...] for block in blocks], axis=0)
    step = min(256, gate_ref.shape[1])
    for c in range(gate_ref.shape[1] // step):
        part = slice(c * step, (c + 1) * step)
        gate_sum[:, part] = jnp.dot(rows, gate_ref[first:, part], preferred_element_type=F32)
        up_sum[:, part] = jnp.dot(rows, up_ref[first:, part], preferred_element_type=F32)


def hidden_kernel(last, count, *refs):
    blocks, sums, (gate_ref, up_ref, hidden_ref) = refs[:count], refs[count:-3], refs[-3:]
    units = gate_ref.shape[1]
    rows = jnp.concatenate([block[...] for block in blocks], axis=0)
    step = min(256, units)
    for c in range(units // step):
        part = slice(c * step, (c + 1) * step)
        gate = jnp.dot(rows, gate_ref[:last, part], preferred_element_type=F32)
        up = jnp.dot(rows, up_ref[:last, part], preferred_element_type=F32)
        if sums:
            gate, up = gate + sums[0][:, part], up + sums[1][:, part]
        hidden_ref[:, part] = (gate / (1.0 + jnp.exp(-gate)) * up).astype(BF16)


def down_sum(columns, which, hiddens, down_ref):
    me = lax.axis_index("ing")
    rows, units = hiddens[0].shape
    slots = rows // columns
    total = jnp.zeros((rows, down_ref.shape[1]), F32)
    for f, hidden in zip(which, hiddens):
        block = jnp.concatenate(
            [hidden[slots * (e ^ f) : slots * ((e ^ f) + 1), :] for e in range(columns)], axis=0
        )
        at = pl.multiple_of((me ^ f) * units, units)
        total += jnp.dot(block, down_ref[pl.ds(at, units), :], preferred_element_type=F32)
    return total


def begin_kernel(columns, which, *refs):
    refs[-1][...] = down_sum(columns, which, refs[:-2], refs[-2])


def down_kernel(columns, which, *refs):
    count = len(which)
    hiddens, (sum_ref, down_ref) = refs[:count], refs[count : count + 2]
    outs, total_ref = refs[count + 2 : -1], refs[-1]
    me = lax.axis_index("ing")
    total_ref[...] = sum_ref[...] + down_sum(columns, which, hiddens, down_ref)
    slots = total_ref.shape[0] // columns
    for s in range(columns):
        at = pl.multiple_of((lax.rem(me + s, columns) ^ me) * slots, slots)
        outs[s][...] = total_ref[pl.ds(at, slots), :].astype(BF16)


def spread_kernel(groups, columns, pick_ref, *refs):
    blocks, outs, back_ref = refs[:columns], refs[columns:-1], refs[-1]
    me, group = lax.axis_index("ing"), lax.axis_index("grp")
    for k in range(columns):
        block = blocks[k][...]
        place = lax.rem(me + columns - (k + 1), columns) ^ me
        back_ref[...] = jnp.dot(pick_ref[:, : block.shape[0]], block, preferred_element_type=F32)
        for s in range(groups):
            at = pl.multiple_of((lax.rem(group + s, groups) ^ group) * CAP, CAP)
            outs[s][place] = back_ref[pl.ds(at, CAP), :].astype(BF16)


def combine_kernel(groups, columns, mixing_ref, *refs):
    backs, (out_ref, rows_ref, held, sems) = refs[:groups], refs[groups:]
    group = lax.axis_index("grp")
    me = lax.axis_index("ing")
    width, half = backs[0].shape[2], held.shape[0] // 2
    copies = []
    for e in range(columns):
        for k in range(groups):
            at = pl.multiple_of((lax.rem(group + groups - (k + 1), groups) ^ group) * CAP, CAP)
            rows_ref[pl.ds(at, CAP), :] = backs[k][e].astype(F32)
        rows = rows_ref[...].astype(BF16)
        part = pl.ds(e * width, width)
        there = pl.ds(pl.multiple_of((me ^ e) * width, width), width)
        for h in range(2):
            mine = pl.ds(h * half, half)
            value = jnp.dot(mixing_ref[mine, :], rows, preferred_element_type=F32)
            held[mine, part] = value.astype(BF16)
            copies.append(
                pltpu.make_async_copy(held.at[mine, part], out_ref.at[mine, there], sems.at[2 * e + h])
            )
            copies[-1].start()
    for copy in copies:
        copy.wait()


def swap(x, name, step):
    if step == 0:
        return x
    return lax.ppermute(x, name, [(a, a ^ step) for a in range(lax.axis_size(name))])


def swap_all(parts, name):
    return [swap(part, name, k) for k, part in enumerate(parts)][::-1]


def local(tokens, router_logits, expert_ids, w_gate, w_up, w_down):
    groups = lax.axis_size("grp")
    columns = lax.axis_size("ing")
    count, features = tokens.shape
    units, share = w_gate.shape[2], w_down.shape[2]
    slots = groups * CAP // 2
    wide = features + LANES
    ids = pltpu.with_memory_space_constraint(expert_ids.T, pltpu.HBM)
    logits = pltpu.with_memory_space_constraint(router_logits.T, pltpu.HBM)

    outbound = pl.pallas_call(
        functools.partial(dispatch_kernel, groups, features // 4),
        out_shape=[jax.ShapeDtypeStruct((CAP, wide), BF16)] * groups,
        in_specs=[ANY, ANY],
        out_specs=[VMEM] * groups,
        scratch_shapes=[
            pltpu.VMEM(ids.shape, jnp.int32),
            pltpu.VMEM((count, features), BF16),
            pltpu.VMEM((count, count), BF16),
            pltpu.SemaphoreType.DMA((5,)),
        ],
        compiler_params=params(2 * count * features),
        name="dispatch",
    )(ids, pltpu.with_memory_space_constraint(tokens, pltpu.HBM))
    arrived = swap_all(outbound, "grp")

    weights = [w_gate[0], w_up[0], w_down[0]]
    weights = [pltpu.with_memory_space_constraint(w, pltpu.HBM) for w in weights]
    gate, up = pl.pallas_call(
        load_kernel,
        out_shape=[pltpu.VMEM(w.shape, BF16) for w in weights[:2]],
        in_specs=[ANY] * 3,
        out_specs=[VMEM] * 2,
        scratch_shapes=[pltpu.SemaphoreType.DMA((8,))],
        compiler_params=params(0),
        name="load",
    )(outbound[0], *weights[:2])

    cut = features // 2
    parts = [(0, cut), (cut, features)] if columns == 4 else [(0, features)]
    *own, pick = pl.pallas_call(
        functools.partial(compact_kernel, groups, slots, parts),
        out_shape=[jax.ShapeDtypeStruct((slots, last - first), BF16) for first, last in parts]
        + [jax.ShapeDtypeStruct((groups * CAP, LANES), BF16)],
        in_specs=[ANY] + [VMEM] * groups,
        out_specs=[VMEM] * (len(parts) + 1),
        compiler_params=params(2 * (groups * CAP + 2 * slots) * wide),
        name="compact",
    )(gate, *arrived)
    if columns == 4:
        near_low, near_high, high, far_high = [swap(part, "ing", e) for part, e in zip(own + own[1:] * 2, (1, 1, 2, 3))]
        low = swap(own[0], "ing", 2)
        far_low = swap(low, "ing", 1)
        sums = pl.pallas_call(
            functools.partial(ahead_kernel, cut, (0, 1, 3, 2)),
            out_shape=[jax.ShapeDtypeStruct((columns * slots, units), F32)] * 2,
            in_specs=[VMEM] * (columns + 2),
            out_specs=[VMEM] * 2,
            compiler_params=params(2 * columns * slots * (features + 4 * units)),
            name="ahead",
        )(own[1], near_high, far_high, high, gate, up)
        blocks = [own[0], near_low, low, far_low]
    else:
        sums, cut = [], features
        blocks = [swap(own[0], "ing", e) for e in range(columns)]

    hidden = pl.pallas_call(
        functools.partial(hidden_kernel, cut, columns),
        out_shape=jax.ShapeDtypeStruct((columns * slots, units), BF16),
        in_specs=[VMEM] * (columns + len(sums) + 2),
        out_specs=VMEM,
        compiler_params=params(2 * columns * slots * (2 * features + 5 * units)),
        name="hidden",
    )(*blocks, *sums, gate, up)
    down, mixing = pl.pallas_call(
        functools.partial(prepare_kernel, groups),
        out_shape=[
            pltpu.VMEM(w_down.shape[1:], BF16),
            jax.ShapeDtypeStruct((count, groups * CAP), BF16),
        ],
        in_specs=[ANY] * 4,
        out_specs=[VMEM] * 2,
        scratch_shapes=[
            pltpu.VMEM(ids.shape, jnp.int32),
            pltpu.VMEM(logits.shape, F32),
            pltpu.SemaphoreType.DMA((6,)),
        ],
        compiler_params=params(0),
        name="prepare",
    )(hidden, ids, logits, weights[2])
    hiddens = [swap(hidden, "ing", f) for f in range(columns)]

    early, late = (0, columns - 1), tuple(range(1, columns - 1))
    begun = pl.pallas_call(
        functools.partial(begin_kernel, columns, early),
        out_shape=jax.ShapeDtypeStruct((columns * slots, share), F32),
        in_specs=[VMEM] * (len(early) + 1),
        out_specs=VMEM,
        compiler_params=params(2 * columns * slots * (2 * units + 4 * share)),
        name="begin",
    )(*[hiddens[f] for f in early], down)
    results = pl.pallas_call(
        functools.partial(down_kernel, columns, late),
        out_shape=[jax.ShapeDtypeStruct((slots, share), BF16)] * columns,
        in_specs=[VMEM] * (len(late) + 2),
        out_specs=[VMEM] * columns,
        scratch_shapes=[pltpu.VMEM((columns * slots, share), F32)],
        compiler_params=params(2 * columns * slots * (columns * units + 8 * share)),
        name="down",
    )(*[hiddens[f] for f in late], begun, down)
    results = [
        lax.ppermute(results[s], "ing", [(a, (a + s) % columns) for a in range(columns)]) for s in range(1, columns)
    ] + [results[0]]

    backs = pl.pallas_call(
        functools.partial(spread_kernel, groups, columns),
        out_shape=[jax.ShapeDtypeStruct((columns, CAP, share), BF16)] * groups,
        in_specs=[VMEM] * (columns + 1),
        out_specs=[VMEM] * groups,
        scratch_shapes=[pltpu.VMEM((groups * CAP, share), F32)],
        compiler_params=params(2 * (groups * CAP + slots) * features + 4 * groups * CAP * share),
        name="spread",
    )(pick, *results)
    backs = [
        lax.ppermute(backs[s], "grp", [(a, (a + s) % groups) for a in range(groups)]) for s in range(1, groups)
    ] + [backs[0]]

    if share % LANES:
        me = lax.axis_index("ing")
        group = lax.axis_index("grp")
        order = (group - 1 - (jnp.arange(groups) ^ group)) % groups
        rows = jnp.stack(backs)[order][:, jnp.arange(columns) ^ me]
        rows = rows.transpose(0, 2, 1, 3).reshape(groups * CAP, features)
        return jnp.dot(mixing, rows, preferred_element_type=F32).astype(BF16)
    return pl.pallas_call(
        functools.partial(combine_kernel, groups, columns),
        out_shape=jax.ShapeDtypeStruct((count, features), BF16),
        in_specs=[VMEM] * (1 + groups),
        out_specs=ANY,
        scratch_shapes=[
            pltpu.VMEM((groups * CAP, share), F32),
            pltpu.VMEM((count, features), BF16),
            pltpu.SemaphoreType.DMA((2 * columns,)),
        ],
        compiler_params=params(2 * (count + groups * CAP) * features),
        name="combine",
    )(mixing, *backs)


def solution(mesh):
    placed = (
        P(("rep", "grp", "ing"), None),
        P(("rep", "grp", "ing"), None),
        P(("rep", "grp", "ing"), None),
        P("grp", None, "ing"),
        P("grp", None, "ing"),
        P("grp", None, "ing"),
    )
    return jax.shard_map(
        local, mesh=mesh, in_specs=placed, out_specs=P(("rep", "grp", "ing"), None), check_vma=False
    )
```

```python
import functools

import jax
import jax.numpy as jnp
from jax import lax
from jax.experimental import pallas as pl
from jax.experimental.pallas import tpu as pltpu
from jax.sharding import PartitionSpec as P

GROUP_EXPERTS = 24
CAP = 8
LANES = 128
ROUTE_SCALE = 2.827
MIB = 1024 * 1024

BF16 = jnp.bfloat16
F32 = jnp.float32
VMEM = pl.BlockSpec(memory_space=pltpu.VMEM)
ANY = pl.BlockSpec(memory_space=pl.ANY)


def params(nbytes):
    return pltpu.CompilerParams(vmem_limit_bytes=2 * nbytes + 4 * MIB)


def named(ids, expert):
    hit = jnp.zeros(expert.shape, F32)
    for k in range(ids.shape[0]):
        hit = jnp.where(ids[k : k + 1, :] == expert, 1.0, hit)
    return hit


def upto(count):
    return (
        lax.broadcasted_iota(jnp.int32, (count, count), 0)
        <= lax.broadcasted_iota(jnp.int32, (count, count), 1)
    ).astype(BF16)


def placing(ids, groups, me, before):
    rows, count = max(groups, 8), ids.shape[1]
    row = lax.broadcasted_iota(jnp.int32, (rows, count), 0)
    hit = named(ids, jnp.where(row < groups, (row ^ me) * GROUP_EXPERTS, -1))
    rank = jnp.dot(hit.astype(BF16), before, preferred_element_type=F32)
    slot = lax.broadcasted_iota(jnp.int32, (CAP, count), 0).astype(F32) + 1.0
    seat = jnp.where(hit > 0.5, rank, 0.0)
    place = [jnp.where(seat[d : d + 1, :] == slot, 1.0, 0.0) for d in range(groups)]
    return jnp.concatenate(place, axis=0), rank[:, count - 1 :]


def dispatch_kernel(groups, width, ids_ref, tokens_ref, *refs):
    outs, (ids_held, staged, before_ref, sems) = refs[:groups], refs[groups:]
    me = lax.axis_index("grp")
    features = tokens_ref.shape[1]
    first = pltpu.make_async_copy(ids_ref, ids_held, sems.at[features // width])
    first.start()
    copies = []
    for c in range(features // width):
        part = pl.ds(c * width, width)
        copies.append(pltpu.make_async_copy(tokens_ref.at[:, part], staged.at[:, part], sems.at[c]))
        copies[-1].start()
    before_ref[...] = upto(tokens_ref.shape[0])
    first.wait()
    place, counts = placing(ids_held[...], groups, me, before_ref[...])
    place = place.astype(BF16)
    slot = lax.broadcasted_iota(jnp.int32, (CAP, LANES), 0).astype(F32)
    for d in range(groups):
        live = slot < jnp.broadcast_to(counts[d : d + 1, :], (CAP, LANES))
        outs[d][:, features:] = jnp.where(live, 1.0, 0.0).astype(BF16)
    for c in range(features // width):
        copies[c].wait()
        part = slice(c * width, (c + 1) * width)
        rows = jnp.dot(place, staged[:, part], preferred_element_type=F32)
        for d in range(groups):
            outs[d][:, part] = rows[d * CAP : (d + 1) * CAP].astype(BF16)


def start_loads(weights, loaded, sems):
    copies = []
    for k in range(len(weights)):
        depth = weights[k].shape[0]
        for c in range(4):
            part = pl.ds(c * (depth // 4), depth // 4)
            copies.append(pltpu.make_async_copy(weights[k].at[part], loaded[k].at[part], sems.at[4 * k + c]))
            copies[-1].start()
    return copies


def load_kernel(after_ref, gate_ref, up_ref, gate_out, up_out, sems):
    del after_ref
    for copy in start_loads([gate_ref, up_ref], [gate_out, up_out], sems):
        copy.wait()


def prepare_kernel(groups, after_ref, ids_ref, logits_ref, down_ref, down_out, out_ref, ids_held, logits_held, sems):
    del after_ref
    small = [
        pltpu.make_async_copy(ids_ref, ids_held, sems.at[4]),
        pltpu.make_async_copy(logits_ref, logits_held, sems.at[5]),
    ]
    for copy in small:
        copy.start()
    copies = start_loads([down_ref], [down_out], sems)
    for copy in small:
        copy.wait()
    me = lax.axis_index("grp")
    ids = ids_held[...]
    place, _ = placing(ids, groups, me, upto(ids.shape[1]))
    group = (lax.broadcasted_iota(jnp.int32, place.shape, 0) // CAP) ^ me
    scores = 1.0 / (1.0 + jnp.exp(-logits_held[...]))
    expert = lax.broadcasted_iota(jnp.int32, scores.shape, 0)
    chosen = jnp.sum(jnp.where(named(ids, expert) > 0.5, scores, 0.0), axis=0, keepdims=True)
    leading = jnp.zeros(place.shape, F32)
    for g in range(groups):
        leading = jnp.where(group == g, scores[g * GROUP_EXPERTS : g * GROUP_EXPERTS + 1, :], leading)
    weight = (ROUTE_SCALE * leading / chosen).astype(BF16).astype(F32)
    out_ref[...] = jnp.where(place > 0.5, weight, 0.0).T.astype(BF16)
    for copy in copies:
        copy.wait()


def compact_kernel(groups, slots, parts, after_ref, *refs):
    del after_ref
    arrived, outs, pick_ref = refs[:groups][::-1], refs[groups:-1], refs[-1]
    rows = groups * CAP
    features = arrived[0].shape[1] - LANES
    live = jnp.concatenate([a[:, features:].astype(F32) for a in arrived], axis=0)
    row = lax.broadcasted_iota(jnp.int32, (rows, rows), 0)
    column = lax.broadcasted_iota(jnp.int32, (rows, rows), 1)
    rank = jnp.dot((column <= row).astype(BF16), live.astype(BF16), preferred_element_type=F32)
    lane = lax.broadcasted_iota(jnp.int32, (rows, LANES), 1).astype(F32)
    pick = jnp.where((live > 0.5) & (rank == lane + 1.0), 1.0, 0.0).astype(BF16)
    pick_ref[...] = pick
    step = 256
    for c in range(features // step):
        at = slice(c * step, (c + 1) * step)
        whole = jnp.concatenate([a[:, at].astype(F32) for a in arrived], axis=0).astype(BF16)
        moved = lax.dot_general(pick[:, :slots], whole, (((0,), (0,)), ((), ())), preferred_element_type=F32)
        for (first, last), out in zip(parts, outs):
            if first <= c * step < last:
                out[:, c * step - first : (c + 1) * step - first] = moved.astype(BF16)


def ahead_kernel(first, order, *refs):
    blocks, (gate_ref, up_ref, gate_sum, up_sum) = [refs[k] for k in order], refs[len(order) :]
    rows = jnp.concatenate([block[...] for block in blocks], axis=0)
    step = min(256, gate_ref.shape[1])
    for c in range(gate_ref.shape[1] // step):
        part = slice(c * step, (c + 1) * step)
        gate_sum[:, part] = jnp.dot(rows, gate_ref[first:, part], preferred_element_type=F32)
        up_sum[:, part] = jnp.dot(rows, up_ref[first:, part], preferred_element_type=F32)


def hidden_kernel(last, count, *refs):
    blocks, sums, (gate_ref, up_ref, hidden_ref) = refs[:count], refs[count:-3], refs[-3:]
    units = gate_ref.shape[1]
    rows = jnp.concatenate([block[...] for block in blocks], axis=0)
    step = min(256, units)
    for c in range(units // step):
        part = slice(c * step, (c + 1) * step)
        gate = jnp.dot(rows, gate_ref[:last, part], preferred_element_type=F32)
        up = jnp.dot(rows, up_ref[:last, part], preferred_element_type=F32)
        if sums:
            gate, up = gate + sums[0][:, part], up + sums[1][:, part]
        hidden_ref[:, part] = (gate / (1.0 + jnp.exp(-gate)) * up).astype(BF16)


def down_sum(columns, which, hiddens, down_ref):
    me = lax.axis_index("ing")
    rows, units = hiddens[0].shape
    slots = rows // columns
    total = jnp.zeros((rows, down_ref.shape[1]), F32)
    for f, hidden in zip(which, hiddens):
        block = jnp.concatenate(
            [hidden[slots * (e ^ f) : slots * ((e ^ f) + 1), :] for e in range(columns)], axis=0
        )
        at = pl.multiple_of((me ^ f) * units, units)
        total += jnp.dot(block, down_ref[pl.ds(at, units), :], preferred_element_type=F32)
    return total


def begin_kernel(columns, which, *refs):
    refs[-1][...] = down_sum(columns, which, refs[:-2], refs[-2])


def down_kernel(columns, which, *refs):
    count = len(which)
    hiddens, (sum_ref, down_ref) = refs[:count], refs[count : count + 2]
    outs, total_ref = refs[count + 2 : -1], refs[-1]
    me = lax.axis_index("ing")
    total_ref[...] = sum_ref[...] + down_sum(columns, which, hiddens, down_ref)
    slots = total_ref.shape[0] // columns
    for s in range(columns):
        at = pl.multiple_of((lax.rem(me + s, columns) ^ me) * slots, slots)
        outs[s][...] = total_ref[pl.ds(at, slots), :].astype(BF16)


def spread_kernel(groups, columns, pick_ref, *refs):
    blocks, outs, back_ref = refs[:columns], refs[columns:-1], refs[-1]
    me, group = lax.axis_index("ing"), lax.axis_index("grp")
    for k in range(columns):
        block = blocks[k][...]
        place = lax.rem(me + columns - (k + 1), columns) ^ me
        back_ref[...] = jnp.dot(pick_ref[:, : block.shape[0]], block, preferred_element_type=F32)
        for s in range(groups):
            at = pl.multiple_of((lax.rem(group + s, groups) ^ group) * CAP, CAP)
            outs[s][place] = back_ref[pl.ds(at, CAP), :].astype(BF16)


def combine_kernel(groups, columns, mixing_ref, *refs):
    backs, (out_ref, rows_ref, held, sems) = refs[:groups], refs[groups:]
    group = lax.axis_index("grp")
    me = lax.axis_index("ing")
    width, half = backs[0].shape[2], held.shape[0] // 2
    copies = []
    for e in range(columns):
        for k in range(groups):
            at = pl.multiple_of((lax.rem(group + groups - (k + 1), groups) ^ group) * CAP, CAP)
            rows_ref[pl.ds(at, CAP), :] = backs[k][e].astype(F32)
        rows = rows_ref[...].astype(BF16)
        part = pl.ds(e * width, width)
        there = pl.ds(pl.multiple_of((me ^ e) * width, width), width)
        for h in range(2):
            mine = pl.ds(h * half, half)
            value = jnp.dot(mixing_ref[mine, :], rows, preferred_element_type=F32)
            held[mine, part] = value.astype(BF16)
            copies.append(
                pltpu.make_async_copy(held.at[mine, part], out_ref.at[mine, there], sems.at[2 * e + h])
            )
            copies[-1].start()
    for copy in copies:
        copy.wait()


def swap(x, name, step):
    if step == 0:
        return x
    return lax.ppermute(x, name, [(a, a ^ step) for a in range(lax.axis_size(name))])


def swap_all(parts, name):
    return [swap(part, name, k) for k, part in enumerate(parts)][::-1]


def local(tokens, router_logits, expert_ids, w_gate, w_up, w_down):
    groups = lax.axis_size("grp")
    columns = lax.axis_size("ing")
    count, features = tokens.shape
    units, share = w_gate.shape[2], w_down.shape[2]
    slots = groups * CAP // 2
    wide = features + LANES
    ids = pltpu.with_memory_space_constraint(expert_ids.T, pltpu.HBM)
    logits = pltpu.with_memory_space_constraint(router_logits.T, pltpu.HBM)

    outbound = pl.pallas_call(
        functools.partial(dispatch_kernel, groups, features // 2),
        out_shape=[jax.ShapeDtypeStruct((CAP, wide), BF16)] * groups,
        in_specs=[ANY, ANY],
        out_specs=[VMEM] * groups,
        scratch_shapes=[
            pltpu.VMEM(ids.shape, jnp.int32),
            pltpu.VMEM((count, features), BF16),
            pltpu.VMEM((count, count), BF16),
            pltpu.SemaphoreType.DMA((5,)),
        ],
        compiler_params=params(2 * count * features),
        name="dispatch",
    )(ids, pltpu.with_memory_space_constraint(tokens, pltpu.HBM))
    arrived = swap_all(outbound, "grp")

    weights = [w_gate[0], w_up[0], w_down[0]]
    weights = [pltpu.with_memory_space_constraint(w, pltpu.HBM) for w in weights]
    gate, up = pl.pallas_call(
        load_kernel,
        out_shape=[pltpu.VMEM(w.shape, BF16) for w in weights[:2]],
        in_specs=[ANY] * 3,
        out_specs=[VMEM] * 2,
        scratch_shapes=[pltpu.SemaphoreType.DMA((8,))],
        compiler_params=params(0),
        name="load",
    )(outbound[0], *weights[:2])

    cut = features // 2
    parts = [(0, cut), (cut, features)] if columns == 4 else [(0, features)]
    *own, pick = pl.pallas_call(
        functools.partial(compact_kernel, groups, slots, parts),
        out_shape=[jax.ShapeDtypeStruct((slots, last - first), BF16) for first, last in parts]
        + [jax.ShapeDtypeStruct((groups * CAP, LANES), BF16)],
        in_specs=[ANY] + [VMEM] * groups,
        out_specs=[VMEM] * (len(parts) + 1),
        compiler_params=params(2 * (groups * CAP + 2 * slots) * wide),
        name="compact",
    )(gate, *arrived)
    if columns == 4:
        near_low, near_high, high, far_high = [swap(part, "ing", e) for part, e in zip(own + own[1:] * 2, (1, 1, 2, 3))]
        low = swap(own[0], "ing", 2)
        far_low = swap(low, "ing", 1)
        sums = pl.pallas_call(
            functools.partial(ahead_kernel, cut, (0, 1, 3, 2)),
            out_shape=[jax.ShapeDtypeStruct((columns * slots, units), F32)] * 2,
            in_specs=[VMEM] * (columns + 2),
            out_specs=[VMEM] * 2,
            compiler_params=params(2 * columns * slots * (features + 4 * units)),
            name="ahead",
        )(own[1], near_high, far_high, high, gate, up)
        blocks = [own[0], near_low, low, far_low]
    else:
        sums, cut = [], features
        blocks = [swap(own[0], "ing", e) for e in range(columns)]

    hidden = pl.pallas_call(
        functools.partial(hidden_kernel, cut, columns),
        out_shape=jax.ShapeDtypeStruct((columns * slots, units), BF16),
        in_specs=[VMEM] * (columns + len(sums) + 2),
        out_specs=VMEM,
        compiler_params=params(2 * columns * slots * (2 * features + 5 * units)),
        name="hidden",
    )(*blocks, *sums, gate, up)
    down, mixing = pl.pallas_call(
        functools.partial(prepare_kernel, groups),
        out_shape=[
            pltpu.VMEM(w_down.shape[1:], BF16),
            jax.ShapeDtypeStruct((count, groups * CAP), BF16),
        ],
        in_specs=[ANY] * 4,
        out_specs=[VMEM] * 2,
        scratch_shapes=[
            pltpu.VMEM(ids.shape, jnp.int32),
            pltpu.VMEM(logits.shape, F32),
            pltpu.SemaphoreType.DMA((6,)),
        ],
        compiler_params=params(0),
        name="prepare",
    )(hidden, ids, logits, weights[2])
    hiddens = [swap(hidden, "ing", f) for f in range(columns)]

    early, late = (0, columns - 1), tuple(range(1, columns - 1))
    begun = pl.pallas_call(
        functools.partial(begin_kernel, columns, early),
        out_shape=jax.ShapeDtypeStruct((columns * slots, share), F32),
        in_specs=[VMEM] * (len(early) + 1),
        out_specs=VMEM,
        compiler_params=params(2 * columns * slots * (2 * units + 4 * share)),
        name="begin",
    )(*[hiddens[f] for f in early], down)
    results = pl.pallas_call(
        functools.partial(down_kernel, columns, late),
        out_shape=[jax.ShapeDtypeStruct((slots, share), BF16)] * columns,
        in_specs=[VMEM] * (len(late) + 2),
        out_specs=[VMEM] * columns,
        scratch_shapes=[pltpu.VMEM((columns * slots, share), F32)],
        compiler_params=params(2 * columns * slots * (columns * units + 8 * share)),
        name="down",
    )(*[hiddens[f] for f in late], begun, down)
    results = [
        lax.ppermute(results[s], "ing", [(a, (a + s) % columns) for a in range(columns)]) for s in range(1, columns)
    ] + [results[0]]

    backs = pl.pallas_call(
        functools.partial(spread_kernel, groups, columns),
        out_shape=[jax.ShapeDtypeStruct((columns, CAP, share), BF16)] * groups,
        in_specs=[VMEM] * (columns + 1),
        out_specs=[VMEM] * groups,
        scratch_shapes=[pltpu.VMEM((groups * CAP, share), F32)],
        compiler_params=params(2 * (groups * CAP + slots) * features + 4 * groups * CAP * share),
        name="spread",
    )(pick, *results)
    backs = [
        lax.ppermute(backs[s], "grp", [(a, (a + s) % groups) for a in range(groups)]) for s in range(1, groups)
    ] + [backs[0]]

    if share % LANES:
        me = lax.axis_index("ing")
        group = lax.axis_index("grp")
        order = (group - 1 - (jnp.arange(groups) ^ group)) % groups
        rows = jnp.stack(backs)[order][:, jnp.arange(columns) ^ me]
        rows = rows.transpose(0, 2, 1, 3).reshape(groups * CAP, features)
        return jnp.dot(mixing, rows, preferred_element_type=F32).astype(BF16)
    return pl.pallas_call(
        functools.partial(combine_kernel, groups, columns),
        out_shape=jax.ShapeDtypeStruct((count, features), BF16),
        in_specs=[VMEM] * (1 + groups),
        out_specs=ANY,
        scratch_shapes=[
            pltpu.VMEM((groups * CAP, share), F32),
            pltpu.VMEM((count, features), BF16),
            pltpu.SemaphoreType.DMA((2 * columns,)),
        ],
        compiler_params=params(2 * (count + groups * CAP) * features),
        name="combine",
    )(mixing, *backs)


def solution(mesh):
    placed = (
        P(("rep", "grp", "ing"), None),
        P(("rep", "grp", "ing"), None),
        P(("rep", "grp", "ing"), None),
        P("grp", None, "ing"),
        P("grp", None, "ing"),
        P("grp", None, "ing"),
    )
    return jax.shard_map(
        local, mesh=mesh, in_specs=placed, out_specs=P(("rep", "grp", "ing"), None), check_vma=False
    )
```
